512 devices in a mesh: seq: 64 (over x, y, core), head: 8 (over z).
Axes of the slice: x: 4, y: 8, z: 8, core: 2. Of those that a mesh axis runs over, the one named last changes fastest.
Arguments:
- queries: bfloat16 [8192, 8, 1024], P(('seq', 'head')), may hold values from -256 to 256
- branch_key_value: bfloat16 [8192, 8, 256], P(('seq', 'head')), may hold values from -4 to 4
- branch_ids: int32 [8192], replicated, may hold values from 0 to 3, never falling along the last dimension, each value on 1 to 4096 neighbouring positions
- pool: bfloat16 [64, 16, 8, 256], P('seq', None, 'head'), may hold values from -4 to 4
- page_table: int32 [8, 32], P('head'), may hold values from 0 to 63, as said below
Outputs:
- attended: bfloat16 [8192, 8, 1024], P(('seq', 'head'))
The draws below stay inside these ranges and needn't reach their ends.
Inputs may be any that keep to these rules, and one draw needn't show every extreme that they name: `branch_ids`: never falls along the rows; each branch covers 1 to 4096 rows and one covers exactly 4096. `page_table`: row h holds 32 distinct page numbers.
All inputs are finite; a program needn't handle non-finite values.
Results may differ from the reference program's by a relative error of at most 0.0085.
Values may be sent and summed in bfloat16 or wider, within the bound.
No kernel may reach another device: no remote copies, remote signals or barrier semaphores. Data moves between devices by JAX's collectives and lax.ppermute only.
A program may use at most 64 MiB of HBM per device.

```python
import math
import jax
import jax.numpy as jnp
import numpy as np
from jax import lax

KEY_VALUE_HEADS = 8
QUERY_GROUP = 8
HEAD_DIM = 128
PAGE_TOKENS = 16
BRANCH_TOKENS = 8192
BRANCH_MOST = 4096
BRANCHES = 4
POOL_PAGES = 64
LPAGES = 32


def shared_keys(key):
    return jnp.clip(jax.random.normal(key, (BRANCH_TOKENS, KEY_VALUE_HEADS, HEAD_DIM), jnp.float32), -4.0, 4.0)


def draw_branch_key_value(key, part):
    keys_part = shared_keys(key)
    key = jax.random.fold_in(key, 11)
    value_rows = jnp.clip(jax.random.normal(key, (BRANCH_TOKENS, KEY_VALUE_HEADS, HEAD_DIM), jnp.float32), -4.0, 4.0)
    return jnp.concatenate([keys_part, value_rows], axis=2).astype(jnp.bfloat16)


def draw_queries(key, part):
    key = jax.random.fold_in(key, 12)
    base_offset = jnp.clip(jax.random.normal(key, (BRANCH_TOKENS, KEY_VALUE_HEADS, QUERY_GROUP * HEAD_DIM), jnp.float32), -4.0, 4.0)
    return base_offset.astype(jnp.bfloat16)


def draw_page_table(key, part):
    key = jax.random.fold_in(key, 13)

    def single_head(head_index):
        sub_key = jax.random.fold_in(key, head_index)
        chosen = jax.random.permutation(sub_key, POOL_PAGES)[:LPAGES].astype(jnp.int32)
        inner = (jax.random.permutation(sub_key, POOL_PAGES - 2)[:LPAGES - 2] + 1).astype(jnp.int32)
        pinned = jnp.concatenate([jnp.array([0, POOL_PAGES - 1], jnp.int32), inner])
        return jnp.where(head_index == 0, pinned, chosen)
    return jax.vmap(single_head)(jnp.arange(KEY_VALUE_HEADS, dtype=jnp.int32))


def block_levels(own_key, shape, shards, low, top_value):
    gain = 1.0
    for dim, parts in shards:
        heights = jax.random.uniform(jax.random.fold_in(jax.random.fold_in(own_key, 6), dim), (parts,), jnp.float32, low / len(shards), top_value / len(shards))
        gain = gain * jnp.repeat(jnp.exp(heights), shape[dim] // parts).reshape((-1,) + (1,) * (len(shape) - 1 - dim))
    return gain


def split_up(amount, total, most, lean):
    weights = [(1 << 20) // math.isqrt(standing ** lean) + 1 for standing in range(2, amount + 1)]
    spare, holding = total - most - (amount - 1), [1] * (amount - 1)
    while spare > 0:
        free = [i for i in range(amount - 1) if holding[i] < most]
        whole, remaining = sum([weights[i] for i in free]), spare
        for i in free:
            addition = min(most - holding[i], max(1, remaining * weights[i] // whole), spare)
            holding[i] = holding[i] + addition
            spare = spare - addition
    return np.array([most] + holding)


def ragged(own_key, amount, total, limit, skew):
    if amount == 2:
        one = jax.random.randint(own_key, (), max(1, total - limit), min(limit, total - 1) + 1)
        return jnp.stack([one, total - one])
    tallies = jnp.asarray(split_up(amount, total, limit, skew), jnp.int32)
    pairs = (amount - 1) // 2
    source_of, taker = tallies[1:1 + 2 * pairs:2], tallies[2:2 + 2 * pairs:2]
    room = jnp.minimum(source_of - 1, limit - taker)
    passed = jax.random.randint(jax.random.fold_in(own_key, 1), (pairs,), 0, 1 << 20) % (room + 1)
    tallies = tallies.at[1:1 + 2 * pairs:2].set(source_of - passed).at[2:2 + 2 * pairs:2].set(taker + passed)
    return tallies[jax.random.permutation(jax.random.fold_in(own_key, 2), amount)]


def bell_draw(key, shape, spread, most, cuts=(), kind=jnp.bfloat16):
    result = jax.random.normal(key, shape, jnp.float32) * spread
    if len(cuts) > 0:
        result = block_levels(key, shape, cuts, -0.22, 0.18) * result
    return jnp.clip(result, min=-most, max=most).astype(kind)


def setup_inputs(seed: int = 0) -> dict:
    key_of = jax.random.split(jax.random.key(seed), 6)
    return {
        "queries": draw_queries(jax.random.fold_in(key_of[5], 71), 0),
        "branch_key_value": draw_branch_key_value(jax.random.fold_in(key_of[5], 71), 0),
        "branch_ids": jnp.searchsorted(jnp.cumsum(ragged(key_of[2], BRANCHES, BRANCH_TOKENS, BRANCH_MOST, 2)), jnp.arange(BRANCH_TOKENS), side="right").astype(jnp.int32),
        "pool": bell_draw(key_of[3], (POOL_PAGES, PAGE_TOKENS, KEY_VALUE_HEADS, 2 * HEAD_DIM), 1.0, 4.0, ((0, 64), (2, 8))),
        "page_table": draw_page_table(jax.random.fold_in(key_of[5], 71), 0),
    }


def reference(queries, branch_key_value, branch_ids, pool, page_table):
    scale = HEAD_DIM ** -0.5
    block_rows = math.gcd(BRANCH_TOKENS, 512)
    block_count = BRANCH_TOKENS // block_rows
    reach_limit = BRANCH_MOST
    padded_key_value = jnp.concatenate([jnp.zeros((reach_limit, KEY_VALUE_HEADS, 2 * HEAD_DIM), branch_key_value.dtype), branch_key_value], axis=0)
    padded_ids = jnp.concatenate([jnp.full((reach_limit,), -1, jnp.int32), branch_ids.astype(jnp.int32)], axis=0)
    row_offsets = jnp.arange(block_rows, dtype=jnp.int32)
    window_offsets = jnp.arange(reach_limit + block_rows, dtype=jnp.int32)

    def single_head(head_index):
        table = lax.dynamic_index_in_dim(page_table, head_index, 0, keepdims=False)
        pool_head = lax.dynamic_index_in_dim(pool, head_index, 2, keepdims=False)
        prefix_pairs = jnp.take(pool_head, table, axis=0).reshape(LPAGES * PAGE_TOKENS, 2 * HEAD_DIM)
        head_queries = lax.dynamic_index_in_dim(queries, head_index, 1, keepdims=False)
        head_kv = lax.dynamic_index_in_dim(padded_key_value, head_index, 1, keepdims=False)

        def one_block(block_index):
            start = (block_index * block_rows).astype(jnp.int32)
            query = lax.dynamic_slice_in_dim(head_queries, start, block_rows, 0)
            query = query.astype(jnp.float32).reshape(block_rows, QUERY_GROUP, HEAD_DIM)
            window = lax.dynamic_slice_in_dim(head_kv, start, reach_limit + block_rows, 0)
            window_ids = lax.dynamic_slice_in_dim(padded_ids, start, reach_limit + block_rows, 0)
            own_ids = lax.dynamic_slice_in_dim(branch_ids.astype(jnp.int32), start, block_rows, 0)
            query_rows = start + row_offsets
            key_rows = start - reach_limit + window_offsets
            allowed = (window_ids[None, :] == own_ids[:, None]) & (key_rows[None, :] <= query_rows[:, None])
            keys = jnp.concatenate([prefix_pairs[:, :HEAD_DIM], window[:, :HEAD_DIM]], axis=0).astype(jnp.float32)
            value_rows = jnp.concatenate([prefix_pairs[:, HEAD_DIM:], window[:, HEAD_DIM:]], axis=0).astype(jnp.float32)
            mask = jnp.concatenate([jnp.ones((block_rows, LPAGES * PAGE_TOKENS), bool), allowed], axis=1)
            scores = jnp.einsum("rgd,kd->rgk", query, keys) * scale
            scores = jnp.where(mask[:, None, :], scores, -jnp.inf)
            top = jnp.max(scores, axis=-1, keepdims=True)
            weights = jnp.exp(scores - top)
            total = jnp.sum(weights, axis=-1, keepdims=True)
            rounded = lax.optimization_barrier(weights.astype(jnp.bfloat16)).astype(jnp.float32)
            mixed = jnp.einsum("rgk,kd->rgd", rounded, value_rows) / total
            return mixed.astype(jnp.bfloat16).reshape(block_rows, QUERY_GROUP * HEAD_DIM)

        blocks = lax.map(one_block, jnp.arange(block_count, dtype=jnp.int32))
        return blocks.reshape(BRANCH_TOKENS, QUERY_GROUP * HEAD_DIM)

    attention_output = lax.map(single_head, jnp.arange(KEY_VALUE_HEADS, dtype=jnp.int32))
    return jnp.transpose(attention_output, (1, 0, 2))
```

```python
import functools

import jax
import jax.numpy as jnp
from jax import lax
from jax.experimental import pallas as pl
from jax.experimental.pallas import tpu as pltpu
from jax.sharding import PartitionSpec as P

D = 128
PAIR = 2 * D
ROWS = 128
GROUP = 8
QR = ROWS * GROUP
NX, NY = 4, 8
PAGES = 32
PAGE = 16
SCALE = D ** (-0.5)
LOG2E = 1.4426950408889634
LOW = -1e30


def x_shift(by):
    return [
        ((x * NY + y) * 2 + c, ((x + by) * NY + y) * 2 + c)
        for x in range(NX) for y in range(NY) for c in range(2) if 0 <= x + by < NX
    ]


def x_ring(by):
    return [
        ((x * NY + y) * 2 + c, (((x + by) % NX) * NY + y) * 2 + c)
        for x in range(NX) for y in range(NY) for c in range(2)
    ]


def y_ring(by):
    return [
        ((x * NY + y) * 2 + c, (x * NY + (y + by) % NY) * 2 + c)
        for x in range(NX) for y in range(NY) for c in range(2)
    ]


SWAP = [(i, i ^ 1) for i in range(2 * NX * NY)]
PLANES = [
    [((x * NY + y) * 2 + c) * 8 + z for y in range(NY) for z in range(8)]
    for x in range(NX) for c in range(2)
]


def fold(keys, values, mask, qt_ref, m_ref, l_ref, acc_ref):
    scores = jnp.dot(keys, qt_ref[...], preferred_element_type=jnp.float32)
    if mask is not None:
        scores = jnp.where(jnp.concatenate([mask] * GROUP, axis=1), scores, LOW)
    old = m_ref[...]
    top = jnp.maximum(old, jnp.max(scores, axis=0, keepdims=True))
    weights = jnp.exp2((scores - top) * (SCALE * LOG2E))
    factor = jnp.exp2((old - top) * (SCALE * LOG2E))
    m_ref[...] = top
    l_ref[...] = l_ref[...] * factor + jnp.sum(weights, axis=0, keepdims=True)
    mixed = lax.dot_general(
        values, weights.astype(jnp.bfloat16), (((0,), (0,)), ((), ())),
        preferred_element_type=jnp.float32,
    )
    acc_ref[...] = acc_ref[...] * factor + mixed


def starts_of(ids_ref, own):
    ids = ids_ref[...]
    starts = [jnp.sum((ids < b).astype(jnp.int32)) for b in range(1, 4)]
    own_ids = ids_ref[pl.ds(own, 1), :]
    row_start = jnp.zeros_like(own_ids)
    for b in range(1, 4):
        row_start = jnp.where(own_ids == b, starts[b - 1], row_start)
    return row_start, jnp.min(row_start), jnp.max(row_start)


def fold_block(block, load, own, limits, qt_ref, m_ref, l_ref, acc_ref):
    row_start, first, last = limits
    valid = (block >= 0) & (block <= own) & (block * ROWS + ROWS > first)
    whole = (block < own) & (block * ROWS >= last)

    @pl.when(valid & whole)
    def _():
        keys, values = load()
        fold(keys, values, None, qt_ref, m_ref, l_ref, acc_ref)

    @pl.when(valid & jnp.logical_not(whole))
    def _():
        keys, values = load()
        key_rows = lax.broadcasted_iota(jnp.int32, (ROWS, ROWS), 0) + block * ROWS
        query_rows = lax.broadcasted_iota(jnp.int32, (ROWS, ROWS), 1) + own * ROWS
        mask = (key_rows >= row_start) & (key_rows <= query_rows)
        fold(keys, values, mask, qt_ref, m_ref, l_ref, acc_ref)


def window(kv_ref, own_load, core, x, y, own, limits, qt_ref, m_ref, l_ref, acc_ref):
    state = (own, limits, qt_ref, m_ref, l_ref, acc_ref)
    fold_block((x * NY + y) * 2 + core, own_load, *state)

    def step(i, carry):
        yy = i % NY
        before = i < NY
        plane = jnp.where(before, x - 1, jnp.where(yy < y, x, x - 2))
        block = jnp.where(plane >= 0, (plane * NY + yy) * 2 + core, -1)

        def load():
            rows = pl.ds(pl.multiple_of(yy * ROWS, ROWS), ROWS)
            cols = pl.multiple_of(jnp.where(before, 0, PAIR), PAIR)
            return kv_ref[rows, pl.ds(cols, D)], kv_ref[rows, pl.ds(cols + D, D)]

        fold_block(block, load, *state)
        return carry

    lax.fori_loop(0, 2 * NY, step, 0)


def place(meta_ref):
    own = meta_ref[0]
    return own, own // (2 * NY), (own // 2) % NY, own % 2


def first_kernel(meta_ref, q_ref, kv_ref, ids_ref, m_ref, l_ref, acc_ref, qt_ref):
    own, x, y, core = place(meta_ref)
    limits = starts_of(ids_ref, own)
    for g in range(GROUP):
        qt_ref[:, g * ROWS:(g + 1) * ROWS] = q_ref[:, g * D:(g + 1) * D].T
    m_ref[...] = jnp.full_like(m_ref, LOW)
    l_ref[...] = jnp.zeros_like(l_ref)
    acc_ref[...] = jnp.zeros_like(acc_ref)

    def own_load():
        base = GROUP * D
        return q_ref[:, base:base + D], q_ref[:, base + D:base + PAIR]

    window(kv_ref, own_load, core, x, y, own, limits, qt_ref, m_ref, l_ref, acc_ref)


def last_kernel(meta_ref, table_ref, qt_ref, kv_ref, side_ref, mine_ref, ids_ref, m_in, l_in, acc_in,
                out_ref, m_ref, l_ref, acc_ref, prefix_ref):
    m_ref[...] = m_in[...]
    l_ref[...] = l_in[...]
    acc_ref[...] = acc_in[...]
    own, x, y, core = place(meta_ref)
    limits = starts_of(ids_ref, own)
    for i in range(PAGES):
        page = table_ref[i]
        off = (y + NY - (page // 2) % NY) % NY
        unit = (x + NX - page // (2 * NY)) % NX + 4 * (off // 4) + 8 * ((off // 2) % 2) + 16 * (off % 2)
        rows = pl.ds(pl.multiple_of(ROWS + unit * PAGE, PAGE), PAGE)

        @pl.when(page % 2 == core)
        def _():
            prefix_ref[i * PAGE:(i + 1) * PAGE, :] = mine_ref[rows, :]

        @pl.when(page % 2 != core)
        def _():
            prefix_ref[i * PAGE:(i + 1) * PAGE, :] = side_ref[rows, :]

    fold(prefix_ref[:, :D], prefix_ref[:, D:], None, qt_ref, m_ref, l_ref, acc_ref)

    def own_load():
        return side_ref[:ROWS, :D], side_ref[:ROWS, D:]

    window(kv_ref, own_load, 1 - core, x, y, own, limits, qt_ref, m_ref, l_ref, acc_ref)
    result = (acc_ref[...] * (1.0 / l_ref[...])).astype(jnp.bfloat16)
    for g in range(GROUP):
        out_ref[:, g * D:(g + 1) * D] = result[:, g * ROWS:(g + 1) * ROWS].T


VM = pl.BlockSpec(memory_space=pltpu.VMEM)
SM = pl.BlockSpec(memory_space=pltpu.SMEM)


def per_device(queries, branch_key_value, branch_ids, pool, page_table):
    me = lax.axis_index("seq")
    y = (me // 2) % NY
    raw = jnp.transpose(branch_key_value, (1, 0, 2))
    two_back = lax.ppermute(raw, "seq", x_shift(2))
    one_back = lax.ppermute(raw, "seq", x_shift(1))
    page = pool.reshape(1, PAGE, PAIR)
    pages = jnp.concatenate([page] + [lax.ppermute(page, "seq", x_ring(k)) for k in (1, 2, 3)], axis=0)
    for by in (4, 2, 1):
        pages = jnp.concatenate([pages, lax.ppermute(pages, "seq", y_ring(by))], axis=0)
    wide = jnp.concatenate([queries, branch_key_value], axis=2)
    wide = lax.all_to_all(wide, "head", split_axis=1, concat_axis=0, tiled=True).reshape(ROWS, GROUP * D + PAIR)
    target = jnp.arange(NY, dtype=jnp.int32)[:, None, None, None]
    mixed = jnp.where(target > y, raw[None], two_back[None])
    send = jnp.concatenate([jnp.broadcast_to(one_back[None], mixed.shape), mixed], axis=3)
    kv = lax.all_to_all(
        send.reshape(NY * 8, 16, 2 * PAIR), ("seq", "head"), split_axis=0, concat_axis=0, tiled=True,
        axis_index_groups=PLANES,
    ).reshape(NY * ROWS, 2 * PAIR)
    mine = jnp.concatenate([wide[:, GROUP * D:], pages.reshape(PAGES * PAGE, PAIR)], axis=0)
    side = lax.ppermute(mine, "seq", SWAP)
    kv_side = lax.ppermute(kv, "seq", SWAP)

    ids = branch_ids.reshape(64, ROWS)
    meta = me.astype(jnp.int32).reshape(1)
    state = [
        jax.ShapeDtypeStruct((1, QR), jnp.float32),
        jax.ShapeDtypeStruct((1, QR), jnp.float32),
        jax.ShapeDtypeStruct((D, QR), jnp.float32),
    ]
    params = pltpu.CompilerParams(vmem_limit_bytes=40 * 1024 * 1024)
    m, l, acc, qt = pl.pallas_call(
        first_kernel,
        out_shape=state + [jax.ShapeDtypeStruct((D, QR), jnp.bfloat16)],
        in_specs=[SM, VM, VM, VM],
        out_specs=[VM] * 4,
        compiler_params=params,
        name="own_parity",
    )(meta, wide, kv, ids)
    out = pl.pallas_call(
        last_kernel,
        out_shape=jax.ShapeDtypeStruct((ROWS, GROUP * D), jnp.bfloat16),
        in_specs=[SM, SM] + [VM] * 8,
        out_specs=VM,
        scratch_shapes=[
            pltpu.VMEM((1, QR), jnp.float32),
            pltpu.VMEM((1, QR), jnp.float32),
            pltpu.VMEM((D, QR), jnp.float32),
            pltpu.VMEM((PAGES * PAGE, PAIR), jnp.bfloat16),
        ],
        compiler_params=params,
        name="other_parity",
    )(meta, page_table.reshape(PAGES), qt, kv_side, side, mine, ids, m, l, acc)
    return lax.all_to_all(out.reshape(ROWS, 1, GROUP * D), "head", split_axis=0, concat_axis=1, tiled=True)


def solution(mesh):
    return jax.shard_map(
        per_device,
        mesh=mesh,
        in_specs=(
            P(("seq", "head"), None, None),
            P(("seq", "head"), None, None),
            P(),
            P("seq", None, "head", None),
            P("head", None),
        ),
        out_specs=P(("seq", "head"), None, None),
        check_vma=False,
    )
```

```python
import jax
import jax.numpy as jnp
from jax import lax
from jax.experimental import pallas as pl
from jax.experimental.pallas import tpu as pltpu
from jax.sharding import PartitionSpec as P

D = 128
PAIR = 2 * D
ROWS = 128
GROUP = 8
QR = ROWS * GROUP
NX, NY = 4, 8
PAGES = 32
PAGE = 16
BLOCKS = 4
TILE = 512
SCALE2 = D ** (-0.5) * 1.4426950408889634
LOW = -1e30


def x_shift(by):
    return [
        ((x * NY + y) * 2 + c, ((x + by) * NY + y) * 2 + c)
        for x in range(NX) for y in range(NY) for c in range(2) if 0 <= x + by < NX
    ]


def x_ring(by):
    return [
        ((x * NY + y) * 2 + c, (((x + by) % NX) * NY + y) * 2 + c)
        for x in range(NX) for y in range(NY) for c in range(2)
    ]


def y_ring(by):
    return [
        ((x * NY + y) * 2 + c, (x * NY + (y + by) % NY) * 2 + c)
        for x in range(NX) for y in range(NY) for c in range(2)
    ]


SWAP = [(i, i ^ 1) for i in range(2 * NX * NY)]
Y_GROUPS = [[(x * NY + y) * 2 + c for y in range(NY)] for x in range(NX) for c in range(2)]


def fold(keys, values, mask, qt_ref, m_ref, l_ref, acc_ref):
    twice = jnp.concatenate([keys, keys], axis=1)
    lifted = jnp.concatenate([values.T, jnp.ones((16, keys.shape[0]), jnp.bfloat16)], axis=0)

    def scores_of(at):
        scores = jnp.dot(twice, qt_ref[:, at:at + TILE], preferred_element_type=jnp.float32)
        if mask is not None:
            scores = jnp.where(jnp.concatenate([mask] * (TILE // ROWS), axis=1), scores, LOW)
        return scores

    coming = scores_of(0)
    for at in range(0, QR, TILE):
        cols = slice(at, at + TILE)
        scores = coming
        if at + TILE < QR:
            coming = scores_of(at + TILE)
        old = m_ref[:, cols]
        top = jnp.maximum(old, jnp.max(scores, axis=0, keepdims=True))
        weights = jnp.exp2(scores - top).astype(jnp.bfloat16)
        factor = jnp.exp2(old - top)
        m_ref[:, cols] = top
        mixed = jnp.dot(lifted, weights, preferred_element_type=jnp.float32)
        l_ref[:, cols] = l_ref[:, cols] * factor + mixed[D:D + 1]
        acc_ref[:, cols] = acc_ref[:, cols] * factor + mixed[:D]


def starts_of(ids_ref, own):
    ids = ids_ref[...]
    starts = [jnp.sum((ids < b).astype(jnp.int32)) for b in range(1, 4)]
    own_ids = ids_ref[pl.ds(own, 1), :]
    row_start = jnp.zeros_like(own_ids)
    for b in range(1, 4):
        row_start = jnp.where(own_ids == b, starts[b - 1], row_start)
    return row_start, jnp.min(row_start), jnp.max(row_start)


def mask_of(block, own, row_start):
    key_rows = lax.broadcasted_iota(jnp.int32, (ROWS, ROWS), 0) + block * ROWS
    query_rows = lax.broadcasted_iota(jnp.int32, (ROWS, ROWS), 1) + own * ROWS
    return (key_rows >= row_start) & (key_rows <= query_rows)


def near_kernel(meta_ref, table_ref, q_ref, mine_ref, side_ref, ids_ref, qt_ref, m_ref, l_ref, acc_ref, prefix_ref):
    own = meta_ref[0]
    core, y, x = own % 2, (own // 2) % NY, own // (2 * NY)
    row_start, first, last = starts_of(ids_ref, own)
    for g in range(GROUP):
        scaled = q_ref[:, g * D:(g + 1) * D].astype(jnp.float32) * SCALE2
        high = scaled.astype(jnp.bfloat16)
        low = (scaled - high.astype(jnp.float32)).astype(jnp.bfloat16)
        qt_ref[:D, g * ROWS:(g + 1) * ROWS] = high.T
        qt_ref[D:, g * ROWS:(g + 1) * ROWS] = low.T
    m_ref[...] = jnp.full_like(m_ref, LOW)
    l_ref[...] = jnp.zeros_like(l_ref)
    acc_ref[...] = jnp.zeros_like(acc_ref)
    state = (qt_ref, m_ref, l_ref, acc_ref)
    fold(mine_ref[:ROWS, :D], mine_ref[:ROWS, D:], mask_of(own, own, row_start), *state)

    @pl.when((core == 1) & (own * ROWS > first))
    def _():
        fold(side_ref[:ROWS, :D], side_ref[:ROWS, D:], mask_of(own - 1, own, row_start), *state)

    for i in range(PAGES):
        page = table_ref[i]
        off = (y + NY - (page // 2) % NY) % NY
        unit = (x + NX - page // (2 * NY)) % NX + 4 * (off // 4) + 8 * ((off // 2) % 2) + 16 * (off % 2)
        rows = pl.ds(pl.multiple_of(ROWS + unit * PAGE, PAGE), PAGE)

        @pl.when(page % 2 == core)
        def _():
            prefix_ref[i * PAGE:(i + 1) * PAGE, :] = mine_ref[rows, :]

        @pl.when(page % 2 != core)
        def _():
            prefix_ref[i * PAGE:(i + 1) * PAGE, :] = side_ref[rows, :]

    fold(prefix_ref[:, :D], prefix_ref[:, D:], None, *state)


def window(kv_ref, core, own, ids_ref, qt_ref, m_ref, l_ref, acc_ref):
    row_start, first, last = starts_of(ids_ref, own)
    chip = own // 2
    x = chip // NY
    lowest = (jnp.maximum(first // ROWS - core, -1) + 1) // 2
    steps = jnp.maximum(chip - lowest + BLOCKS - 1, 0) // BLOCKS

    def step(i, carry):
        base = chip - BLOCKS * (i + 1)
        pairs = []
        for b in range(BLOCKS):
            at = jnp.maximum(base + b, 0)
            slot = (at % NY) * 2 + jnp.where(at // NY == x - 1, 0, 1)
            pairs.append(kv_ref[pl.ds(pl.multiple_of(slot * ROWS, ROWS), ROWS), :])
        keys = jnp.concatenate([pair[:, :D] for pair in pairs], axis=0)
        values = jnp.concatenate([pair[:, D:] for pair in pairs], axis=0)
        whole = (2 * base + core) * ROWS >= last

        @pl.when(whole)
        def _():
            fold(keys, values, None, qt_ref, m_ref, l_ref, acc_ref)

        @pl.when(jnp.logical_not(whole))
        def _():
            mask = jnp.concatenate(
                [mask_of(2 * (base + b) + core, own, row_start) for b in range(BLOCKS)], axis=0
            )
            fold(keys, values, mask, qt_ref, m_ref, l_ref, acc_ref)

        return carry

    lax.fori_loop(0, steps, step, 0)


def own_kernel(meta_ref, kv_ref, ids_ref, qt_ref, m_in, l_in, acc_in, m_ref, l_ref, acc_ref):
    m_ref[...] = m_in[...]
    l_ref[...] = l_in[...]
    acc_ref[...] = acc_in[...]
    own = meta_ref[0]
    window(kv_ref, own % 2, own, ids_ref, qt_ref, m_ref, l_ref, acc_ref)


def last_kernel(meta_ref, kv_ref, ids_ref, qt_ref, m_in, l_in, acc_in, out_ref, m_ref, l_ref, acc_ref):
    m_ref[...] = m_in[...]
    l_ref[...] = l_in[...]
    acc_ref[...] = acc_in[...]
    own = meta_ref[0]
    window(kv_ref, 1 - own % 2, own, ids_ref, qt_ref, m_ref, l_ref, acc_ref)
    result = (acc_ref[...] * (1.0 / l_ref[...])).astype(jnp.bfloat16)
    for g in range(GROUP):
        out_ref[:, g * D:(g + 1) * D] = result[:, g * ROWS:(g + 1) * ROWS].T


VM = pl.BlockSpec(memory_space=pltpu.VMEM)
SM = pl.BlockSpec(memory_space=pltpu.SMEM)


def cost(keys):
    return pl.CostEstimate(flops=4 * D * QR * keys, bytes_accessed=1 << 20, transcendentals=QR * keys)


def per_device(queries, branch_key_value, branch_ids, pool, page_table):
    me = lax.axis_index("seq")
    y = (me // 2) % NY
    page = pool.reshape(1, PAGE, PAIR)
    pages = jnp.concatenate([page] + [lax.ppermute(page, "seq", x_ring(k)) for k in (1, 2, 3)], axis=0)
    for by in (4, 2, 1):
        pages = jnp.concatenate([pages, lax.ppermute(pages, "seq", y_ring(by))], axis=0)
    wide = jnp.concatenate([queries, branch_key_value], axis=2)
    wide = lax.all_to_all(wide, "head", split_axis=1, concat_axis=0, tiled=True).reshape(ROWS, GROUP * D + PAIR)
    own = wide[:, GROUP * D:]
    two_back = lax.ppermute(own, "seq", x_shift(2))
    one_back = lax.ppermute(own, "seq", x_shift(1))
    target = jnp.arange(NY, dtype=jnp.int32)[:, None, None]
    mixed = jnp.where(target > y, own[None], two_back[None])
    send = jnp.stack([jnp.broadcast_to(one_back[None], mixed.shape), mixed], axis=1)
    kv = lax.all_to_all(send, "seq", split_axis=0, concat_axis=0, tiled=True, axis_index_groups=Y_GROUPS)
    kv = kv.reshape(2 * NY * ROWS, PAIR)
    mine = jnp.concatenate([own, pages.reshape(PAGES * PAGE, PAIR)], axis=0)
    side = lax.ppermute(mine, "seq", SWAP)
    kv_side = lax.ppermute(kv, "seq", SWAP)

    ids = branch_ids.reshape(2 * NX * NY, ROWS)
    meta = me.astype(jnp.int32).reshape(1)
    state = [
        jax.ShapeDtypeStruct((1, QR), jnp.float32),
        jax.ShapeDtypeStruct((1, QR), jnp.float32),
        jax.ShapeDtypeStruct((D, QR), jnp.float32),
    ]
    params = pltpu.CompilerParams(vmem_limit_bytes=40 * 1024 * 1024)
    qt, m, l, acc = pl.pallas_call(
        near_kernel,
        out_shape=[jax.ShapeDtypeStruct((PAIR, QR), jnp.bfloat16)] + state,
        in_specs=[SM, SM, VM, VM, VM, VM],
        out_specs=[VM] * 4,
        scratch_shapes=[pltpu.VMEM((PAGES * PAGE, PAIR), jnp.bfloat16)],
        compiler_params=params,
        cost_estimate=cost(768),
        name="near_keys",
    )(meta, page_table.reshape(PAGES), wide, mine, side, ids)
    m, l, acc = pl.pallas_call(
        own_kernel,
        out_shape=state,
        in_specs=[SM] + [VM] * 6,
        out_specs=[VM] * 3,
        compiler_params=params,
        cost_estimate=cost(2048),
        name="own_parity",
    )(meta, kv, ids, qt, m, l, acc)
    out = pl.pallas_call(
        last_kernel,
        out_shape=jax.ShapeDtypeStruct((ROWS, GROUP * D), jnp.bfloat16),
        in_specs=[SM] + [VM] * 6,
        out_specs=VM,
        scratch_shapes=[
            pltpu.VMEM((1, QR), jnp.float32),
            pltpu.VMEM((1, QR), jnp.float32),
            pltpu.VMEM((D, QR), jnp.float32),
        ],
        compiler_params=params,
        cost_estimate=cost(2048),
        name="other_parity",
    )(meta, kv_side, ids, qt, m, l, acc)
    out = lax.all_to_all(out.reshape(8, ROWS // 8, GROUP * D), "head", split_axis=0, concat_axis=0, tiled=True)
    return jnp.transpose(out, (1, 0, 2))


def solution(mesh):
    return jax.shard_map(
        per_device,
        mesh=mesh,
        in_specs=(
            P(("seq", "head"), None, None),
            P(("seq", "head"), None, None),
            P(),
            P("seq", None, "head", None),
            P("head", None),
        ),
        out_specs=P(("seq", "head"), None, None),
        check_vma=False,
    )
```

```python
import jax
import jax.numpy as jnp
from jax import lax
from jax.experimental import pallas as pl
from jax.experimental.pallas import tpu as pltpu
from jax.sharding import PartitionSpec as P

D = 128
PAIR = 2 * D
ROWS = 128
GROUP = 8
QR = ROWS * GROUP
NX, NY = 4, 8
PAGES = 32
PAGE = 16
BLOCKS = 4
TILE = 512
SCALE2 = D ** (-0.5) * 1.4426950408889634
LOW = -1e30


def x_shift(by):
    return [
        ((x * NY + y) * 2 + c, ((x + by) * NY + y) * 2 + c)
        for x in range(NX) for y in range(NY) for c in range(2) if 0 <= x + by < NX
    ]


def x_ring(by):
    return [
        ((x * NY + y) * 2 + c, (((x + by) % NX) * NY + y) * 2 + c)
        for x in range(NX) for y in range(NY) for c in range(2)
    ]


def y_ring(by):
    return [
        ((x * NY + y) * 2 + c, (x * NY + (y + by) % NY) * 2 + c)
        for x in range(NX) for y in range(NY) for c in range(2)
    ]


SWAP = [(i, i ^ 1) for i in range(2 * NX * NY)]
Y_GROUPS = [[(x * NY + y) * 2 + c for y in range(NY)] for x in range(NX) for c in range(2)]


def fold(keys, values, mask, qt_ref, m_ref, l_ref, acc_ref):
    twice = jnp.concatenate([keys, keys], axis=1)
    lifted = jnp.concatenate([values.T, jnp.ones((16, keys.shape[0]), jnp.bfloat16)], axis=0)

    def scores_of(at):
        scores = jnp.dot(twice, qt_ref[:, at:at + TILE], preferred_element_type=jnp.float32)
        if mask is not None:
            scores = jnp.where(jnp.concatenate([mask] * (TILE // ROWS), axis=1), scores, LOW)
        return scores

    coming = scores_of(0)
    for at in range(0, QR, TILE):
        cols = slice(at, at + TILE)
        scores = coming
        if at + TILE < QR:
            coming = scores_of(at + TILE)
        old = m_ref[:, cols]
        top = jnp.maximum(old, jnp.max(scores, axis=0, keepdims=True))
        weights = jnp.exp2(scores - top).astype(jnp.bfloat16)
        factor = jnp.exp2(old - top)
        m_ref[:, cols] = top
        mixed = jnp.dot(lifted, weights, preferred_element_type=jnp.float32)
        l_ref[:, cols] = l_ref[:, cols] * factor + mixed[D:D + 1]
        acc_ref[:, cols] = acc_ref[:, cols] * factor + mixed[:D]


def starts_of(ids_ref, own):
    ids = ids_ref[...]
    starts = [jnp.sum((ids < b).astype(jnp.int32)) for b in range(1, 4)]
    own_ids = ids_ref[pl.ds(own, 1), :]
    row_start = jnp.zeros_like(own_ids)
    for b in range(1, 4):
        row_start = jnp.where(own_ids == b, starts[b - 1], row_start)
    return row_start, jnp.min(row_start), jnp.max(row_start)


def mask_of(block, own, row_start):
    key_rows = lax.broadcasted_iota(jnp.int32, (ROWS, ROWS), 0) + block * ROWS
    query_rows = lax.broadcasted_iota(jnp.int32, (ROWS, ROWS), 1) + own * ROWS
    return (key_rows >= row_start) & (key_rows <= query_rows)


def near_kernel(meta_ref, table_ref, q_ref, mine_ref, side_ref, ids_ref, qt_ref, m_ref, l_ref, acc_ref, prefix_ref):
    own = meta_ref[0]
    core, y, x = own % 2, (own // 2) % NY, own // (2 * NY)
    row_start, first, last = starts_of(ids_ref, own)
    for g in range(GROUP):
        scaled = q_ref[:, g * D:(g + 1) * D].astype(jnp.float32) * SCALE2
        high = scaled.astype(jnp.bfloat16)
        low = (scaled - high.astype(jnp.float32)).astype(jnp.bfloat16)
        qt_ref[:D, g * ROWS:(g + 1) * ROWS] = high.T
        qt_ref[D:, g * ROWS:(g + 1) * ROWS] = low.T
    m_ref[...] = jnp.full_like(m_ref, LOW)
    l_ref[...] = jnp.zeros_like(l_ref)
    acc_ref[...] = jnp.zeros_like(acc_ref)
    state = (qt_ref, m_ref, l_ref, acc_ref)
    fold(mine_ref[:ROWS, :D], mine_ref[:ROWS, D:], mask_of(own, own, row_start), *state)

    @pl.when((core == 1) & (own * ROWS > first))
    def _():
        fold(side_ref[:ROWS, :D], side_ref[:ROWS, D:], mask_of(own - 1, own, row_start), *state)

    for i in range(PAGES):
        page = table_ref[i]
        off = (y + NY - (page // 2) % NY) % NY
        unit = NY * ((x + NX - page // (2 * NY)) % NX) + off // 4 + 2 * (off % 4)
        rows = pl.ds(pl.multiple_of(ROWS + unit * PAGE, PAGE), PAGE)

        @pl.when(page % 2 == core)
        def _():
            prefix_ref[i * PAGE:(i + 1) * PAGE, :] = mine_ref[rows, :]

        @pl.when(page % 2 != core)
        def _():
            prefix_ref[i * PAGE:(i + 1) * PAGE, :] = side_ref[rows, :]

    fold(prefix_ref[:, :D], prefix_ref[:, D:], None, *state)


def window(kv_ref, core, own, ids_ref, qt_ref, m_ref, l_ref, acc_ref):
    row_start, first, last = starts_of(ids_ref, own)
    chip = own // 2
    x = chip // NY
    lowest = (jnp.maximum(first // ROWS - core, -1) + 1) // 2
    steps = jnp.maximum(chip - lowest + BLOCKS - 1, 0) // BLOCKS

    def step(i, carry):
        base = chip - BLOCKS * (i + 1)
        pairs = []
        for b in range(BLOCKS):
            at = jnp.maximum(base + b, 0)
            slot = (at % NY) * 2 + jnp.where(at // NY == x - 1, 0, 1)
            pairs.append(kv_ref[pl.ds(pl.multiple_of(slot * ROWS, ROWS), ROWS), :])
        keys = jnp.concatenate([pair[:, :D] for pair in pairs], axis=0)
        values = jnp.concatenate([pair[:, D:] for pair in pairs], axis=0)
        whole = (2 * base + core) * ROWS >= last

        @pl.when(whole)
        def _():
            fold(keys, values, None, qt_ref, m_ref, l_ref, acc_ref)

        @pl.when(jnp.logical_not(whole))
        def _():
            mask = jnp.concatenate(
                [mask_of(2 * (base + b) + core, own, row_start) for b in range(BLOCKS)], axis=0
            )
            fold(keys, values, mask, qt_ref, m_ref, l_ref, acc_ref)

        return carry

    lax.fori_loop(0, steps, step, 0)


def own_kernel(meta_ref, kv_ref, ids_ref, qt_ref, m_in, l_in, acc_in, m_ref, l_ref, acc_ref):
    m_ref[...] = m_in[...]
    l_ref[...] = l_in[...]
    acc_ref[...] = acc_in[...]
    own = meta_ref[0]
    window(kv_ref, own % 2, own, ids_ref, qt_ref, m_ref, l_ref, acc_ref)


def last_kernel(meta_ref, kv_ref, ids_ref, qt_ref, m_in, l_in, acc_in, out_ref, m_ref, l_ref, acc_ref):
    m_ref[...] = m_in[...]
    l_ref[...] = l_in[...]
    acc_ref[...] = acc_in[...]
    own = meta_ref[0]
    window(kv_ref, 1 - own % 2, own, ids_ref, qt_ref, m_ref, l_ref, acc_ref)
    result = (acc_ref[...] * (1.0 / l_ref[...])).astype(jnp.bfloat16)
    for g in range(GROUP):
        out_ref[:, g * D:(g + 1) * D] = result[:, g * ROWS:(g + 1) * ROWS].T


VM = pl.BlockSpec(memory_space=pltpu.VMEM)
SM = pl.BlockSpec(memory_space=pltpu.SMEM)


def cost(keys):
    return pl.CostEstimate(flops=4 * D * QR * keys, bytes_accessed=1 << 20, transcendentals=QR * keys)


def per_device(queries, branch_key_value, branch_ids, pool, page_table):
    me = lax.axis_index("seq")
    y = (me // 2) % NY
    pages = pool.reshape(1, PAGE, PAIR)
    pages = jnp.concatenate([pages, lax.ppermute(pages, "seq", y_ring(4))], axis=0)
    pages = jnp.concatenate([pages] + [lax.ppermute(pages, "seq", y_ring(k)) for k in (1, 2, 3)], axis=0)
    pages = pages.reshape(NY * PAGE, PAIR)
    wide = jnp.concatenate([queries, branch_key_value], axis=2)
    wide = lax.all_to_all(wide, "head", split_axis=1, concat_axis=0, tiled=True).reshape(ROWS, GROUP * D + PAIR)
    own = wide[:, GROUP * D:]
    near = jnp.concatenate([own, pages], axis=0)
    two_back = lax.ppermute(near, "seq", x_ring(2))
    one_back = lax.ppermute(near, "seq", x_ring(1))
    target = jnp.arange(NY, dtype=jnp.int32)[:, None, None]
    mixed = jnp.where(target > y, own[None], two_back[None, :ROWS])
    send = jnp.stack([jnp.broadcast_to(one_back[None, :ROWS], mixed.shape), mixed], axis=1)
    kv = lax.all_to_all(send, "seq", split_axis=0, concat_axis=0, tiled=True, axis_index_groups=Y_GROUPS)
    kv = kv.reshape(2 * NY * ROWS, PAIR)
    far, _ = lax.optimization_barrier((two_back[ROWS:], send))
    three_back = lax.ppermute(far, "seq", x_ring(1))
    mine = jnp.concatenate([near, one_back[ROWS:], two_back[ROWS:], three_back], axis=0)
    side = lax.ppermute(mine, "seq", SWAP)
    ids = branch_ids.reshape(2 * NX * NY, ROWS)
    meta = me.astype(jnp.int32).reshape(1)
    state = [
        jax.ShapeDtypeStruct((1, QR), jnp.float32),
        jax.ShapeDtypeStruct((1, QR), jnp.float32),
        jax.ShapeDtypeStruct((D, QR), jnp.float32),
    ]
    params = pltpu.CompilerParams(vmem_limit_bytes=40 * 1024 * 1024)
    qt, m, l, acc = pl.pallas_call(
        near_kernel,
        out_shape=[jax.ShapeDtypeStruct((PAIR, QR), jnp.bfloat16)] + state,
        in_specs=[SM, SM, VM, VM, VM, VM],
        out_specs=[VM] * 4,
        scratch_shapes=[pltpu.VMEM((PAGES * PAGE, PAIR), jnp.bfloat16)],
        compiler_params=params,
        cost_estimate=cost(768),
        name="near_keys",
    )(meta, page_table.reshape(PAGES), wide, mine, side, ids)
    kv, m = lax.optimization_barrier((kv, m))
    kv_side = lax.ppermute(kv, "seq", SWAP)
    m, l, acc = pl.pallas_call(
        own_kernel,
        out_shape=state,
        in_specs=[SM] + [VM] * 6,
        out_specs=[VM] * 3,
        compiler_params=params,
        cost_estimate=cost(2048),
        name="own_parity",
    )(meta, kv, ids, qt, m, l, acc)
    out = pl.pallas_call(
        last_kernel,
        out_shape=jax.ShapeDtypeStruct((ROWS, GROUP * D), jnp.bfloat16),
        in_specs=[SM] + [VM] * 6,
        out_specs=VM,
        scratch_shapes=[
            pltpu.VMEM((1, QR), jnp.float32),
            pltpu.VMEM((1, QR), jnp.float32),
            pltpu.VMEM((D, QR), jnp.float32),
        ],
        compiler_params=params,
        cost_estimate=cost(2048),
        name="other_parity",
    )(meta, kv_side, ids, qt, m, l, acc)
    out = lax.all_to_all(out.reshape(8, ROWS // 8, GROUP * D), "head", split_axis=0, concat_axis=0, tiled=True)
    return jnp.transpose(out, (1, 0, 2))


def solution(mesh):
    return jax.shard_map(
        per_device,
        mesh=mesh,
        in_specs=(
            P(("seq", "head"), None, None),
            P(("seq", "head"), None, None),
            P(),
            P("seq", None, "head", None),
            P("head", None),
        ),
        out_specs=P(("seq", "head"), None, None),
        check_vma=False,
    )
```

```python
import jax
import jax.numpy as jnp
from jax import lax
from jax.experimental import pallas as pl
from jax.experimental.pallas import tpu as pltpu
from jax.sharding import PartitionSpec as P

D = 128
PAIR = 2 * D
ROWS = 128
GROUP = 8
QR = ROWS * GROUP
NX, NY = 4, 8
PAGES = 32
PAGE = 16
BLOCKS = 4
TILE = 512
SCALE2 = D ** (-0.5) * 1.4426950408889634
LOW = -1e30


def x_shift(by):
    return [
        ((x * NY + y) * 2 + c, ((x + by) * NY + y) * 2 + c)
        for x in range(NX) for y in range(NY) for c in range(2) if 0 <= x + by < NX
    ]


def x_ring(by):
    return [
        ((x * NY + y) * 2 + c, (((x + by) % NX) * NY + y) * 2 + c)
        for x in range(NX) for y in range(NY) for c in range(2)
    ]


def y_ring(by):
    return [
        ((x * NY + y) * 2 + c, (x * NY + (y + by) % NY) * 2 + c)
        for x in range(NX) for y in range(NY) for c in range(2)
    ]


SWAP = [(i, i ^ 1) for i in range(2 * NX * NY)]
Y_GROUPS = [[(x * NY + y) * 2 + c for y in range(NY)] for x in range(NX) for c in range(2)]


def fold(keys, values, mask, qt_ref, m_ref, l_ref, acc_ref):
    twice = jnp.concatenate([keys, keys], axis=1)
    lifted = jnp.concatenate([values.T, jnp.ones((16, keys.shape[0]), jnp.bfloat16)], axis=0)

    def scores_of(at):
        scores = jnp.dot(twice, qt_ref[:, at:at + TILE], preferred_element_type=jnp.float32)
        if mask is not None:
            scores = jnp.where(jnp.concatenate([mask] * (TILE // ROWS), axis=1), scores, LOW)
        return scores

    coming = scores_of(0)
    for at in range(0, QR, TILE):
        cols = slice(at, at + TILE)
        scores = coming
        if at + TILE < QR:
            coming = scores_of(at + TILE)
        old = m_ref[:, cols]
        top = jnp.maximum(old, jnp.max(scores, axis=0, keepdims=True))
        weights = jnp.exp2(scores - top).astype(jnp.bfloat16)
        factor = jnp.exp2(old - top)
        m_ref[:, cols] = top
        mixed = jnp.dot(lifted, weights, preferred_element_type=jnp.float32)
        l_ref[:, cols] = l_ref[:, cols] * factor + mixed[D:D + 1]
        acc_ref[:, cols] = acc_ref[:, cols] * factor + mixed[:D]


def starts_of(ids_ref, own):
    ids = ids_ref[...]
    starts = [jnp.sum((ids < b).astype(jnp.int32)) for b in range(1, 4)]
    own_ids = ids_ref[pl.ds(own, 1), :]
    row_start = jnp.zeros_like(own_ids)
    for b in range(1, 4):
        row_start = jnp.where(own_ids == b, starts[b - 1], row_start)
    return row_start, jnp.min(row_start), jnp.max(row_start)


def mask_of(block, own, row_start):
    key_rows = lax.broadcasted_iota(jnp.int32, (ROWS, ROWS), 0) + block * ROWS
    query_rows = lax.broadcasted_iota(jnp.int32, (ROWS, ROWS), 1) + own * ROWS
    return (key_rows >= row_start) & (key_rows <= query_rows)


def near_kernel(meta_ref, table_ref, q_ref, mine_ref, side_ref, ids_ref, qt_ref, m_ref, l_ref, acc_ref, prefix_ref):
    own = meta_ref[0]
    core, y, x = own % 2, (own // 2) % NY, own // (2 * NY)
    row_start, first, last = starts_of(ids_ref, own)
    for g in range(GROUP):
        scaled = q_ref[:, g * D:(g + 1) * D].astype(jnp.float32) * SCALE2
        high = scaled.astype(jnp.bfloat16)
        low = (scaled - high.astype(jnp.float32)).astype(jnp.bfloat16)
        qt_ref[:D, g * ROWS:(g + 1) * ROWS] = high.T
        qt_ref[D:, g * ROWS:(g + 1) * ROWS] = low.T
    m_ref[...] = jnp.full_like(m_ref, LOW)
    l_ref[...] = jnp.zeros_like(l_ref)
    acc_ref[...] = jnp.zeros_like(acc_ref)
    state = (qt_ref, m_ref, l_ref, acc_ref)
    fold(mine_ref[:ROWS, :D], mine_ref[:ROWS, D:], mask_of(own, own, row_start), *state)

    @pl.when((core == 1) & (own * ROWS > first))
    def _():
        fold(side_ref[:ROWS, :D], side_ref[:ROWS, D:], mask_of(own - 1, own, row_start), *state)

    for i in range(PAGES):
        page = table_ref[i]
        off = (y + NY - (page // 2) % NY) % NY
        unit = (x + NX - page // (2 * NY)) % NX
        shift = jnp.where(off % 4 == 3, 2, jnp.where(off % 4 == 2, 3, off % 4))
        half = jnp.where(off % 4 == 3, 1 - off // 4, off // 4)
        unit = unit + 4 * half + 8 * shift
        rows = pl.ds(pl.multiple_of(ROWS + unit * PAGE, PAGE), PAGE)

        @pl.when(page % 2 == core)
        def _():
            prefix_ref[i * PAGE:(i + 1) * PAGE, :] = mine_ref[rows, :]

        @pl.when(page % 2 != core)
        def _():
            prefix_ref[i * PAGE:(i + 1) * PAGE, :] = side_ref[rows, :]

    fold(prefix_ref[:, :D], prefix_ref[:, D:], None, *state)


def window(kv_ref, core, own, ids_ref, qt_ref, m_ref, l_ref, acc_ref):
    row_start, first, last = starts_of(ids_ref, own)
    chip = own // 2
    x = chip // NY
    lowest = (jnp.maximum(first // ROWS - core, -1) + 1) // 2
    steps = jnp.maximum(chip - lowest + BLOCKS - 1, 0) // BLOCKS

    def step(i, carry):
        base = chip - BLOCKS * (i + 1)
        pairs = []
        for b in range(BLOCKS):
            at = jnp.maximum(base + b, 0)
            slot = (at % NY) * 2 + jnp.where(at // NY == x - 1, 0, 1)
            pairs.append(kv_ref[pl.ds(pl.multiple_of(slot * ROWS, ROWS), ROWS), :])
        keys = jnp.concatenate([pair[:, :D] for pair in pairs], axis=0)
        values = jnp.concatenate([pair[:, D:] for pair in pairs], axis=0)
        whole = (2 * base + core) * ROWS >= last

        @pl.when(whole)
        def _():
            fold(keys, values, None, qt_ref, m_ref, l_ref, acc_ref)

        @pl.when(jnp.logical_not(whole))
        def _():
            mask = jnp.concatenate(
                [mask_of(2 * (base + b) + core, own, row_start) for b in range(BLOCKS)], axis=0
            )
            fold(keys, values, mask, qt_ref, m_ref, l_ref, acc_ref)

        return carry

    lax.fori_loop(0, steps, step, 0)


def own_kernel(meta_ref, kv_ref, ids_ref, qt_ref, m_in, l_in, acc_in, m_ref, l_ref, acc_ref):
    m_ref[...] = m_in[...]
    l_ref[...] = l_in[...]
    acc_ref[...] = acc_in[...]
    own = meta_ref[0]
    window(kv_ref, own % 2, own, ids_ref, qt_ref, m_ref, l_ref, acc_ref)


def last_kernel(meta_ref, kv_ref, ids_ref, qt_ref, m_in, l_in, acc_in, out_ref, m_ref, l_ref, acc_ref):
    m_ref[...] = m_in[...]
    l_ref[...] = l_in[...]
    acc_ref[...] = acc_in[...]
    own = meta_ref[0]
    window(kv_ref, 1 - own % 2, own, ids_ref, qt_ref, m_ref, l_ref, acc_ref)
    result = (acc_ref[...] * (1.0 / l_ref[...])).astype(jnp.bfloat16)
    for g in range(GROUP):
        out_ref[:, g * D:(g + 1) * D] = result[:, g * ROWS:(g + 1) * ROWS].T


VM = pl.BlockSpec(memory_space=pltpu.VMEM)
SM = pl.BlockSpec(memory_space=pltpu.SMEM)


def cost(keys):
    return pl.CostEstimate(flops=4 * D * QR * keys, bytes_accessed=1 << 20, transcendentals=QR * keys)


def per_device(queries, branch_key_value, branch_ids, pool, page_table):
    me = lax.axis_index("seq")
    y = (me // 2) % NY
    page = pool.reshape(1, PAGE, PAIR)
    raw = jnp.concatenate([jnp.transpose(branch_key_value, (1, 0, 2)), page], axis=0)
    two_raw = lax.ppermute(raw, "seq", x_ring(2))
    one_raw = lax.ppermute(raw, "seq", x_ring(1))
    three_page = lax.ppermute(page, "seq", x_ring(3))
    wide = jnp.concatenate([jnp.transpose(queries, (1, 0, 2)), raw[:8], one_raw[:8], two_raw[:8]], axis=2)
    wide = lax.all_to_all(wide, "head", split_axis=0, concat_axis=0, tiled=True).reshape(ROWS, -1)
    at = GROUP * D
    own, one_back, two_back = (wide[:, at + i * PAIR:at + (i + 1) * PAIR] for i in range(3))
    pages = jnp.concatenate([page, one_raw[8:], two_raw[8:], three_page], axis=0)
    pages = jnp.concatenate([pages, lax.ppermute(pages, "seq", y_ring(4))], axis=0)
    target = jnp.arange(NY, dtype=jnp.int32)[:, None, None]
    mixed = jnp.where(target > y, own[None], two_back[None])
    send = jnp.stack([jnp.broadcast_to(one_back[None], mixed.shape), mixed], axis=1)
    kv = lax.all_to_all(send, "seq", split_axis=0, concat_axis=0, tiled=True, axis_index_groups=Y_GROUPS)
    kv = kv.reshape(2 * NY * ROWS, PAIR)
    later, _ = lax.optimization_barrier((pages, send))
    pages = jnp.concatenate([pages] + [lax.ppermute(later, "seq", y_ring(k)) for k in (1, -1, 2)], axis=0)
    mine = jnp.concatenate([own, pages.reshape(PAGES * PAGE, PAIR)], axis=0)
    side = lax.ppermute(mine, "seq", SWAP)
    ids = branch_ids.reshape(2 * NX * NY, ROWS)
    meta = me.astype(jnp.int32).reshape(1)
    state = [
        jax.ShapeDtypeStruct((1, QR), jnp.float32),
        jax.ShapeDtypeStruct((1, QR), jnp.float32),
        jax.ShapeDtypeStruct((D, QR), jnp.float32),
    ]
    params = pltpu.CompilerParams(vmem_limit_bytes=40 * 1024 * 1024)
    qt, m, l, acc = pl.pallas_call(
        near_kernel,
        out_shape=[jax.ShapeDtypeStruct((PAIR, QR), jnp.bfloat16)] + state,
        in_specs=[SM, SM, VM, VM, VM, VM],
        out_specs=[VM] * 4,
        scratch_shapes=[pltpu.VMEM((PAGES * PAGE, PAIR), jnp.bfloat16)],
        compiler_params=params,
        cost_estimate=cost(768),
        name="near_keys",
    )(meta, page_table.reshape(PAGES), wide, mine, side, ids)
    kv, m = lax.optimization_barrier((kv, m))
    kv_side = lax.ppermute(kv, "seq", SWAP)
    m, l, acc = pl.pallas_call(
        own_kernel,
        out_shape=state,
        in_specs=[SM] + [VM] * 6,
        out_specs=[VM] * 3,
        compiler_params=params,
        cost_estimate=cost(2048),
        name="own_parity",
    )(meta, kv, ids, qt, m, l, acc)
    out = pl.pallas_call(
        last_kernel,
        out_shape=jax.ShapeDtypeStruct((ROWS, GROUP * D), jnp.bfloat16),
        in_specs=[SM] + [VM] * 6,
        out_specs=VM,
        scratch_shapes=[
            pltpu.VMEM((1, QR), jnp.float32),
            pltpu.VMEM((1, QR), jnp.float32),
            pltpu.VMEM((D, QR), jnp.float32),
        ],
        compiler_params=params,
        cost_estimate=cost(2048),
        name="other_parity",
    )(meta, kv_side, ids, qt, m, l, acc)
    out = lax.all_to_all(out.reshape(8, ROWS // 8, GROUP * D), "head", split_axis=0, concat_axis=0, tiled=True)
    return jnp.transpose(out, (1, 0, 2))


def solution(mesh):
    return jax.shard_map(
        per_device,
        mesh=mesh,
        in_specs=(
            P(("seq", "head"), None, None),
            P(("seq", "head"), None, None),
            P(),
            P("seq", None, "head", None),
            P("head", None),
        ),
        out_specs=P(("seq", "head"), None, None),
        check_vma=False,
    )
```

```python
import jax
import jax.numpy as jnp
from jax import lax
from jax.experimental import pallas as pl
from jax.experimental.pallas import tpu as pltpu
from jax.sharding import PartitionSpec as P

D = 128
PAIR = 2 * D
ROWS = 128
GROUP = 8
QR = ROWS * GROUP
NX, NY = 4, 8
PAGES = 32
PAGE = 16
BLOCKS = 4
TILE = 512
SCALE2 = D ** (-0.5) * 1.4426950408889634
LOW = -1e30


def x_shift(by):
    return [
        ((x * NY + y) * 2 + c, ((x + by) * NY + y) * 2 + c)
        for x in range(NX) for y in range(NY) for c in range(2) if 0 <= x + by < NX
    ]


def x_ring(by):
    return [
        ((x * NY + y) * 2 + c, (((x + by) % NX) * NY + y) * 2 + c)
        for x in range(NX) for y in range(NY) for c in range(2)
    ]


def y_ring(by):
    return [
        ((x * NY + y) * 2 + c, (x * NY + (y + by) % NY) * 2 + c)
        for x in range(NX) for y in range(NY) for c in range(2)
    ]


SWAP = [(i, i ^ 1) for i in range(2 * NX * NY)]
Y_GROUPS = [[(x * NY + y) * 2 + c for y in range(NY)] for x in range(NX) for c in range(2)]


def fold(keys, values, mask, qt_ref, m_ref, l_ref, acc_ref):
    twice = jnp.concatenate([keys, keys], axis=1)
    lifted = jnp.concatenate([values.T, jnp.ones((16, keys.shape[0]), jnp.bfloat16)], axis=0)

    def scores_of(at):
        scores = jnp.dot(twice, qt_ref[:, at:at + TILE], preferred_element_type=jnp.float32)
        if mask is not None:
            scores = jnp.where(jnp.concatenate([mask] * (TILE // ROWS), axis=1), scores, LOW)
        return scores

    coming = scores_of(0)
    for at in range(0, QR, TILE):
        cols = slice(at, at + TILE)
        scores = coming
        if at + TILE < QR:
            coming = scores_of(at + TILE)
        old = m_ref[:, cols]
        top = jnp.maximum(old, jnp.max(scores, axis=0, keepdims=True))
        weights = jnp.exp2(scores - top).astype(jnp.bfloat16)
        factor = jnp.exp2(old - top)
        m_ref[:, cols] = top
        mixed = jnp.dot(lifted, weights, preferred_element_type=jnp.float32)
        l_ref[:, cols] = l_ref[:, cols] * factor + mixed[D:D + 1]
        acc_ref[:, cols] = acc_ref[:, cols] * factor + mixed[:D]


def starts_of(ids_ref, own):
    ids = ids_ref[...]
    starts = [jnp.sum((ids < b).astype(jnp.int32)) for b in range(1, 4)]
    own_ids = ids_ref[pl.ds(own, 1), :]
    row_start = jnp.zeros_like(own_ids)
    for b in range(1, 4):
        row_start = jnp.where(own_ids == b, starts[b - 1], row_start)
    return row_start, jnp.min(row_start), jnp.max(row_start)


def mask_of(block, own, row_start):
    key_rows = lax.broadcasted_iota(jnp.int32, (ROWS, ROWS), 0) + block * ROWS
    query_rows = lax.broadcasted_iota(jnp.int32, (ROWS, ROWS), 1) + own * ROWS
    return (key_rows >= row_start) & (key_rows <= query_rows)


def near_kernel(meta_ref, table_ref, q_ref, mine_ref, side_ref, ids_ref, qt_ref, m_ref, l_ref, acc_ref, prefix_ref):
    own = meta_ref[0]
    core, y, x = own % 2, (own // 2) % NY, own // (2 * NY)
    row_start, first, last = starts_of(ids_ref, own)
    for g in range(GROUP):
        scaled = q_ref[:, g * D:(g + 1) * D].astype(jnp.float32) * SCALE2
        high = scaled.astype(jnp.bfloat16)
        low = (scaled - high.astype(jnp.float32)).astype(jnp.bfloat16)
        qt_ref[:D, g * ROWS:(g + 1) * ROWS] = high.T
        qt_ref[D:, g * ROWS:(g + 1) * ROWS] = low.T
    m_ref[...] = jnp.full_like(m_ref, LOW)
    l_ref[...] = jnp.zeros_like(l_ref)
    acc_ref[...] = jnp.zeros_like(acc_ref)
    state = (qt_ref, m_ref, l_ref, acc_ref)
    fold(mine_ref[:ROWS, :D], mine_ref[:ROWS, D:], mask_of(own, own, row_start), *state)

    @pl.when((core == 1) & (own * ROWS > first))
    def _():
        fold(side_ref[:ROWS, :D], side_ref[:ROWS, D:], mask_of(own - 1, own, row_start), *state)

    for i in range(PAGES):
        page = table_ref[i]
        off = (y + NY - (page // 2) % NY) % NY
        shift = jnp.where(off % 4 == 3, 2, jnp.where(off % 4 == 2, 3, off % 4))
        half = jnp.where(off % 4 == 3, 1 - off // 4, off // 4)
        unit = NY * ((x + NX - page // (2 * NY)) % NX) + half + 2 * shift
        rows = pl.ds(pl.multiple_of(ROWS + unit * PAGE, PAGE), PAGE)

        @pl.when(page % 2 == core)
        def _():
            prefix_ref[i * PAGE:(i + 1) * PAGE, :] = mine_ref[rows, :]

        @pl.when(page % 2 != core)
        def _():
            prefix_ref[i * PAGE:(i + 1) * PAGE, :] = side_ref[rows, :]

    fold(prefix_ref[:, :D], prefix_ref[:, D:], None, *state)


def window(kv_ref, core, own, ids_ref, qt_ref, m_ref, l_ref, acc_ref):
    row_start, first, last = starts_of(ids_ref, own)
    chip = own // 2
    x = chip // NY
    lowest = (jnp.maximum(first // ROWS - core, -1) + 1) // 2
    steps = jnp.maximum(chip - lowest + BLOCKS - 1, 0) // BLOCKS

    def step(i, carry):
        base = chip - BLOCKS * (i + 1)
        pairs = []
        for b in range(BLOCKS):
            at = jnp.maximum(base + b, 0)
            slot = (at % NY) * 2 + jnp.where(at // NY == x - 1, 0, 1)
            pairs.append(kv_ref[pl.ds(pl.multiple_of(slot * ROWS, ROWS), ROWS), :])
        keys = jnp.concatenate([pair[:, :D] for pair in pairs], axis=0)
        values = jnp.concatenate([pair[:, D:] for pair in pairs], axis=0)
        whole = (2 * base + core) * ROWS >= last

        @pl.when(whole)
        def _():
            fold(keys, values, None, qt_ref, m_ref, l_ref, acc_ref)

        @pl.when(jnp.logical_not(whole))
        def _():
            mask = jnp.concatenate(
                [mask_of(2 * (base + b) + core, own, row_start) for b in range(BLOCKS)], axis=0
            )
            fold(keys, values, mask, qt_ref, m_ref, l_ref, acc_ref)

        return carry

    lax.fori_loop(0, steps, step, 0)


def own_kernel(meta_ref, kv_ref, ids_ref, qt_ref, m_in, l_in, acc_in, m_ref, l_ref, acc_ref):
    m_ref[...] = m_in[...]
    l_ref[...] = l_in[...]
    acc_ref[...] = acc_in[...]
    own = meta_ref[0]
    window(kv_ref, own % 2, own, ids_ref, qt_ref, m_ref, l_ref, acc_ref)


def last_kernel(meta_ref, kv_ref, ids_ref, qt_ref, m_in, l_in, acc_in, out_ref, m_ref, l_ref, acc_ref):
    m_ref[...] = m_in[...]
    l_ref[...] = l_in[...]
    acc_ref[...] = acc_in[...]
    own = meta_ref[0]
    window(kv_ref, 1 - own % 2, own, ids_ref, qt_ref, m_ref, l_ref, acc_ref)
    result = (acc_ref[...] * (1.0 / l_ref[...])).astype(jnp.bfloat16)
    for g in range(GROUP):
        out_ref[:, g * D:(g + 1) * D] = result[:, g * ROWS:(g + 1) * ROWS].T


VM = pl.BlockSpec(memory_space=pltpu.VMEM)
SM = pl.BlockSpec(memory_space=pltpu.SMEM)


def cost(keys):
    return pl.CostEstimate(flops=4 * D * QR * keys, bytes_accessed=1 << 20, transcendentals=QR * keys)


def per_device(queries, branch_key_value, branch_ids, pool, page_table):
    me = lax.axis_index("seq")
    y = (me // 2) % NY
    page = pool.reshape(1, PAGE, PAIR)
    pages = jnp.concatenate([page, lax.ppermute(page, "seq", y_ring(4))], axis=0)
    raw = jnp.transpose(branch_key_value, (1, 0, 2))
    two_raw = lax.ppermute(raw, "seq", x_shift(2))
    one_raw = lax.ppermute(raw, "seq", x_shift(1))
    wide = jnp.concatenate([jnp.transpose(queries, (1, 0, 2)), raw, one_raw, two_raw], axis=2)
    wide = lax.all_to_all(wide, "head", split_axis=0, concat_axis=0, tiled=True).reshape(ROWS, -1)
    pages = jnp.concatenate([pages] + [lax.ppermute(pages, "seq", y_ring(k)) for k in (1, -1, 2)], axis=0)
    wide, pages = lax.optimization_barrier((wide, pages))
    at = GROUP * D
    own, one_back, two_back = (wide[:, at + i * PAIR:at + (i + 1) * PAIR] for i in range(3))
    target = jnp.arange(NY, dtype=jnp.int32)[:, None, None]
    mixed = jnp.where(target > y, own[None], two_back[None])
    send = jnp.stack([jnp.broadcast_to(one_back[None], mixed.shape), mixed], axis=1)
    kv = lax.all_to_all(send, "seq", split_axis=0, concat_axis=0, tiled=True, axis_index_groups=Y_GROUPS)
    kv = kv.reshape(2 * NY * ROWS, PAIR)
    later, _ = lax.optimization_barrier((pages, send))
    pages = jnp.concatenate([pages] + [lax.ppermute(later, "seq", x_ring(k)) for k in (1, 2, 3)], axis=0)
    mine = jnp.concatenate([own, pages.reshape(PAGES * PAGE, PAIR)], axis=0)
    side = lax.ppermute(mine, "seq", SWAP)
    ids = branch_ids.reshape(2 * NX * NY, ROWS)
    meta = me.astype(jnp.int32).reshape(1)
    state = [
        jax.ShapeDtypeStruct((1, QR), jnp.float32),
        jax.ShapeDtypeStruct((1, QR), jnp.float32),
        jax.ShapeDtypeStruct((D, QR), jnp.float32),
    ]
    params = pltpu.CompilerParams(vmem_limit_bytes=40 * 1024 * 1024)
    qt, m, l, acc = pl.pallas_call(
        near_kernel,
        out_shape=[jax.ShapeDtypeStruct((PAIR, QR), jnp.bfloat16)] + state,
        in_specs=[SM, SM, VM, VM, VM, VM],
        out_specs=[VM] * 4,
        scratch_shapes=[pltpu.VMEM((PAGES * PAGE, PAIR), jnp.bfloat16)],
        compiler_params=params,
        cost_estimate=cost(768),
        name="near_keys",
    )(meta, page_table.reshape(PAGES), wide, mine, side, ids)
    kv, m = lax.optimization_barrier((kv, m))
    kv_side = lax.ppermute(kv, "seq", SWAP)
    m, l, acc = pl.pallas_call(
        own_kernel,
        out_shape=state,
        in_specs=[SM] + [VM] * 6,
        out_specs=[VM] * 3,
        compiler_params=params,
        cost_estimate=cost(2048),
        name="own_parity",
    )(meta, kv, ids, qt, m, l, acc)
    out = pl.pallas_call(
        last_kernel,
        out_shape=jax.ShapeDtypeStruct((ROWS, GROUP * D), jnp.bfloat16),
        in_specs=[SM] + [VM] * 6,
        out_specs=VM,
        scratch_shapes=[
            pltpu.VMEM((1, QR), jnp.float32),
            pltpu.VMEM((1, QR), jnp.float32),
            pltpu.VMEM((D, QR), jnp.float32),
        ],
        compiler_params=params,
        cost_estimate=cost(2048),
        name="other_parity",
    )(meta, kv_side, ids, qt, m, l, acc)
    out = lax.all_to_all(out.reshape(8, ROWS // 8, GROUP * D), "head", split_axis=0, concat_axis=0, tiled=True)
    return jnp.transpose(out, (1, 0, 2))


def solution(mesh):
    return jax.shard_map(
        per_device,
        mesh=mesh,
        in_specs=(
            P(("seq", "head"), None, None),
            P(("seq", "head"), None, None),
            P(),
            P("seq", None, "head", None),
            P("head", None),
        ),
        out_specs=P(("seq", "head"), None, None),
        check_vma=False,
    )
```

```python
import jax
import jax.numpy as jnp
from jax import lax
from jax.experimental import pallas as pl
from jax.experimental.pallas import tpu as pltpu
from jax.sharding import PartitionSpec as P

D = 128
PAIR = 2 * D
ROWS = 128
GROUP = 8
QR = ROWS * GROUP
NX, NY = 4, 8
PAGES = 32
PAGE = 16
BLOCKS = 4
TILE = 512
SCALE2 = D ** (-0.5) * 1.4426950408889634
LOW = -1e30
SLOT = 2 * ROWS + NX * PAGE


def x_ring(by):
    return [
        ((x * NY + y) * 2 + c, (((x + by) % NX) * NY + y) * 2 + c)
        for x in range(NX) for y in range(NY) for c in range(2)
    ]


SWAP = [(i, i ^ 1) for i in range(2 * NX * NY)]
Y_GROUPS = [[(x * NY + y) * 2 + c for y in range(NY)] for x in range(NX) for c in range(2)]


def fold(keys, values, mask, qt_ref, m_ref, l_ref, acc_ref):
    twice = jnp.concatenate([keys, keys], axis=1)
    lifted = jnp.concatenate([values.T, jnp.ones((16, keys.shape[0]), jnp.bfloat16)], axis=0)

    def scores_of(at):
        scores = jnp.dot(twice, qt_ref[:, at:at + TILE], preferred_element_type=jnp.float32)
        if mask is not None:
            scores = jnp.where(jnp.concatenate([mask] * (TILE // ROWS), axis=1), scores, LOW)
        return scores

    coming = scores_of(0)
    for at in range(0, QR, TILE):
        cols = slice(at, at + TILE)
        scores = coming
        if at + TILE < QR:
            coming = scores_of(at + TILE)
        old = m_ref[:, cols]
        top = jnp.maximum(old, jnp.max(scores, axis=0, keepdims=True))
        weights = jnp.exp2(scores - top).astype(jnp.bfloat16)
        factor = jnp.exp2(old - top)
        m_ref[:, cols] = top
        mixed = jnp.dot(lifted, weights, preferred_element_type=jnp.float32)
        l_ref[:, cols] = l_ref[:, cols] * factor + mixed[D:D + 1]
        acc_ref[:, cols] = acc_ref[:, cols] * factor + mixed[:D]


def starts_of(ids_ref, own):
    ids = ids_ref[...]
    starts = [jnp.sum((ids < b).astype(jnp.int32)) for b in range(1, 4)]
    own_ids = ids_ref[pl.ds(own, 1), :]
    row_start = jnp.zeros_like(own_ids)
    for b in range(1, 4):
        row_start = jnp.where(own_ids == b, starts[b - 1], row_start)
    return row_start, jnp.min(row_start), jnp.max(row_start)


def mask_of(block, own, row_start):
    key_rows = lax.broadcasted_iota(jnp.int32, (ROWS, ROWS), 0) + block * ROWS
    query_rows = lax.broadcasted_iota(jnp.int32, (ROWS, ROWS), 1) + own * ROWS
    return (key_rows >= row_start) & (key_rows <= query_rows)


def near_kernel(meta_ref, mine_ref, side_ref, ids_ref, *refs):
    q_refs, (qt_ref, m_ref, l_ref, acc_ref, q_ref) = refs[:8], refs[8:]
    own, z = meta_ref[0], meta_ref[1]
    row_start, first, last = starts_of(ids_ref, own)
    for k in range(8):
        source = (z + 8 - k) % 8
        q_ref[pl.ds(pl.multiple_of(source * 16, 16), 16), :] = q_refs[k][...]
    for g in range(GROUP):
        scaled = q_ref[:, g * D:(g + 1) * D].astype(jnp.float32) * SCALE2
        high = scaled.astype(jnp.bfloat16)
        low = (scaled - high.astype(jnp.float32)).astype(jnp.bfloat16)
        qt_ref[:D, g * ROWS:(g + 1) * ROWS] = high.T
        qt_ref[D:, g * ROWS:(g + 1) * ROWS] = low.T
    m_ref[...] = jnp.full_like(m_ref, LOW)
    l_ref[...] = jnp.zeros_like(l_ref)
    acc_ref[...] = jnp.zeros_like(acc_ref)
    state = (qt_ref, m_ref, l_ref, acc_ref)
    fold(mine_ref[:, :D], mine_ref[:, D:], mask_of(own, own, row_start), *state)

    @pl.when((own % 2 == 1) & (own * ROWS > first))
    def _():
        fold(side_ref[:, :D], side_ref[:, D:], mask_of(own - 1, own, row_start), *state)


def window(kv_ref, core, own, ids_ref, qt_ref, m_ref, l_ref, acc_ref):
    row_start, first, last = starts_of(ids_ref, own)
    chip = own // 2
    x = chip // NY
    lowest = (jnp.maximum(first // ROWS - core, -1) + 1) // 2
    steps = jnp.maximum(chip - lowest + BLOCKS - 1, 0) // BLOCKS

    def step(i, carry):
        base = chip - BLOCKS * (i + 1)
        pairs = []
        for b in range(BLOCKS):
            at = jnp.maximum(base + b, 0)
            start = (at % NY) * SLOT + jnp.where(at // NY == x - 1, 0, ROWS)
            pairs.append(kv_ref[pl.ds(pl.multiple_of(start, PAGE), ROWS), :])
        keys = jnp.concatenate([pair[:, :D] for pair in pairs], axis=0)
        values = jnp.concatenate([pair[:, D:] for pair in pairs], axis=0)
        whole = (2 * base + core) * ROWS >= last

        @pl.when(whole)
        def _():
            fold(keys, values, None, qt_ref, m_ref, l_ref, acc_ref)

        @pl.when(jnp.logical_not(whole))
        def _():
            mask = jnp.concatenate(
                [mask_of(2 * (base + b) + core, own, row_start) for b in range(BLOCKS)], axis=0
            )
            fold(keys, values, mask, qt_ref, m_ref, l_ref, acc_ref)

        return carry

    lax.fori_loop(0, steps, step, 0)


def own_kernel(meta_ref, kv_ref, ids_ref, qt_ref, m_in, l_in, acc_in, m_ref, l_ref, acc_ref):
    m_ref[...] = m_in[...]
    l_ref[...] = l_in[...]
    acc_ref[...] = acc_in[...]
    own = meta_ref[0]
    window(kv_ref, own % 2, own, ids_ref, qt_ref, m_ref, l_ref, acc_ref)


def last_kernel(meta_ref, table_ref, mine_ref, kv_ref, ids_ref, qt_ref, m_in, l_in, acc_in,
                out_ref, m_ref, l_ref, acc_ref, prefix_ref):
    m_ref[...] = m_in[...]
    l_ref[...] = l_in[...]
    acc_ref[...] = acc_in[...]
    own = meta_ref[0]
    core, x = own % 2, own // (2 * NY)
    for i in range(PAGES):
        page = table_ref[i]
        start = (page // 2) % NY * SLOT + 2 * ROWS + (x + NX - page // (2 * NY)) % NX * PAGE
        rows = pl.ds(pl.multiple_of(start, PAGE), PAGE)

        @pl.when(page % 2 == core)
        def _():
            prefix_ref[i * PAGE:(i + 1) * PAGE, :] = mine_ref[rows, :]

        @pl.when(page % 2 != core)
        def _():
            prefix_ref[i * PAGE:(i + 1) * PAGE, :] = kv_ref[rows, :]

    fold(prefix_ref[:, :D], prefix_ref[:, D:], None, qt_ref, m_ref, l_ref, acc_ref)
    window(kv_ref, 1 - core, own, ids_ref, qt_ref, m_ref, l_ref, acc_ref)
    result = (acc_ref[...] * (1.0 / l_ref[...])).astype(jnp.bfloat16)
    for g in range(GROUP):
        out_ref[:, g * D:(g + 1) * D] = result[:, g * ROWS:(g + 1) * ROWS].T


VM = pl.BlockSpec(memory_space=pltpu.VMEM)
SM = pl.BlockSpec(memory_space=pltpu.SMEM)


def cost(keys):
    return pl.CostEstimate(flops=4 * D * QR * keys, bytes_accessed=1 << 20, transcendentals=QR * keys)


def per_device(queries, branch_key_value, branch_ids, pool, page_table):
    me = lax.axis_index("seq")
    y = (me // 2) % NY
    z = lax.axis_index("head")
    page = pool.reshape(PAGE, PAIR)
    own = lax.all_to_all(
        jnp.transpose(branch_key_value, (1, 0, 2)), "head", split_axis=0, concat_axis=0, tiled=True
    ).reshape(ROWS, PAIR)
    three_page = lax.ppermute(page, "seq", x_ring(3))
    own, three_page = lax.optimization_barrier((own, three_page))
    near = jnp.concatenate([own, page], axis=0)
    two_back = lax.ppermute(near, "seq", x_ring(2))
    one_back = lax.ppermute(near, "seq", x_ring(1))
    target = jnp.arange(NY, dtype=jnp.int32)[:, None, None]
    mixed = jnp.where(target > y, own[None], two_back[None, :ROWS])
    pages = jnp.concatenate([page, one_back[ROWS:], two_back[ROWS:], three_page], axis=0)
    send = jnp.concatenate([
        jnp.broadcast_to(one_back[None, :ROWS], mixed.shape), mixed,
        jnp.broadcast_to(pages[None], (NY, NX * PAGE, PAIR)),
    ], axis=1)
    kv = lax.all_to_all(send, "seq", split_axis=0, concat_axis=0, tiled=True, axis_index_groups=Y_GROUPS)
    kv = kv.reshape(NY * SLOT, PAIR)
    by_head, later, _ = lax.optimization_barrier((jnp.transpose(queries, (1, 0, 2)), own, send))
    side = lax.ppermute(later, "seq", SWAP)
    parts = [lax.dynamic_index_in_dim(by_head, z, 0, keepdims=False)]
    for k in range(1, 8):
        part = lax.dynamic_index_in_dim(by_head, (z + k) % 8, 0, keepdims=False)
        parts.append(lax.ppermute(part, "head", [(i, (i + k) % 8) for i in range(8)]))

    ids = branch_ids.reshape(2 * NX * NY, ROWS)
    meta = jnp.stack([me, z]).astype(jnp.int32)
    state = [
        jax.ShapeDtypeStruct((1, QR), jnp.float32),
        jax.ShapeDtypeStruct((1, QR), jnp.float32),
        jax.ShapeDtypeStruct((D, QR), jnp.float32),
    ]
    params = pltpu.CompilerParams(vmem_limit_bytes=40 * 1024 * 1024)
    qt, m, l, acc = pl.pallas_call(
        near_kernel,
        out_shape=[jax.ShapeDtypeStruct((PAIR, QR), jnp.bfloat16)] + state,
        in_specs=[SM] + [VM] * 11,
        out_specs=[VM] * 4,
        scratch_shapes=[pltpu.VMEM((ROWS, GROUP * D), jnp.bfloat16)],
        compiler_params=params,
        cost_estimate=cost(256),
        name="near_keys",
    )(meta, own, side, ids, *parts)
    kv, m = lax.optimization_barrier((kv, m))
    kv_side = lax.ppermute(kv, "seq", SWAP)
    m, l, acc = pl.pallas_call(
        own_kernel,
        out_shape=state,
        in_specs=[SM] + [VM] * 6,
        out_specs=[VM] * 3,
        compiler_params=params,
        cost_estimate=cost(2048),
        name="own_parity",
    )(meta, kv, ids, qt, m, l, acc)
    out = pl.pallas_call(
        last_kernel,
        out_shape=jax.ShapeDtypeStruct((ROWS, GROUP * D), jnp.bfloat16),
        in_specs=[SM, SM] + [VM] * 7,
        out_specs=VM,
        scratch_shapes=[
            pltpu.VMEM((1, QR), jnp.float32),
            pltpu.VMEM((1, QR), jnp.float32),
            pltpu.VMEM((D, QR), jnp.float32),
            pltpu.VMEM((PAGES * PAGE, PAIR), jnp.bfloat16),
        ],
        compiler_params=params,
        cost_estimate=cost(2560),
        name="other_parity",
    )(meta, page_table.reshape(PAGES), kv, kv_side, ids, qt, m, l, acc)
    out = lax.all_to_all(out.reshape(8, ROWS // 8, GROUP * D), "head", split_axis=0, concat_axis=0, tiled=True)
    return jnp.transpose(out, (1, 0, 2))


def solution(mesh):
    return jax.shard_map(
        per_device,
        mesh=mesh,
        in_specs=(
            P(("seq", "head"), None, None),
            P(("seq", "head"), None, None),
            P(),
            P("seq", None, "head", None),
            P("head", None),
        ),
        out_specs=P(("seq", "head"), None, None),
        check_vma=False,
    )
```

```python
import jax
import jax.numpy as jnp
from jax import lax
from jax.experimental import pallas as pl
from jax.experimental.pallas import tpu as pltpu
from jax.sharding import PartitionSpec as P

D = 128
PAIR = 2 * D
ROWS = 128
GROUP = 8
QR = ROWS * GROUP
NX, NY = 4, 8
PAGES = 32
PAGE = 16
BLOCKS = 4
TILE = 512
SCALE2 = D ** (-0.5) * 1.4426950408889634
LOW = -1e30
SLOT = 2 * ROWS + NX * PAGE


def x_ring(by):
    return [
        ((x * NY + y) * 2 + c, (((x + by) % NX) * NY + y) * 2 + c)
        for x in range(NX) for y in range(NY) for c in range(2)
    ]


SWAP = [(i, i ^ 1) for i in range(2 * NX * NY)]
Y_GROUPS = [[(x * NY + y) * 2 + c for y in range(NY)] for x in range(NX) for c in range(2)]


def fold(keys, values, mask, qt_ref, m_ref, l_ref, acc_ref):
    twice = jnp.concatenate([keys, keys], axis=1)
    lifted = jnp.concatenate([values.T, jnp.ones((16, keys.shape[0]), jnp.bfloat16)], axis=0)

    def scores_of(at):
        scores = jnp.dot(twice, qt_ref[:, at:at + TILE], preferred_element_type=jnp.float32)
        if mask is not None:
            scores = jnp.where(jnp.concatenate([mask] * (TILE // ROWS), axis=1), scores, LOW)
        return scores

    coming = scores_of(0)
    for at in range(0, QR, TILE):
        cols = slice(at, at + TILE)
        scores = coming
        if at + TILE < QR:
            coming = scores_of(at + TILE)
        old = m_ref[:, cols]
        top = jnp.maximum(old, jnp.max(scores, axis=0, keepdims=True))
        weights = jnp.exp2(scores - top).astype(jnp.bfloat16)
        factor = jnp.exp2(old - top)
        m_ref[:, cols] = top
        mixed = jnp.dot(lifted, weights, preferred_element_type=jnp.float32)
        l_ref[:, cols] = l_ref[:, cols] * factor + mixed[D:D + 1]
        acc_ref[:, cols] = acc_ref[:, cols] * factor + mixed[:D]


def starts_of(ids_ref, own):
    ids = ids_ref[...]
    starts = [jnp.sum((ids < b).astype(jnp.int32)) for b in range(1, 4)]
    own_ids = ids_ref[pl.ds(own, 1), :]
    row_start = jnp.zeros_like(own_ids)
    for b in range(1, 4):
        row_start = jnp.where(own_ids == b, starts[b - 1], row_start)
    return row_start, jnp.min(row_start), jnp.max(row_start)


def mask_of(block, own, row_start):
    key_rows = lax.broadcasted_iota(jnp.int32, (ROWS, ROWS), 0) + block * ROWS
    query_rows = lax.broadcasted_iota(jnp.int32, (ROWS, ROWS), 1) + own * ROWS
    return (key_rows >= row_start) & (key_rows <= query_rows)


def near_kernel(meta_ref, mine_ref, side_ref, ids_ref, q_ref, qt_ref, m_ref, l_ref, acc_ref):
    own = meta_ref[0]
    row_start, first, last = starts_of(ids_ref, own)
    for g in range(GROUP):
        scaled = q_ref[:, g * D:(g + 1) * D].astype(jnp.float32) * SCALE2
        high = scaled.astype(jnp.bfloat16)
        low = (scaled - high.astype(jnp.float32)).astype(jnp.bfloat16)
        qt_ref[:D, g * ROWS:(g + 1) * ROWS] = high.T
        qt_ref[D:, g * ROWS:(g + 1) * ROWS] = low.T
    m_ref[...] = jnp.full_like(m_ref, LOW)
    l_ref[...] = jnp.zeros_like(l_ref)
    acc_ref[...] = jnp.zeros_like(acc_ref)
    state = (qt_ref, m_ref, l_ref, acc_ref)
    fold(mine_ref[:, :D], mine_ref[:, D:], mask_of(own, own, row_start), *state)

    @pl.when((own % 2 == 1) & (own * ROWS > first))
    def _():
        fold(side_ref[:, :D], side_ref[:, D:], mask_of(own - 1, own, row_start), *state)


def window(kv_ref, core, own, ids_ref, qt_ref, m_ref, l_ref, acc_ref):
    row_start, first, last = starts_of(ids_ref, own)
    chip = own // 2
    x = chip // NY
    lowest = (jnp.maximum(first // ROWS - core, -1) + 1) // 2
    steps = jnp.maximum(chip - lowest + BLOCKS - 1, 0) // BLOCKS

    def step(i, carry):
        base = chip - BLOCKS * (i + 1)
        pairs = []
        for b in range(BLOCKS):
            at = jnp.maximum(base + b, 0)
            start = (at % NY) * SLOT + jnp.where(at // NY == x - 1, 0, ROWS)
            pairs.append(kv_ref[pl.ds(pl.multiple_of(start, PAGE), ROWS), :])
        keys = jnp.concatenate([pair[:, :D] for pair in pairs], axis=0)
        values = jnp.concatenate([pair[:, D:] for pair in pairs], axis=0)
        whole = (2 * base + core) * ROWS >= last

        @pl.when(whole)
        def _():
            fold(keys, values, None, qt_ref, m_ref, l_ref, acc_ref)

        @pl.when(jnp.logical_not(whole))
        def _():
            mask = jnp.concatenate(
                [mask_of(2 * (base + b) + core, own, row_start) for b in range(BLOCKS)], axis=0
            )
            fold(keys, values, mask, qt_ref, m_ref, l_ref, acc_ref)

        return carry

    lax.fori_loop(0, steps, step, 0)


def own_kernel(meta_ref, kv_ref, ids_ref, qt_ref, m_in, l_in, acc_in, m_ref, l_ref, acc_ref):
    m_ref[...] = m_in[...]
    l_ref[...] = l_in[...]
    acc_ref[...] = acc_in[...]
    own = meta_ref[0]
    window(kv_ref, own % 2, own, ids_ref, qt_ref, m_ref, l_ref, acc_ref)


def last_kernel(meta_ref, table_ref, mine_ref, kv_ref, ids_ref, qt_ref, m_in, l_in, acc_in,
                out_ref, m_ref, l_ref, acc_ref, prefix_ref):
    m_ref[...] = m_in[...]
    l_ref[...] = l_in[...]
    acc_ref[...] = acc_in[...]
    own = meta_ref[0]
    core, x = own % 2, own // (2 * NY)
    for i in range(PAGES):
        page = table_ref[i]
        start = (page // 2) % NY * SLOT + 2 * ROWS + (x + NX - page // (2 * NY)) % NX * PAGE
        rows = pl.ds(pl.multiple_of(start, PAGE), PAGE)

        @pl.when(page % 2 == core)
        def _():
            prefix_ref[i * PAGE:(i + 1) * PAGE, :] = mine_ref[rows, :]

        @pl.when(page % 2 != core)
        def _():
            prefix_ref[i * PAGE:(i + 1) * PAGE, :] = kv_ref[rows, :]

    fold(prefix_ref[:, :D], prefix_ref[:, D:], None, qt_ref, m_ref, l_ref, acc_ref)
    window(kv_ref, 1 - core, own, ids_ref, qt_ref, m_ref, l_ref, acc_ref)
    result = (acc_ref[...] * (1.0 / l_ref[...])).astype(jnp.bfloat16)
    for g in range(GROUP):
        out_ref[:, g * D:(g + 1) * D] = result[:, g * ROWS:(g + 1) * ROWS].T


VM = pl.BlockSpec(memory_space=pltpu.VMEM)
SM = pl.BlockSpec(memory_space=pltpu.SMEM)


def cost(keys):
    return pl.CostEstimate(flops=4 * D * QR * keys, bytes_accessed=1 << 20, transcendentals=QR * keys)


def per_device(queries, branch_key_value, branch_ids, pool, page_table):
    me = lax.axis_index("seq")
    y = (me // 2) % NY
    z = lax.axis_index("head")
    gathered = lax.all_gather(jnp.transpose(queries, (1, 0, 2)), "head", axis=0, tiled=False)
    query = lax.dynamic_index_in_dim(gathered, z, 1, keepdims=False).reshape(ROWS, GROUP * D)
    page = pool.reshape(1, PAGE, PAIR)
    raw = jnp.concatenate([jnp.transpose(branch_key_value, (1, 0, 2)), page], axis=0)
    two_raw = lax.ppermute(raw, "seq", x_ring(2))
    one_raw = lax.ppermute(raw, "seq", x_ring(1))
    three_page = lax.ppermute(page, "seq", x_ring(3))
    pages = jnp.concatenate([page, one_raw[8:], two_raw[8:], three_page], axis=0).reshape(NX * PAGE, PAIR)
    wide = jnp.concatenate([raw[:8], one_raw[:8], two_raw[:8]], axis=2)
    wide = lax.all_to_all(wide, "head", split_axis=0, concat_axis=0, tiled=True).reshape(ROWS, 3 * PAIR)
    own, one_back, two_back = (wide[:, i * PAIR:(i + 1) * PAIR] for i in range(3))
    target = jnp.arange(NY, dtype=jnp.int32)[:, None, None]
    mixed = jnp.where(target > y, own[None], two_back[None])
    send = jnp.concatenate([
        jnp.broadcast_to(one_back[None], mixed.shape), mixed,
        jnp.broadcast_to(pages[None], (NY, NX * PAGE, PAIR)),
    ], axis=1)
    kv = lax.all_to_all(send, "seq", split_axis=0, concat_axis=0, tiled=True, axis_index_groups=Y_GROUPS)
    kv = kv.reshape(NY * SLOT, PAIR)
    later, _ = lax.optimization_barrier((own, send))
    side = lax.ppermute(later, "seq", SWAP)

    ids = branch_ids.reshape(2 * NX * NY, ROWS)
    meta = me.astype(jnp.int32).reshape(1)
    state = [
        jax.ShapeDtypeStruct((1, QR), jnp.float32),
        jax.ShapeDtypeStruct((1, QR), jnp.float32),
        jax.ShapeDtypeStruct((D, QR), jnp.float32),
    ]
    params = pltpu.CompilerParams(vmem_limit_bytes=40 * 1024 * 1024)
    qt, m, l, acc = pl.pallas_call(
        near_kernel,
        out_shape=[jax.ShapeDtypeStruct((PAIR, QR), jnp.bfloat16)] + state,
        in_specs=[SM] + [VM] * 4,
        out_specs=[VM] * 4,
        compiler_params=params,
        cost_estimate=cost(256),
        name="near_keys",
    )(meta, own, side, ids, query)
    kv, m = lax.optimization_barrier((kv, m))
    kv_side = lax.ppermute(kv, "seq", SWAP)
    m, l, acc = pl.pallas_call(
        own_kernel,
        out_shape=state,
        in_specs=[SM] + [VM] * 6,
        out_specs=[VM] * 3,
        compiler_params=params,
        cost_estimate=cost(2048),
        name="own_parity",
    )(meta, kv, ids, qt, m, l, acc)
    out = pl.pallas_call(
        last_kernel,
        out_shape=jax.ShapeDtypeStruct((ROWS, GROUP * D), jnp.bfloat16),
        in_specs=[SM, SM] + [VM] * 7,
        out_specs=VM,
        scratch_shapes=[
            pltpu.VMEM((1, QR), jnp.float32),
            pltpu.VMEM((1, QR), jnp.float32),
            pltpu.VMEM((D, QR), jnp.float32),
            pltpu.VMEM((PAGES * PAGE, PAIR), jnp.bfloat16),
        ],
        compiler_params=params,
        cost_estimate=cost(2560),
        name="other_parity",
    )(meta, page_table.reshape(PAGES), kv, kv_side, ids, qt, m, l, acc)
    out = lax.all_to_all(out.reshape(8, ROWS // 8, GROUP * D), "head", split_axis=0, concat_axis=0, tiled=True)
    return jnp.transpose(out, (1, 0, 2))


def solution(mesh):
    return jax.shard_map(
        per_device,
        mesh=mesh,
        in_specs=(
            P(("seq", "head"), None, None),
            P(("seq", "head"), None, None),
            P(),
            P("seq", None, "head", None),
            P("head", None),
        ),
        out_specs=P(("seq", "head"), None, None),
        check_vma=False,
    )
```

```python
import jax
import jax.numpy as jnp
from jax import lax
from jax.experimental import pallas as pl
from jax.experimental.pallas import tpu as pltpu
from jax.sharding import PartitionSpec as P

D = 128
PAIR = 2 * D
ROWS = 128
GROUP = 8
QR = ROWS * GROUP
NX, NY = 4, 8
PAGES = 32
PAGE = 16
BLOCKS = 4
TILE = 512
SCALE2 = D ** (-0.5) * 1.4426950408889634
LOW = -1e30
SLOT = ROWS + PAGE
NEAR = 8


def x_ring(by):
    return [
        ((x * NY + y) * 2 + c, (((x + by) % NX) * NY + y) * 2 + c)
        for x in range(NX) for y in range(NY) for c in range(2)
    ]


SWAP = [(i, i ^ 1) for i in range(2 * NX * NY)]
Y_GROUPS = [[(x * NY + y) * 2 + c for y in range(NY)] for x in range(NX) for c in range(2)]


def fold(keys, values, mask, qt_ref, m_ref, l_ref, acc_ref):
    twice = jnp.concatenate([keys, keys], axis=1)
    lifted = jnp.concatenate([values.T, jnp.ones((16, keys.shape[0]), jnp.bfloat16)], axis=0)

    def scores_of(at):
        scores = jnp.dot(twice, qt_ref[:, at:at + TILE], preferred_element_type=jnp.float32)
        if mask is not None:
            scores = jnp.where(jnp.concatenate([mask] * (TILE // ROWS), axis=1), scores, LOW)
        return scores

    coming = scores_of(0)
    for at in range(0, QR, TILE):
        cols = slice(at, at + TILE)
        scores = coming
        if at + TILE < QR:
            coming = scores_of(at + TILE)
        old = m_ref[:, cols]
        top = jnp.maximum(old, jnp.max(scores, axis=0, keepdims=True))
        weights = jnp.exp2(scores - top).astype(jnp.bfloat16)
        factor = jnp.exp2(old - top)
        m_ref[:, cols] = top
        mixed = jnp.dot(lifted, weights, preferred_element_type=jnp.float32)
        l_ref[:, cols] = l_ref[:, cols] * factor + mixed[D:D + 1]
        acc_ref[:, cols] = acc_ref[:, cols] * factor + mixed[:D]


def starts_of(ids_ref, own):
    ids = ids_ref[...]
    starts = [jnp.sum((ids < b).astype(jnp.int32)) for b in range(1, 4)]
    own_ids = ids_ref[pl.ds(own, 1), :]
    row_start = jnp.zeros_like(own_ids)
    for b in range(1, 4):
        row_start = jnp.where(own_ids == b, starts[b - 1], row_start)
    return row_start, jnp.min(row_start), jnp.max(row_start)


def mask_of(block, own, row_start):
    key_rows = lax.broadcasted_iota(jnp.int32, (ROWS, ROWS), 0) + block * ROWS
    query_rows = lax.broadcasted_iota(jnp.int32, (ROWS, ROWS), 1) + own * ROWS
    return (key_rows >= row_start) & (key_rows <= query_rows)


def own_kernel(meta_ref, mine_ref, side_ref, ids_ref, q_ref, qt_ref, m_ref, l_ref, acc_ref):
    own = meta_ref[0]
    row_start, first, last = starts_of(ids_ref, own)
    for g in range(GROUP):
        scaled = q_ref[:, g * D:(g + 1) * D].astype(jnp.float32) * SCALE2
        high = scaled.astype(jnp.bfloat16)
        low = (scaled - high.astype(jnp.float32)).astype(jnp.bfloat16)
        qt_ref[:D, g * ROWS:(g + 1) * ROWS] = high.T
        qt_ref[D:, g * ROWS:(g + 1) * ROWS] = low.T
    m_ref[...] = jnp.full_like(m_ref, LOW)
    l_ref[...] = jnp.zeros_like(l_ref)
    acc_ref[...] = jnp.zeros_like(acc_ref)
    state = (qt_ref, m_ref, l_ref, acc_ref)
    fold(mine_ref[:, :D], mine_ref[:, D:], mask_of(own, own, row_start), *state)

    @pl.when((own % 2 == 1) & (own * ROWS > first))
    def _():
        fold(side_ref[:, :D], side_ref[:, D:], mask_of(own - 1, own, row_start), *state)


def window(kv_ref, skip, core, own, limits, qt_ref, m_ref, l_ref, acc_ref):
    row_start, first, last = limits
    chip = own // 2 - skip
    lowest = jnp.maximum((jnp.maximum(first // ROWS - core, -1) + 1) // 2, chip - NEAR)
    steps = jnp.maximum(chip - lowest + BLOCKS - 1, 0) // BLOCKS

    def step(i, carry):
        base = chip - BLOCKS * (i + 1)
        pairs = []
        for b in range(BLOCKS):
            start = (base + b + 4 * NY) % NY * SLOT
            pairs.append(kv_ref[pl.ds(pl.multiple_of(start, PAGE), ROWS), :])
        keys = jnp.concatenate([pair[:, :D] for pair in pairs], axis=0)
        values = jnp.concatenate([pair[:, D:] for pair in pairs], axis=0)
        whole = (2 * base + core) * ROWS >= last

        @pl.when(whole)
        def _():
            fold(keys, values, None, qt_ref, m_ref, l_ref, acc_ref)

        @pl.when(jnp.logical_not(whole))
        def _():
            mask = jnp.concatenate(
                [mask_of(2 * (base + b) + core, own, row_start) for b in range(BLOCKS)], axis=0
            )
            fold(keys, values, mask, qt_ref, m_ref, l_ref, acc_ref)

        return carry

    lax.fori_loop(0, steps, step, 0)


def near_kernel(meta_ref, kv_ref, side_ref, ids_ref, qt_ref, m_in, l_in, acc_in, m_ref, l_ref, acc_ref):
    m_ref[...] = m_in[...]
    l_ref[...] = l_in[...]
    acc_ref[...] = acc_in[...]
    own = meta_ref[0]
    limits = starts_of(ids_ref, own)
    window(kv_ref, 0, own % 2, own, limits, qt_ref, m_ref, l_ref, acc_ref)
    window(side_ref, 0, 1 - own % 2, own, limits, qt_ref, m_ref, l_ref, acc_ref)


def far_kernel(meta_ref, kv_ref, ids_ref, qt_ref, m_in, l_in, acc_in, m_ref, l_ref, acc_ref):
    m_ref[...] = m_in[...]
    l_ref[...] = l_in[...]
    acc_ref[...] = acc_in[...]
    own = meta_ref[0]
    window(kv_ref, NEAR, own % 2, own, starts_of(ids_ref, own), qt_ref, m_ref, l_ref, acc_ref)


def last_kernel(meta_ref, table_ref, near_ref, near_side_ref, far_ref, far_side_ref, two_ref, three_ref, ids_ref,
                qt_ref, m_in, l_in, acc_in, out_ref, m_ref, l_ref, acc_ref, prefix_ref):
    m_ref[...] = m_in[...]
    l_ref[...] = l_in[...]
    acc_ref[...] = acc_in[...]
    own = meta_ref[0]
    core, x = own % 2, own // (2 * NY)
    for i in range(PAGES):
        page = table_ref[i]
        yy = (page // 2) % NY
        back = (x + NX - page // (2 * NY)) % NX
        side = jnp.where(page % 2 == core, 0, 1)
        in_slot = pl.ds(pl.multiple_of(yy * SLOT + ROWS, PAGE), PAGE)
        in_page = pl.ds(pl.multiple_of((side * NY + yy) * PAGE, PAGE), PAGE)
        into = slice(i * PAGE, (i + 1) * PAGE)
        places = [
            (near_ref, in_slot), (near_side_ref, in_slot), (far_ref, in_slot), (far_side_ref, in_slot),
            (two_ref, in_page), (three_ref, in_page),
        ]
        for n, (ref, rows) in enumerate(places):

            @pl.when(jnp.where(back < 2, 2 * back + side, back + 2) == n)
            def _():
                prefix_ref[into, :] = ref[rows, :]

    fold(prefix_ref[:, :D], prefix_ref[:, D:], None, qt_ref, m_ref, l_ref, acc_ref)
    window(far_side_ref, NEAR, 1 - core, own, starts_of(ids_ref, own), qt_ref, m_ref, l_ref, acc_ref)
    result = (acc_ref[...] * (1.0 / l_ref[...])).astype(jnp.bfloat16)
    for g in range(GROUP):
        out_ref[:, g * D:(g + 1) * D] = result[:, g * ROWS:(g + 1) * ROWS].T


VM = pl.BlockSpec(memory_space=pltpu.VMEM)
SM = pl.BlockSpec(memory_space=pltpu.SMEM)


def cost(keys):
    return pl.CostEstimate(flops=4 * D * QR * keys, bytes_accessed=1 << 20, transcendentals=QR * keys)


def per_device(queries, branch_key_value, branch_ids, pool, page_table):
    me = lax.axis_index("seq")
    y = (me // 2) % NY
    page = pool.reshape(PAGE, PAIR)
    raw = jnp.transpose(branch_key_value, (1, 0, 2))
    one_raw = lax.ppermute(raw, "seq", x_ring(1))
    wide = jnp.concatenate([jnp.transpose(queries, (1, 0, 2)), raw, one_raw], axis=2)
    wide = lax.all_to_all(wide, "head", split_axis=0, concat_axis=0, tiled=True).reshape(ROWS, -1)
    own, before = wide[:, GROUP * D:GROUP * D + PAIR], wide[:, GROUP * D + PAIR:]
    target = jnp.arange(NY, dtype=jnp.int32)[:, None, None]
    block = jnp.where(target > y, own[None], before[None])
    send = jnp.concatenate([block, jnp.broadcast_to(page[None], (NY, PAGE, PAIR))], axis=1)
    near = lax.all_to_all(send, "seq", split_axis=0, concat_axis=0, tiled=True, axis_index_groups=Y_GROUPS)
    far = lax.ppermute(near, "seq", x_ring(1))
    later, _ = lax.optimization_barrier((own, send))
    side = lax.ppermute(later, "seq", SWAP)
    near_side = lax.ppermute(near, "seq", SWAP)
    far_side = lax.ppermute(far, "seq", SWAP)
    pages = jnp.concatenate([near[:, ROWS:], near_side[:, ROWS:]], axis=0).reshape(2 * NY * PAGE, PAIR)
    two_pages = lax.ppermute(pages, "seq", x_ring(2))
    three_pages = lax.ppermute(pages, "seq", x_ring(3))
    near, near_side, far, far_side = (a.reshape(NY * SLOT, PAIR) for a in (near, near_side, far, far_side))

    ids = branch_ids.reshape(2 * NX * NY, ROWS)
    meta = me.astype(jnp.int32).reshape(1)
    state = [
        jax.ShapeDtypeStruct((1, QR), jnp.float32),
        jax.ShapeDtypeStruct((1, QR), jnp.float32),
        jax.ShapeDtypeStruct((D, QR), jnp.float32),
    ]
    params = pltpu.CompilerParams(vmem_limit_bytes=40 * 1024 * 1024)
    qt, *now = pl.pallas_call(
        own_kernel,
        out_shape=[jax.ShapeDtypeStruct((PAIR, QR), jnp.bfloat16)] + state,
        in_specs=[SM] + [VM] * 4,
        out_specs=[VM] * 4,
        compiler_params=params,
        cost_estimate=cost(256),
        name="own_chip",
    )(meta, own, side, ids, wide)
    now = pl.pallas_call(
        near_kernel,
        out_shape=state,
        in_specs=[SM] + [VM] * 7,
        out_specs=[VM] * 3,
        compiler_params=params,
        cost_estimate=cost(2048),
        name="near_window",
    )(meta, near, near_side, ids, qt, *now)
    now = pl.pallas_call(
        far_kernel,
        out_shape=state,
        in_specs=[SM] + [VM] * 6,
        out_specs=[VM] * 3,
        compiler_params=params,
        cost_estimate=cost(1024),
        name="far_window",
    )(meta, far, ids, qt, *now)
    out = pl.pallas_call(
        last_kernel,
        out_shape=jax.ShapeDtypeStruct((ROWS, GROUP * D), jnp.bfloat16),
        in_specs=[SM, SM] + [VM] * 11,
        out_specs=VM,
        scratch_shapes=[
            pltpu.VMEM((1, QR), jnp.float32),
            pltpu.VMEM((1, QR), jnp.float32),
            pltpu.VMEM((D, QR), jnp.float32),
            pltpu.VMEM((PAGES * PAGE, PAIR), jnp.bfloat16),
        ],
        compiler_params=params,
        cost_estimate=cost(1536),
        name="far_other_core_and_prefix",
    )(meta, page_table.reshape(PAGES), near, near_side, far, far_side, two_pages, three_pages, ids, qt, *now)
    out = lax.all_to_all(out.reshape(8, ROWS // 8, GROUP * D), "head", split_axis=0, concat_axis=0, tiled=True)
    return jnp.transpose(out, (1, 0, 2))


def solution(mesh):
    return jax.shard_map(
        per_device,
        mesh=mesh,
        in_specs=(
            P(("seq", "head"), None, None),
            P(("seq", "head"), None, None),
            P(),
            P("seq", None, "head", None),
            P("head", None),
        ),
        out_specs=P(("seq", "head"), None, None),
        check_vma=False,
    )
```

```python
import jax
import jax.numpy as jnp
from jax import lax
from jax.experimental import pallas as pl
from jax.experimental.pallas import tpu as pltpu
from jax.sharding import PartitionSpec as P

D = 128
PAIR = 2 * D
ROWS = 128
GROUP = 8
QR = ROWS * GROUP
NX, NY = 4, 8
PAGES = 32
PAGE = 16
BLOCKS = 4
TILE = 512
SCALE2 = D ** (-0.5) * 1.4426950408889634
LOW = -1e30
SLOT = ROWS + NX * PAGE
NEAR = 8


def x_ring(by):
    return [
        ((x * NY + y) * 2 + c, (((x + by) % NX) * NY + y) * 2 + c)
        for x in range(NX) for y in range(NY) for c in range(2)
    ]


SWAP = [(i, i ^ 1) for i in range(2 * NX * NY)]
Y_GROUPS = [[(x * NY + y) * 2 + c for y in range(NY)] for x in range(NX) for c in range(2)]


def fold(keys, values, mask, qt_ref, m_ref, l_ref, acc_ref):
    twice = jnp.concatenate([keys, keys], axis=1)
    lifted = jnp.concatenate([values.T, jnp.ones((16, keys.shape[0]), jnp.bfloat16)], axis=0)

    def scores_of(at):
        scores = jnp.dot(twice, qt_ref[:, at:at + TILE], preferred_element_type=jnp.float32)
        if mask is not None:
            scores = jnp.where(jnp.concatenate([mask] * (TILE // ROWS), axis=1), scores, LOW)
        return scores

    coming = scores_of(0)
    for at in range(0, QR, TILE):
        cols = slice(at, at + TILE)
        scores = coming
        if at + TILE < QR:
            coming = scores_of(at + TILE)
        old = m_ref[:, cols]
        top = jnp.maximum(old, jnp.max(scores, axis=0, keepdims=True))
        weights = jnp.exp2(scores - top).astype(jnp.bfloat16)
        factor = jnp.exp2(old - top)
        m_ref[:, cols] = top
        mixed = jnp.dot(lifted, weights, preferred_element_type=jnp.float32)
        l_ref[:, cols] = l_ref[:, cols] * factor + mixed[D:D + 1]
        acc_ref[:, cols] = acc_ref[:, cols] * factor + mixed[:D]


def starts_of(ids_ref, own):
    ids = ids_ref[...]
    starts = [jnp.sum((ids < b).astype(jnp.int32)) for b in range(1, 4)]
    own_ids = ids_ref[pl.ds(own, 1), :]
    row_start = jnp.zeros_like(own_ids)
    for b in range(1, 4):
        row_start = jnp.where(own_ids == b, starts[b - 1], row_start)
    return row_start, jnp.min(row_start), jnp.max(row_start)


def mask_of(block, own, row_start):
    key_rows = lax.broadcasted_iota(jnp.int32, (ROWS, ROWS), 0) + block * ROWS
    query_rows = lax.broadcasted_iota(jnp.int32, (ROWS, ROWS), 1) + own * ROWS
    return (key_rows >= row_start) & (key_rows <= query_rows)


def own_kernel(meta_ref, mine_ref, side_ref, ids_ref, q_ref, qt_ref, m_ref, l_ref, acc_ref):
    own = meta_ref[0]
    row_start, first, last = starts_of(ids_ref, own)
    for g in range(GROUP):
        scaled = q_ref[:, g * D:(g + 1) * D].astype(jnp.float32) * SCALE2
        high = scaled.astype(jnp.bfloat16)
        low = (scaled - high.astype(jnp.float32)).astype(jnp.bfloat16)
        qt_ref[:D, g * ROWS:(g + 1) * ROWS] = high.T
        qt_ref[D:, g * ROWS:(g + 1) * ROWS] = low.T
    m_ref[...] = jnp.full_like(m_ref, LOW)
    l_ref[...] = jnp.zeros_like(l_ref)
    acc_ref[...] = jnp.zeros_like(acc_ref)
    state = (qt_ref, m_ref, l_ref, acc_ref)
    fold(mine_ref[:, :D], mine_ref[:, D:], mask_of(own, own, row_start), *state)

    @pl.when((own % 2 == 1) & (own * ROWS > first))
    def _():
        fold(side_ref[:, :D], side_ref[:, D:], mask_of(own - 1, own, row_start), *state)


def window(kv_ref, skip, slot, core, own, limits, qt_ref, m_ref, l_ref, acc_ref):
    row_start, first, last = limits
    chip = own // 2 - skip
    lowest = jnp.maximum((jnp.maximum(first // ROWS - core, -1) + 1) // 2, chip - NEAR)
    steps = jnp.maximum(chip - lowest + BLOCKS - 1, 0) // BLOCKS

    def step(i, carry):
        base = chip - BLOCKS * (i + 1)
        pairs = []
        for b in range(BLOCKS):
            start = (base + b + 4 * NY) % NY * slot
            pairs.append(kv_ref[pl.ds(pl.multiple_of(start, PAGE), ROWS), :])
        keys = jnp.concatenate([pair[:, :D] for pair in pairs], axis=0)
        values = jnp.concatenate([pair[:, D:] for pair in pairs], axis=0)
        whole = (2 * base + core) * ROWS >= last

        @pl.when(whole)
        def _():
            fold(keys, values, None, qt_ref, m_ref, l_ref, acc_ref)

        @pl.when(jnp.logical_not(whole))
        def _():
            mask = jnp.concatenate(
                [mask_of(2 * (base + b) + core, own, row_start) for b in range(BLOCKS)], axis=0
            )
            fold(keys, values, mask, qt_ref, m_ref, l_ref, acc_ref)

        return carry

    lax.fori_loop(0, steps, step, 0)


def near_kernel(meta_ref, table_ref, kv_ref, side_ref, ids_ref, qt_ref, m_in, l_in, acc_in,
                m_ref, l_ref, acc_ref, prefix_ref):
    m_ref[...] = m_in[...]
    l_ref[...] = l_in[...]
    acc_ref[...] = acc_in[...]
    own = meta_ref[0]
    core, x = own % 2, own // (2 * NY)
    for i in range(PAGES):
        page = table_ref[i]
        start = (page // 2) % NY * SLOT + ROWS + (x + NX - page // (2 * NY)) % NX * PAGE
        rows = pl.ds(pl.multiple_of(start, PAGE), PAGE)

        @pl.when(page % 2 == core)
        def _():
            prefix_ref[i * PAGE:(i + 1) * PAGE, :] = kv_ref[rows, :]

        @pl.when(page % 2 != core)
        def _():
            prefix_ref[i * PAGE:(i + 1) * PAGE, :] = side_ref[rows, :]

    fold(prefix_ref[:, :D], prefix_ref[:, D:], None, qt_ref, m_ref, l_ref, acc_ref)
    limits = starts_of(ids_ref, own)
    window(kv_ref, 0, SLOT, core, own, limits, qt_ref, m_ref, l_ref, acc_ref)
    window(side_ref, 0, SLOT, 1 - core, own, limits, qt_ref, m_ref, l_ref, acc_ref)


def far_kernel(meta_ref, kv_ref, ids_ref, qt_ref, m_in, l_in, acc_in, m_ref, l_ref, acc_ref):
    m_ref[...] = m_in[...]
    l_ref[...] = l_in[...]
    acc_ref[...] = acc_in[...]
    own = meta_ref[0]
    window(kv_ref, NEAR, ROWS, own % 2, own, starts_of(ids_ref, own), qt_ref, m_ref, l_ref, acc_ref)


def last_kernel(meta_ref, kv_ref, ids_ref, qt_ref, m_in, l_in, acc_in, out_ref, m_ref, l_ref, acc_ref):
    m_ref[...] = m_in[...]
    l_ref[...] = l_in[...]
    acc_ref[...] = acc_in[...]
    own = meta_ref[0]
    window(kv_ref, NEAR, ROWS, 1 - own % 2, own, starts_of(ids_ref, own), qt_ref, m_ref, l_ref, acc_ref)
    result = (acc_ref[...] * (1.0 / l_ref[...])).astype(jnp.bfloat16)
    for g in range(GROUP):
        out_ref[:, g * D:(g + 1) * D] = result[:, g * ROWS:(g + 1) * ROWS].T


VM = pl.BlockSpec(memory_space=pltpu.VMEM)
SM = pl.BlockSpec(memory_space=pltpu.SMEM)


def cost(keys):
    return pl.CostEstimate(flops=4 * D * QR * keys, bytes_accessed=1 << 20, transcendentals=QR * keys)


def per_device(queries, branch_key_value, branch_ids, pool, page_table):
    me = lax.axis_index("seq")
    y = (me // 2) % NY
    page = pool.reshape(1, PAGE, PAIR)
    raw = jnp.concatenate([jnp.transpose(branch_key_value, (1, 0, 2)), page], axis=0)
    one_raw = lax.ppermute(raw, "seq", x_ring(1))
    wide = jnp.concatenate([jnp.transpose(queries, (1, 0, 2)), raw[:8], one_raw[:8]], axis=2)
    wide = lax.all_to_all(wide, "head", split_axis=0, concat_axis=0, tiled=True).reshape(ROWS, -1)
    own, before = wide[:, GROUP * D:GROUP * D + PAIR], wide[:, GROUP * D + PAIR:]
    two_page = lax.ppermute(page, "seq", x_ring(2))
    three_page = lax.ppermute(page, "seq", x_ring(3))
    target = jnp.arange(NY, dtype=jnp.int32)[:, None, None]
    block = jnp.where(target > y, own[None], before[None])
    pages = jnp.concatenate([page, one_raw[8:], two_page, three_page], axis=0).reshape(1, NX * PAGE, PAIR)
    send = jnp.concatenate([block, jnp.broadcast_to(pages, (NY, NX * PAGE, PAIR))], axis=1)
    near = lax.all_to_all(send, "seq", split_axis=0, concat_axis=0, tiled=True, axis_index_groups=Y_GROUPS)
    later, _ = lax.optimization_barrier((own, send))
    side = lax.ppermute(later, "seq", SWAP)

    ids = branch_ids.reshape(2 * NX * NY, ROWS)
    meta = me.astype(jnp.int32).reshape(1)
    state = [
        jax.ShapeDtypeStruct((1, QR), jnp.float32),
        jax.ShapeDtypeStruct((1, QR), jnp.float32),
        jax.ShapeDtypeStruct((D, QR), jnp.float32),
    ]
    params = pltpu.CompilerParams(vmem_limit_bytes=40 * 1024 * 1024)
    qt, *now = pl.pallas_call(
        own_kernel,
        out_shape=[jax.ShapeDtypeStruct((PAIR, QR), jnp.bfloat16)] + state,
        in_specs=[SM] + [VM] * 4,
        out_specs=[VM] * 4,
        compiler_params=params,
        cost_estimate=cost(256),
        name="own_chip",
    )(meta, own, side, ids, wide)
    near, now = lax.optimization_barrier((near, now))
    far = lax.ppermute(near[:, :ROWS], "seq", x_ring(1))
    near = near.reshape(NY * SLOT, PAIR)
    near_side = lax.ppermute(near, "seq", SWAP)
    now = pl.pallas_call(
        near_kernel,
        out_shape=state,
        in_specs=[SM, SM] + [VM] * 7,
        out_specs=[VM] * 3,
        scratch_shapes=[pltpu.VMEM((PAGES * PAGE, PAIR), jnp.bfloat16)],
        compiler_params=params,
        cost_estimate=cost(2560),
        name="near_window_and_prefix",
    )(meta, page_table.reshape(PAGES), near, near_side, ids, qt, *now)
    far, now = lax.optimization_barrier((far, now))
    far = far.reshape(NY * ROWS, PAIR)
    far_side = lax.ppermute(far, "seq", SWAP)
    now = pl.pallas_call(
        far_kernel,
        out_shape=state,
        in_specs=[SM] + [VM] * 6,
        out_specs=[VM] * 3,
        compiler_params=params,
        cost_estimate=cost(1024),
        name="far_window",
    )(meta, far, ids, qt, *now)
    out = pl.pallas_call(
        last_kernel,
        out_shape=jax.ShapeDtypeStruct((ROWS, GROUP * D), jnp.bfloat16),
        in_specs=[SM] + [VM] * 6,
        out_specs=VM,
        scratch_shapes=[
            pltpu.VMEM((1, QR), jnp.float32),
            pltpu.VMEM((1, QR), jnp.float32),
            pltpu.VMEM((D, QR), jnp.float32),
        ],
        compiler_params=params,
        cost_estimate=cost(1024),
        name="far_other_core",
    )(meta, far_side, ids, qt, *now)
    out = lax.all_to_all(out.reshape(8, ROWS // 8, GROUP * D), "head", split_axis=0, concat_axis=0, tiled=True)
    return jnp.transpose(out, (1, 0, 2))


def solution(mesh):
    return jax.shard_map(
        per_device,
        mesh=mesh,
        in_specs=(
            P(("seq", "head"), None, None),
            P(("seq", "head"), None, None),
            P(),
            P("seq", None, "head", None),
            P("head", None),
        ),
        out_specs=P(("seq", "head"), None, None),
        check_vma=False,
    )
```

```python
import jax
import jax.numpy as jnp
from jax import lax
from jax.experimental import pallas as pl
from jax.experimental.pallas import tpu as pltpu
from jax.sharding import PartitionSpec as P

D = 128
PAIR = 2 * D
ROWS = 128
GROUP = 8
QR = ROWS * GROUP
NX, NY = 4, 8
PAGES = 32
PAGE = 16
BLOCKS = 4
TILE = 512
SCALE2 = D ** (-0.5) * 1.4426950408889634
LOW = -1e30
SLOT = 2 * ROWS + NX * PAGE


def x_ring(by):
    return [
        ((x * NY + y) * 2 + c, (((x + by) % NX) * NY + y) * 2 + c)
        for x in range(NX) for y in range(NY) for c in range(2)
    ]


SWAP = [(i, i ^ 1) for i in range(2 * NX * NY)]
Y_GROUPS = [[(x * NY + y) * 2 + c for y in range(NY)] for x in range(NX) for c in range(2)]


def fold(keys, values, mask, qt_ref, m_ref, l_ref, acc_ref):
    twice = jnp.concatenate([keys, keys], axis=1)
    lifted = jnp.concatenate([values.T, jnp.ones((16, keys.shape[0]), jnp.bfloat16)], axis=0)

    def scores_of(at):
        scores = jnp.dot(twice, qt_ref[:, at:at + TILE], preferred_element_type=jnp.float32)
        if mask is not None:
            scores = jnp.where(jnp.concatenate([mask] * (TILE // ROWS), axis=1), scores, LOW)
        return scores

    coming = scores_of(0)
    for at in range(0, QR, TILE):
        cols = slice(at, at + TILE)
        scores = coming
        if at + TILE < QR:
            coming = scores_of(at + TILE)
        old = m_ref[:, cols]
        top = jnp.maximum(old, jnp.max(scores, axis=0, keepdims=True))
        weights = jnp.exp2(scores - top).astype(jnp.bfloat16)
        factor = jnp.exp2(old - top)
        m_ref[:, cols] = top
        mixed = jnp.dot(lifted, weights, preferred_element_type=jnp.float32)
        l_ref[:, cols] = l_ref[:, cols] * factor + mixed[D:D + 1]
        acc_ref[:, cols] = acc_ref[:, cols] * factor + mixed[:D]


def starts_of(ids_ref, own):
    ids = ids_ref[...]
    starts = [jnp.sum((ids < b).astype(jnp.int32)) for b in range(1, 4)]
    own_ids = ids_ref[pl.ds(own, 1), :]
    row_start = jnp.zeros_like(own_ids)
    for b in range(1, 4):
        row_start = jnp.where(own_ids == b, starts[b - 1], row_start)
    return row_start, jnp.min(row_start), jnp.max(row_start)


def mask_of(block, own, row_start):
    key_rows = lax.broadcasted_iota(jnp.int32, (ROWS, ROWS), 0) + block * ROWS
    query_rows = lax.broadcasted_iota(jnp.int32, (ROWS, ROWS), 1) + own * ROWS
    return (key_rows >= row_start) & (key_rows <= query_rows)


def near_kernel(meta_ref, mine_ref, side_ref, ids_ref, q_ref, qt_ref, m_ref, l_ref, acc_ref):
    own = meta_ref[0]
    row_start, first, last = starts_of(ids_ref, own)
    for g in range(GROUP):
        scaled = q_ref[:, g * D:(g + 1) * D].astype(jnp.float32) * SCALE2
        high = scaled.astype(jnp.bfloat16)
        low = (scaled - high.astype(jnp.float32)).astype(jnp.bfloat16)
        qt_ref[:D, g * ROWS:(g + 1) * ROWS] = high.T
        qt_ref[D:, g * ROWS:(g + 1) * ROWS] = low.T
    m_ref[...] = jnp.full_like(m_ref, LOW)
    l_ref[...] = jnp.zeros_like(l_ref)
    acc_ref[...] = jnp.zeros_like(acc_ref)
    state = (qt_ref, m_ref, l_ref, acc_ref)
    fold(mine_ref[:, :D], mine_ref[:, D:], mask_of(own, own, row_start), *state)

    @pl.when((own % 2 == 1) & (own * ROWS > first))
    def _():
        fold(side_ref[:, :D], side_ref[:, D:], mask_of(own - 1, own, row_start), *state)


def window(kv_ref, core, own, ids_ref, qt_ref, m_ref, l_ref, acc_ref):
    row_start, first, last = starts_of(ids_ref, own)
    chip = own // 2
    x = chip // NY
    lowest = (jnp.maximum(first // ROWS - core, -1) + 1) // 2
    steps = jnp.maximum(chip - lowest + BLOCKS - 1, 0) // BLOCKS

    def step(i, carry):
        base = chip - BLOCKS * (i + 1)
        pairs = []
        for b in range(BLOCKS):
            at = jnp.maximum(base + b, 0)
            start = (at % NY) * SLOT + jnp.where(at // NY == x - 1, 0, ROWS)
            pairs.append(kv_ref[pl.ds(pl.multiple_of(start, PAGE), ROWS), :])
        keys = jnp.concatenate([pair[:, :D] for pair in pairs], axis=0)
        values = jnp.concatenate([pair[:, D:] for pair in pairs], axis=0)
        whole = (2 * base + core) * ROWS >= last

        @pl.when(whole)
        def _():
            fold(keys, values, None, qt_ref, m_ref, l_ref, acc_ref)

        @pl.when(jnp.logical_not(whole))
        def _():
            mask = jnp.concatenate(
                [mask_of(2 * (base + b) + core, own, row_start) for b in range(BLOCKS)], axis=0
            )
            fold(keys, values, mask, qt_ref, m_ref, l_ref, acc_ref)

        return carry

    lax.fori_loop(0, steps, step, 0)


def own_kernel(meta_ref, kv_ref, ids_ref, qt_ref, m_in, l_in, acc_in, m_ref, l_ref, acc_ref):
    m_ref[...] = m_in[...]
    l_ref[...] = l_in[...]
    acc_ref[...] = acc_in[...]
    own = meta_ref[0]
    window(kv_ref, own % 2, own, ids_ref, qt_ref, m_ref, l_ref, acc_ref)


def last_kernel(meta_ref, table_ref, mine_ref, kv_ref, ids_ref, qt_ref, m_in, l_in, acc_in,
                out_ref, m_ref, l_ref, acc_ref, prefix_ref):
    m_ref[...] = m_in[...]
    l_ref[...] = l_in[...]
    acc_ref[...] = acc_in[...]
    own = meta_ref[0]
    core, x = own % 2, own // (2 * NY)
    for i in range(PAGES):
        page = table_ref[i]
        start = (page // 2) % NY * SLOT + 2 * ROWS + (x + NX - page // (2 * NY)) % NX * PAGE
        rows = pl.ds(pl.multiple_of(start, PAGE), PAGE)

        @pl.when(page % 2 == core)
        def _():
            prefix_ref[i * PAGE:(i + 1) * PAGE, :] = mine_ref[rows, :]

        @pl.when(page % 2 != core)
        def _():
            prefix_ref[i * PAGE:(i + 1) * PAGE, :] = kv_ref[rows, :]

    fold(prefix_ref[:, :D], prefix_ref[:, D:], None, qt_ref, m_ref, l_ref, acc_ref)
    window(kv_ref, 1 - core, own, ids_ref, qt_ref, m_ref, l_ref, acc_ref)
    result = (acc_ref[...] * (1.0 / l_ref[...])).astype(jnp.bfloat16)
    for g in range(GROUP):
        out_ref[:, g * D:(g + 1) * D] = result[:, g * ROWS:(g + 1) * ROWS].T


VM = pl.BlockSpec(memory_space=pltpu.VMEM)
SM = pl.BlockSpec(memory_space=pltpu.SMEM)


def cost(keys):
    return pl.CostEstimate(flops=4 * D * QR * keys, bytes_accessed=1 << 20, transcendentals=QR * keys)


def per_device(queries, branch_key_value, branch_ids, pool, page_table):
    me = lax.axis_index("seq")
    y = (me // 2) % NY
    page = pool.reshape(1, PAGE, PAIR)
    raw = jnp.concatenate([jnp.transpose(branch_key_value, (1, 0, 2)), page], axis=0)
    two_raw = lax.ppermute(raw, "seq", x_ring(2))
    one_raw = lax.ppermute(raw, "seq", x_ring(1))
    three_page = lax.ppermute(page, "seq", x_ring(3))
    pages = jnp.concatenate([page, one_raw[8:], two_raw[8:], three_page], axis=0).reshape(NX * PAGE, PAIR)
    wide = jnp.concatenate([jnp.transpose(queries, (1, 0, 2)), raw[:8], one_raw[:8], two_raw[:8]], axis=2)
    wide = lax.all_to_all(wide, "head", split_axis=0, concat_axis=0, tiled=True).reshape(ROWS, -1)
    at = GROUP * D
    own, one_back, two_back = (wide[:, at + i * PAIR:at + (i + 1) * PAIR] for i in range(3))
    target = jnp.arange(NY, dtype=jnp.int32)[:, None, None]
    mixed = jnp.where(target > y, own[None], two_back[None])
    send = jnp.concatenate([
        jnp.broadcast_to(one_back[None], mixed.shape), mixed,
        jnp.broadcast_to(pages[None], (NY, NX * PAGE, PAIR)),
    ], axis=1)
    kv = lax.all_to_all(send, "seq", split_axis=0, concat_axis=0, tiled=True, axis_index_groups=Y_GROUPS)
    kv = kv.reshape(NY * SLOT, PAIR)
    later, _ = lax.optimization_barrier((own, send))
    side = lax.ppermute(later, "seq", SWAP)

    ids = branch_ids.reshape(2 * NX * NY, ROWS)
    meta = me.astype(jnp.int32).reshape(1)
    state = [
        jax.ShapeDtypeStruct((1, QR), jnp.float32),
        jax.ShapeDtypeStruct((1, QR), jnp.float32),
        jax.ShapeDtypeStruct((D, QR), jnp.float32),
    ]
    params = pltpu.CompilerParams(vmem_limit_bytes=40 * 1024 * 1024)
    qt, m, l, acc = pl.pallas_call(
        near_kernel,
        out_shape=[jax.ShapeDtypeStruct((PAIR, QR), jnp.bfloat16)] + state,
        in_specs=[SM] + [VM] * 4,
        out_specs=[VM] * 4,
        compiler_params=params,
        cost_estimate=cost(256),
        name="near_keys",
    )(meta, own, side, ids, wide)
    kv, m = lax.optimization_barrier((kv, m))
    kv_side = lax.ppermute(kv, "seq", SWAP)
    m, l, acc = pl.pallas_call(
        own_kernel,
        out_shape=state,
        in_specs=[SM] + [VM] * 6,
        out_specs=[VM] * 3,
        compiler_params=params,
        cost_estimate=cost(2048),
        name="own_parity",
    )(meta, kv, ids, qt, m, l, acc)
    out = pl.pallas_call(
        last_kernel,
        out_shape=jax.ShapeDtypeStruct((ROWS, GROUP * D), jnp.bfloat16),
        in_specs=[SM, SM] + [VM] * 7,
        out_specs=VM,
        scratch_shapes=[
            pltpu.VMEM((1, QR), jnp.float32),
            pltpu.VMEM((1, QR), jnp.float32),
            pltpu.VMEM((D, QR), jnp.float32),
            pltpu.VMEM((PAGES * PAGE, PAIR), jnp.bfloat16),
        ],
        compiler_params=params,
        cost_estimate=cost(2560),
        name="other_parity",
    )(meta, page_table.reshape(PAGES), kv, kv_side, ids, qt, m, l, acc)
    out = lax.all_to_all(out.reshape(8, ROWS // 8, GROUP * D), "head", split_axis=0, concat_axis=0, tiled=True)
    return jnp.transpose(out, (1, 0, 2))


def solution(mesh):
    return jax.shard_map(
        per_device,
        mesh=mesh,
        in_specs=(
            P(("seq", "head"), None, None),
            P(("seq", "head"), None, None),
            P(),
            P("seq", None, "head", None),
            P("head", None),
        ),
        out_specs=P(("seq", "head"), None, None),
        check_vma=False,
    )
```

```python
import jax
import jax.numpy as jnp
from jax import lax
from jax.experimental import pallas as pl
from jax.experimental.pallas import tpu as pltpu
from jax.sharding import PartitionSpec as P

D = 128
PAIR = 2 * D
ROWS = 128
GROUP = 8
QR = ROWS * GROUP
NX, NY = 4, 8
PAGES = 32
PAGE = 16
BLOCKS = 4
TILE = 512
SCALE2 = D ** (-0.5) * 1.4426950408889634
LOW = -1e30
SLOT = ROWS + NX * PAGE
NEAR = 8


def x_ring(by):
    return [
        ((x * NY + y) * 2 + c, (((x + by) % NX) * NY + y) * 2 + c)
        for x in range(NX) for y in range(NY) for c in range(2)
    ]


SWAP = [(i, i ^ 1) for i in range(2 * NX * NY)]
Y_GROUPS = [[(x * NY + y) * 2 + c for y in range(NY)] for x in range(NX) for c in range(2)]


def fold(keys, values, mask, qt_ref, m_ref, l_ref, acc_ref):
    twice = jnp.concatenate([keys, keys], axis=1)
    lifted = jnp.concatenate([values.T, jnp.ones((16, keys.shape[0]), jnp.bfloat16)], axis=0)

    def scores_of(at):
        scores = jnp.dot(twice, qt_ref[:, at:at + TILE], preferred_element_type=jnp.float32)
        if mask is not None:
            scores = jnp.where(jnp.concatenate([mask] * (TILE // ROWS), axis=1), scores, LOW)
        return scores

    coming = scores_of(0)
    for at in range(0, QR, TILE):
        cols = slice(at, at + TILE)
        scores = coming
        if at + TILE < QR:
            coming = scores_of(at + TILE)
        old = m_ref[:, cols]
        top = jnp.maximum(old, jnp.max(scores, axis=0, keepdims=True))
        weights = jnp.exp2(scores - top).astype(jnp.bfloat16)
        factor = jnp.exp2(old - top)
        m_ref[:, cols] = top
        mixed = jnp.dot(lifted, weights, preferred_element_type=jnp.float32)
        l_ref[:, cols] = l_ref[:, cols] * factor + mixed[D:D + 1]
        acc_ref[:, cols] = acc_ref[:, cols] * factor + mixed[:D]


def starts_of(ids_ref, own):
    ids = ids_ref[...]
    starts = [jnp.sum((ids < b).astype(jnp.int32)) for b in range(1, 4)]
    own_ids = ids_ref[pl.ds(own, 1), :]
    row_start = jnp.zeros_like(own_ids)
    for b in range(1, 4):
        row_start = jnp.where(own_ids == b, starts[b - 1], row_start)
    return row_start, jnp.min(row_start), jnp.max(row_start)


def mask_of(block, own, row_start):
    key_rows = lax.broadcasted_iota(jnp.int32, (ROWS, ROWS), 0) + block * ROWS
    query_rows = lax.broadcasted_iota(jnp.int32, (ROWS, ROWS), 1) + own * ROWS
    return (key_rows >= row_start) & (key_rows <= query_rows)


def own_kernel(meta_ref, mine_ref, side_ref, ids_ref, q_ref, qt_ref, m_ref, l_ref, acc_ref):
    own = meta_ref[0]
    row_start, first, last = starts_of(ids_ref, own)
    for g in range(GROUP):
        scaled = q_ref[:, g * D:(g + 1) * D].astype(jnp.float32) * SCALE2
        high = scaled.astype(jnp.bfloat16)
        low = (scaled - high.astype(jnp.float32)).astype(jnp.bfloat16)
        qt_ref[:D, g * ROWS:(g + 1) * ROWS] = high.T
        qt_ref[D:, g * ROWS:(g + 1) * ROWS] = low.T
    m_ref[...] = jnp.full_like(m_ref, LOW)
    l_ref[...] = jnp.zeros_like(l_ref)
    acc_ref[...] = jnp.zeros_like(acc_ref)
    state = (qt_ref, m_ref, l_ref, acc_ref)
    fold(mine_ref[:, :D], mine_ref[:, D:], mask_of(own, own, row_start), *state)

    @pl.when((own % 2 == 1) & (own * ROWS > first))
    def _():
        fold(side_ref[:, :D], side_ref[:, D:], mask_of(own - 1, own, row_start), *state)


def window(kv_ref, skip, slot, core, own, limits, qt_ref, m_ref, l_ref, acc_ref):
    row_start, first, last = limits
    chip = own // 2 - skip
    lowest = jnp.maximum((jnp.maximum(first // ROWS - core, -1) + 1) // 2, chip - NEAR)
    steps = jnp.maximum(chip - lowest + BLOCKS - 1, 0) // BLOCKS

    def step(i, carry):
        base = chip - BLOCKS * (i + 1)
        pairs = []
        for b in range(BLOCKS):
            start = (base + b + 4 * NY) % NY * slot
            pairs.append(kv_ref[pl.ds(pl.multiple_of(start, PAGE), ROWS), :])
        keys = jnp.concatenate([pair[:, :D] for pair in pairs], axis=0)
        values = jnp.concatenate([pair[:, D:] for pair in pairs], axis=0)
        whole = (2 * base + core) * ROWS >= last

        @pl.when(whole)
        def _():
            fold(keys, values, None, qt_ref, m_ref, l_ref, acc_ref)

        @pl.when(jnp.logical_not(whole))
        def _():
            mask = jnp.concatenate(
                [mask_of(2 * (base + b) + core, own, row_start) for b in range(BLOCKS)], axis=0
            )
            fold(keys, values, mask, qt_ref, m_ref, l_ref, acc_ref)

        return carry

    lax.fori_loop(0, steps, step, 0)


def near_kernel(meta_ref, table_ref, kv_ref, side_ref, ids_ref, qt_ref, m_in, l_in, acc_in,
                m_ref, l_ref, acc_ref, prefix_ref):
    m_ref[...] = m_in[...]
    l_ref[...] = l_in[...]
    acc_ref[...] = acc_in[...]
    own = meta_ref[0]
    core, x = own % 2, own // (2 * NY)
    for i in range(PAGES):
        page = table_ref[i]
        start = (page // 2) % NY * SLOT + ROWS + (x + NX - page // (2 * NY)) % NX * PAGE
        rows = pl.ds(pl.multiple_of(start, PAGE), PAGE)

        @pl.when(page % 2 == core)
        def _():
            prefix_ref[i * PAGE:(i + 1) * PAGE, :] = kv_ref[rows, :]

        @pl.when(page % 2 != core)
        def _():
            prefix_ref[i * PAGE:(i + 1) * PAGE, :] = side_ref[rows, :]

    fold(prefix_ref[:, :D], prefix_ref[:, D:], None, qt_ref, m_ref, l_ref, acc_ref)
    limits = starts_of(ids_ref, own)
    window(kv_ref, 0, SLOT, core, own, limits, qt_ref, m_ref, l_ref, acc_ref)
    window(side_ref, 0, SLOT, 1 - core, own, limits, qt_ref, m_ref, l_ref, acc_ref)


def far_kernel(meta_ref, kv_ref, ids_ref, qt_ref, m_in, l_in, acc_in, m_ref, l_ref, acc_ref):
    m_ref[...] = m_in[...]
    l_ref[...] = l_in[...]
    acc_ref[...] = acc_in[...]
    own = meta_ref[0]
    window(kv_ref, NEAR, ROWS, own % 2, own, starts_of(ids_ref, own), qt_ref, m_ref, l_ref, acc_ref)


def last_kernel(meta_ref, kv_ref, ids_ref, qt_ref, m_in, l_in, acc_in, out_ref, m_ref, l_ref, acc_ref):
    m_ref[...] = m_in[...]
    l_ref[...] = l_in[...]
    acc_ref[...] = acc_in[...]
    own = meta_ref[0]
    window(kv_ref, NEAR, ROWS, 1 - own % 2, own, starts_of(ids_ref, own), qt_ref, m_ref, l_ref, acc_ref)
    result = (acc_ref[...] * (1.0 / l_ref[...])).astype(jnp.bfloat16)
    for g in range(GROUP):
        out_ref[:, g * D:(g + 1) * D] = result[:, g * ROWS:(g + 1) * ROWS].T


VM = pl.BlockSpec(memory_space=pltpu.VMEM)
SM = pl.BlockSpec(memory_space=pltpu.SMEM)


def cost(keys):
    return pl.CostEstimate(flops=4 * D * QR * keys, bytes_accessed=1 << 20, transcendentals=QR * keys)


def per_device(queries, branch_key_value, branch_ids, pool, page_table):
    me = lax.axis_index("seq")
    y = (me // 2) % NY
    page = pool.reshape(1, PAGE, PAIR)
    raw = jnp.concatenate([jnp.transpose(branch_key_value, (1, 0, 2)), page], axis=0)
    one_raw = lax.ppermute(raw, "seq", x_ring(1))
    wide = jnp.concatenate([jnp.transpose(queries, (1, 0, 2)), raw[:8], one_raw[:8]], axis=2)
    wide = lax.all_to_all(wide, "head", split_axis=0, concat_axis=0, tiled=True).reshape(ROWS, -1)
    own, before = wide[:, GROUP * D:GROUP * D + PAIR], wide[:, GROUP * D + PAIR:]
    two_page = lax.ppermute(page, "seq", x_ring(2))
    three_page = lax.ppermute(page, "seq", x_ring(3))
    target = jnp.arange(NY, dtype=jnp.int32)[:, None, None]
    block = jnp.where(target > y, own[None], before[None])
    pages = jnp.concatenate([page, one_raw[8:], two_page, three_page], axis=0).reshape(1, NX * PAGE, PAIR)
    send = jnp.concatenate([block, jnp.broadcast_to(pages, (NY, NX * PAGE, PAIR))], axis=1)
    near = lax.all_to_all(send, "seq", split_axis=0, concat_axis=0, tiled=True, axis_index_groups=Y_GROUPS)
    later, _ = lax.optimization_barrier((own, send))
    side = lax.ppermute(later, "seq", SWAP)
    far = lax.ppermute(near[:, :ROWS], "seq", x_ring(1))
    near, own = lax.optimization_barrier((near, own))

    ids = branch_ids.reshape(2 * NX * NY, ROWS)
    meta = me.astype(jnp.int32).reshape(1)
    state = [
        jax.ShapeDtypeStruct((1, QR), jnp.float32),
        jax.ShapeDtypeStruct((1, QR), jnp.float32),
        jax.ShapeDtypeStruct((D, QR), jnp.float32),
    ]
    params = pltpu.CompilerParams(vmem_limit_bytes=40 * 1024 * 1024)
    qt, *now = pl.pallas_call(
        own_kernel,
        out_shape=[jax.ShapeDtypeStruct((PAIR, QR), jnp.bfloat16)] + state,
        in_specs=[SM] + [VM] * 4,
        out_specs=[VM] * 4,
        compiler_params=params,
        cost_estimate=cost(256),
        name="own_chip",
    )(meta, own, side, ids, wide)
    near, now = lax.optimization_barrier((near, now))
    near = near.reshape(NY * SLOT, PAIR)
    near_side = lax.ppermute(near, "seq", SWAP)
    now = pl.pallas_call(
        near_kernel,
        out_shape=state,
        in_specs=[SM, SM] + [VM] * 7,
        out_specs=[VM] * 3,
        scratch_shapes=[pltpu.VMEM((PAGES * PAGE, PAIR), jnp.bfloat16)],
        compiler_params=params,
        cost_estimate=cost(2560),
        name="near_window_and_prefix",
    )(meta, page_table.reshape(PAGES), near, near_side, ids, qt, *now)
    far, now = lax.optimization_barrier((far, now))
    far = far.reshape(NY * ROWS, PAIR)
    far_side = lax.ppermute(far, "seq", SWAP)
    now = pl.pallas_call(
        far_kernel,
        out_shape=state,
        in_specs=[SM] + [VM] * 6,
        out_specs=[VM] * 3,
        compiler_params=params,
        cost_estimate=cost(1024),
        name="far_window",
    )(meta, far, ids, qt, *now)
    out = pl.pallas_call(
        last_kernel,
        out_shape=jax.ShapeDtypeStruct((ROWS, GROUP * D), jnp.bfloat16),
        in_specs=[SM] + [VM] * 6,
        out_specs=VM,
        scratch_shapes=[
            pltpu.VMEM((1, QR), jnp.float32),
            pltpu.VMEM((1, QR), jnp.float32),
            pltpu.VMEM((D, QR), jnp.float32),
        ],
        compiler_params=params,
        cost_estimate=cost(1024),
        name="far_other_core",
    )(meta, far_side, ids, qt, *now)
    out = lax.all_to_all(out.reshape(8, ROWS // 8, GROUP * D), "head", split_axis=0, concat_axis=0, tiled=True)
    return jnp.transpose(out, (1, 0, 2))


def solution(mesh):
    return jax.shard_map(
        per_device,
        mesh=mesh,
        in_specs=(
            P(("seq", "head"), None, None),
            P(("seq", "head"), None, None),
            P(),
            P("seq", None, "head", None),
            P("head", None),
        ),
        out_specs=P(("seq", "head"), None, None),
        check_vma=False,
    )
```

```python
import jax
import jax.numpy as jnp
from jax import lax
from jax.experimental import pallas as pl
from jax.experimental.pallas import tpu as pltpu
from jax.sharding import PartitionSpec as P

D = 128
PAIR = 2 * D
ROWS = 128
GROUP = 8
QR = ROWS * GROUP
NX, NY = 4, 8
PAGES = 32
PAGE = 16
BLOCKS = 4
TILE = 512
SCALE2 = D ** (-0.5) * 1.4426950408889634
LOW = -1e30
SLOT = ROWS + NX * PAGE
NEAR = 8


def x_ring(by):
    return [
        ((x * NY + y) * 2 + c, (((x + by) % NX) * NY + y) * 2 + c)
        for x in range(NX) for y in range(NY) for c in range(2)
    ]


SWAP = [(i, i ^ 1) for i in range(2 * NX * NY)]
Y_GROUPS = [[(x * NY + y) * 2 + c for y in range(NY)] for x in range(NX) for c in range(2)]


def fold(keys, values, mask, qt_ref, m_ref, l_ref, acc_ref):
    twice = jnp.concatenate([keys, keys], axis=1)
    lifted = jnp.concatenate([values.T, jnp.ones((16, keys.shape[0]), jnp.bfloat16)], axis=0)

    def scores_of(at):
        scores = jnp.dot(twice, qt_ref[:, at:at + TILE], preferred_element_type=jnp.float32)
        if mask is not None:
            scores = jnp.where(jnp.concatenate([mask] * (TILE // ROWS), axis=1), scores, LOW)
        return scores

    coming = scores_of(0)
    for at in range(0, QR, TILE):
        cols = slice(at, at + TILE)
        scores = coming
        if at + TILE < QR:
            coming = scores_of(at + TILE)
        old = m_ref[:, cols]
        top = jnp.maximum(old, jnp.max(scores, axis=0, keepdims=True))
        weights = jnp.exp2(scores - top).astype(jnp.bfloat16)
        factor = jnp.exp2(old - top)
        m_ref[:, cols] = top
        mixed = jnp.dot(lifted, weights, preferred_element_type=jnp.float32)
        l_ref[:, cols] = l_ref[:, cols] * factor + mixed[D:D + 1]
        acc_ref[:, cols] = acc_ref[:, cols] * factor + mixed[:D]


def starts_of(ids_ref, own):
    ids = ids_ref[...]
    starts = [jnp.sum((ids < b).astype(jnp.int32)) for b in range(1, 4)]
    own_ids = ids_ref[pl.ds(own, 1), :]
    row_start = jnp.zeros_like(own_ids)
    for b in range(1, 4):
        row_start = jnp.where(own_ids == b, starts[b - 1], row_start)
    return row_start, jnp.min(row_start), jnp.max(row_start)


def mask_of(block, own, row_start):
    key_rows = lax.broadcasted_iota(jnp.int32, (ROWS, ROWS), 0) + block * ROWS
    query_rows = lax.broadcasted_iota(jnp.int32, (ROWS, ROWS), 1) + own * ROWS
    return (key_rows >= row_start) & (key_rows <= query_rows)


def own_kernel(meta_ref, mine_ref, side_ref, ids_ref, q_ref, qt_ref, m_ref, l_ref, acc_ref):
    own = meta_ref[0]
    row_start, first, last = starts_of(ids_ref, own)
    for g in range(GROUP):
        scaled = q_ref[:, g * D:(g + 1) * D].astype(jnp.float32) * SCALE2
        high = scaled.astype(jnp.bfloat16)
        low = (scaled - high.astype(jnp.float32)).astype(jnp.bfloat16)
        qt_ref[:D, g * ROWS:(g + 1) * ROWS] = high.T
        qt_ref[D:, g * ROWS:(g + 1) * ROWS] = low.T
    m_ref[...] = jnp.full_like(m_ref, LOW)
    l_ref[...] = jnp.zeros_like(l_ref)
    acc_ref[...] = jnp.zeros_like(acc_ref)
    state = (qt_ref, m_ref, l_ref, acc_ref)
    fold(mine_ref[:, :D], mine_ref[:, D:], mask_of(own, own, row_start), *state)

    @pl.when((own % 2 == 1) & (own * ROWS > first))
    def _():
        fold(side_ref[:, :D], side_ref[:, D:], mask_of(own - 1, own, row_start), *state)


def window(kv_ref, skip, slot, core, own, limits, qt_ref, m_ref, l_ref, acc_ref):
    row_start, first, last = limits
    chip = own // 2 - skip
    lowest = jnp.maximum((jnp.maximum(first // ROWS - core, -1) + 1) // 2, chip - NEAR)
    steps = jnp.maximum(chip - lowest + BLOCKS - 1, 0) // BLOCKS

    def step(i, carry):
        base = chip - BLOCKS * (i + 1)
        pairs = []
        for b in range(BLOCKS):
            start = (base + b + 4 * NY) % NY * slot
            pairs.append(kv_ref[pl.ds(pl.multiple_of(start, PAGE), ROWS), :])
        keys = jnp.concatenate([pair[:, :D] for pair in pairs], axis=0)
        values = jnp.concatenate([pair[:, D:] for pair in pairs], axis=0)
        whole = (2 * base + core) * ROWS >= last

        @pl.when(whole)
        def _():
            fold(keys, values, None, qt_ref, m_ref, l_ref, acc_ref)

        @pl.when(jnp.logical_not(whole))
        def _():
            mask = jnp.concatenate(
                [mask_of(2 * (base + b) + core, own, row_start) for b in range(BLOCKS)], axis=0
            )
            fold(keys, values, mask, qt_ref, m_ref, l_ref, acc_ref)

        return carry

    lax.fori_loop(0, steps, step, 0)


def near_kernel(meta_ref, table_ref, kv_ref, side_ref, ids_ref, qt_ref, m_in, l_in, acc_in,
                m_ref, l_ref, acc_ref, prefix_ref):
    m_ref[...] = m_in[...]
    l_ref[...] = l_in[...]
    acc_ref[...] = acc_in[...]
    own = meta_ref[0]
    core, x = own % 2, own // (2 * NY)
    for i in range(PAGES):
        page = table_ref[i]
        start = (page // 2) % NY * SLOT + ROWS + (x + NX - page // (2 * NY)) % NX * PAGE
        rows = pl.ds(pl.multiple_of(start, PAGE), PAGE)

        @pl.when(page % 2 == core)
        def _():
            prefix_ref[i * PAGE:(i + 1) * PAGE, :] = kv_ref[rows, :]

        @pl.when(page % 2 != core)
        def _():
            prefix_ref[i * PAGE:(i + 1) * PAGE, :] = side_ref[rows, :]

    fold(prefix_ref[:, :D], prefix_ref[:, D:], None, qt_ref, m_ref, l_ref, acc_ref)
    limits = starts_of(ids_ref, own)
    window(kv_ref, 0, SLOT, core, own, limits, qt_ref, m_ref, l_ref, acc_ref)
    window(side_ref, 0, SLOT, 1 - core, own, limits, qt_ref, m_ref, l_ref, acc_ref)


def far_kernel(meta_ref, kv_ref, ids_ref, qt_ref, m_in, l_in, acc_in, m_ref, l_ref, acc_ref):
    m_ref[...] = m_in[...]
    l_ref[...] = l_in[...]
    acc_ref[...] = acc_in[...]
    own = meta_ref[0]
    window(kv_ref, NEAR, ROWS, own % 2, own, starts_of(ids_ref, own), qt_ref, m_ref, l_ref, acc_ref)


def last_kernel(meta_ref, kv_ref, ids_ref, qt_ref, m_in, l_in, acc_in, out_ref, m_ref, l_ref, acc_ref):
    m_ref[...] = m_in[...]
    l_ref[...] = l_in[...]
    acc_ref[...] = acc_in[...]
    own = meta_ref[0]
    window(kv_ref, NEAR, ROWS, 1 - own % 2, own, starts_of(ids_ref, own), qt_ref, m_ref, l_ref, acc_ref)
    result = (acc_ref[...] * (1.0 / l_ref[...])).astype(jnp.bfloat16)
    for g in range(GROUP):
        out_ref[:, g * D:(g + 1) * D] = result[:, g * ROWS:(g + 1) * ROWS].T


VM = pl.BlockSpec(memory_space=pltpu.VMEM)
SM = pl.BlockSpec(memory_space=pltpu.SMEM)


def cost(keys):
    return pl.CostEstimate(flops=4 * D * QR * keys, bytes_accessed=1 << 20, transcendentals=QR * keys)


def per_device(queries, branch_key_value, branch_ids, pool, page_table):
    me = lax.axis_index("seq")
    y = (me // 2) % NY
    page = pool.reshape(1, PAGE, PAIR)
    raw = jnp.concatenate([jnp.transpose(branch_key_value, (1, 0, 2)), page], axis=0)
    one_raw = lax.ppermute(raw, "seq", x_ring(1))
    wide = jnp.concatenate([jnp.transpose(queries, (1, 0, 2)), raw[:8], one_raw[:8]], axis=2)
    wide = lax.all_to_all(wide, "head", split_axis=0, concat_axis=0, tiled=True).reshape(ROWS, -1)
    own, before = wide[:, GROUP * D:GROUP * D + PAIR], wide[:, GROUP * D + PAIR:]
    two_page = lax.ppermute(page, "seq", x_ring(2))
    three_page = lax.ppermute(page, "seq", x_ring(3))
    target = jnp.arange(NY, dtype=jnp.int32)[:, None, None]
    block = jnp.where(target > y, own[None], before[None])
    pages = jnp.concatenate([page, one_raw[8:], two_page, three_page], axis=0).reshape(1, NX * PAGE, PAIR)
    send = jnp.concatenate([block, jnp.broadcast_to(pages, (NY, NX * PAGE, PAIR))], axis=1)
    near = lax.all_to_all(send, "seq", split_axis=0, concat_axis=0, tiled=True, axis_index_groups=Y_GROUPS)
    later, _ = lax.optimization_barrier((own, send))
    side = lax.ppermute(later, "seq", SWAP)
    far = lax.ppermute(near[:, :ROWS], "seq", x_ring(1))
    near, own = lax.optimization_barrier((near, own))

    ids = branch_ids.reshape(2 * NX * NY, ROWS)
    meta = me.astype(jnp.int32).reshape(1)
    state = [
        jax.ShapeDtypeStruct((1, QR), jnp.float32),
        jax.ShapeDtypeStruct((1, QR), jnp.float32),
        jax.ShapeDtypeStruct((D, QR), jnp.float32),
    ]
    params = pltpu.CompilerParams(vmem_limit_bytes=40 * 1024 * 1024)
    qt, *now = pl.pallas_call(
        own_kernel,
        out_shape=[jax.ShapeDtypeStruct((PAIR, QR), jnp.bfloat16)] + state,
        in_specs=[SM] + [VM] * 4,
        out_specs=[VM] * 4,
        compiler_params=params,
        cost_estimate=cost(8),
        name="own_chip",
    )(meta, own, side, ids, wide)
    near, now = lax.optimization_barrier((near, now))
    near = near.reshape(NY * SLOT, PAIR)
    near_side = lax.ppermute(near, "seq", SWAP)
    now = pl.pallas_call(
        near_kernel,
        out_shape=state,
        in_specs=[SM, SM] + [VM] * 7,
        out_specs=[VM] * 3,
        scratch_shapes=[pltpu.VMEM((PAGES * PAGE, PAIR), jnp.bfloat16)],
        compiler_params=params,
        cost_estimate=cost(8),
        name="near_window_and_prefix",
    )(meta, page_table.reshape(PAGES), near, near_side, ids, qt, *now)
    far, now = lax.optimization_barrier((far, now))
    far = far.reshape(NY * ROWS, PAIR)
    far_side = lax.ppermute(far, "seq", SWAP)
    now = pl.pallas_call(
        far_kernel,
        out_shape=state,
        in_specs=[SM] + [VM] * 6,
        out_specs=[VM] * 3,
        compiler_params=params,
        cost_estimate=cost(1024),
        name="far_window",
    )(meta, far, ids, qt, *now)
    out = pl.pallas_call(
        last_kernel,
        out_shape=jax.ShapeDtypeStruct((ROWS, GROUP * D), jnp.bfloat16),
        in_specs=[SM] + [VM] * 6,
        out_specs=VM,
        scratch_shapes=[
            pltpu.VMEM((1, QR), jnp.float32),
            pltpu.VMEM((1, QR), jnp.float32),
            pltpu.VMEM((D, QR), jnp.float32),
        ],
        compiler_params=params,
        cost_estimate=cost(1024),
        name="far_other_core",
    )(meta, far_side, ids, qt, *now)
    out = lax.all_to_all(out.reshape(8, ROWS // 8, GROUP * D), "head", split_axis=0, concat_axis=0, tiled=True)
    return jnp.transpose(out, (1, 0, 2))


def solution(mesh):
    return jax.shard_map(
        per_device,
        mesh=mesh,
        in_specs=(
            P(("seq", "head"), None, None),
            P(("seq", "head"), None, None),
            P(),
            P("seq", None, "head", None),
            P("head", None),
        ),
        out_specs=P(("seq", "head"), None, None),
        check_vma=False,
    )
```

```python
import jax
import jax.numpy as jnp
from jax import lax
from jax.experimental import pallas as pl
from jax.experimental.pallas import tpu as pltpu
from jax.sharding import PartitionSpec as P

D = 128
PAIR = 2 * D
ROWS = 128
GROUP = 8
QR = ROWS * GROUP
NX, NY = 4, 8
PAGES = 32
PAGE = 16
BLOCKS = 4
TILE = 512
SCALE2 = D ** (-0.5) * 1.4426950408889634
LOW = -1e30
SLOT = ROWS + NX * PAGE
NEAR = 8


def x_ring(by):
    return [
        ((x * NY + y) * 2 + c, (((x + by) % NX) * NY + y) * 2 + c)
        for x in range(NX) for y in range(NY) for c in range(2)
    ]


SWAP = [(i, i ^ 1) for i in range(2 * NX * NY)]
Y_GROUPS = [[(x * NY + y) * 2 + c for y in range(NY)] for x in range(NX) for c in range(2)]


def fold(keys, values, mask, qt_ref, m_ref, l_ref, acc_ref):
    twice = jnp.concatenate([keys, keys], axis=1)
    lifted = jnp.concatenate([values.T, jnp.ones((16, keys.shape[0]), jnp.bfloat16)], axis=0)

    def scores_of(at):
        scores = jnp.dot(twice, qt_ref[:, at:at + TILE], preferred_element_type=jnp.float32)
        if mask is not None:
            scores = jnp.where(jnp.concatenate([mask] * (TILE // ROWS), axis=1), scores, LOW)
        return scores

    coming = scores_of(0)
    for at in range(0, QR, TILE):
        cols = slice(at, at + TILE)
        scores = coming
        if at + TILE < QR:
            coming = scores_of(at + TILE)
        old = m_ref[:, cols]
        top = jnp.maximum(old, jnp.max(scores, axis=0, keepdims=True))
        weights = jnp.exp2(scores - top).astype(jnp.bfloat16)
        factor = jnp.exp2(old - top)
        m_ref[:, cols] = top
        mixed = jnp.dot(lifted, weights, preferred_element_type=jnp.float32)
        l_ref[:, cols] = l_ref[:, cols] * factor + mixed[D:D + 1]
        acc_ref[:, cols] = acc_ref[:, cols] * factor + mixed[:D]


def starts_of(ids_ref, own):
    ids = ids_ref[...]
    starts = [jnp.sum((ids < b).astype(jnp.int32)) for b in range(1, 4)]
    own_ids = ids_ref[pl.ds(own, 1), :]
    row_start = jnp.zeros_like(own_ids)
    for b in range(1, 4):
        row_start = jnp.where(own_ids == b, starts[b - 1], row_start)
    return row_start, jnp.min(row_start), jnp.max(row_start)


def mask_of(block, own, row_start):
    key_rows = lax.broadcasted_iota(jnp.int32, (ROWS, ROWS), 0) + block * ROWS
    query_rows = lax.broadcasted_iota(jnp.int32, (ROWS, ROWS), 1) + own * ROWS
    return (key_rows >= row_start) & (key_rows <= query_rows)


def own_kernel(meta_ref, mine_ref, side_ref, ids_ref, q_ref, qt_ref, m_ref, l_ref, acc_ref):
    own = meta_ref[0]
    row_start, first, last = starts_of(ids_ref, own)
    for g in range(GROUP):
        scaled = q_ref[:, g * D:(g + 1) * D].astype(jnp.float32) * SCALE2
        high = scaled.astype(jnp.bfloat16)
        low = (scaled - high.astype(jnp.float32)).astype(jnp.bfloat16)
        qt_ref[:D, g * ROWS:(g + 1) * ROWS] = high.T
        qt_ref[D:, g * ROWS:(g + 1) * ROWS] = low.T
    m_ref[...] = jnp.full_like(m_ref, LOW)
    l_ref[...] = jnp.zeros_like(l_ref)
    acc_ref[...] = jnp.zeros_like(acc_ref)
    state = (qt_ref, m_ref, l_ref, acc_ref)
    fold(mine_ref[:, :D], mine_ref[:, D:], mask_of(own, own, row_start), *state)

    @pl.when((own % 2 == 1) & (own * ROWS > first))
    def _():
        fold(side_ref[:, :D], side_ref[:, D:], mask_of(own - 1, own, row_start), *state)


def window(kv_ref, skip, slot, core, own, limits, qt_ref, m_ref, l_ref, acc_ref):
    row_start, first, last = limits
    chip = own // 2 - skip
    lowest = jnp.maximum((jnp.maximum(first // ROWS - core, -1) + 1) // 2, chip - NEAR)
    steps = jnp.maximum(chip - lowest + BLOCKS - 1, 0) // BLOCKS

    def step(i, carry):
        base = chip - BLOCKS * (i + 1)
        pairs = []
        for b in range(BLOCKS):
            start = (base + b + 4 * NY) % NY * slot
            pairs.append(kv_ref[pl.ds(pl.multiple_of(start, PAGE), ROWS), :])
        keys = jnp.concatenate([pair[:, :D] for pair in pairs], axis=0)
        values = jnp.concatenate([pair[:, D:] for pair in pairs], axis=0)
        whole = (2 * base + core) * ROWS >= last

        @pl.when(whole)
        def _():
            fold(keys, values, None, qt_ref, m_ref, l_ref, acc_ref)

        @pl.when(jnp.logical_not(whole))
        def _():
            mask = jnp.concatenate(
                [mask_of(2 * (base + b) + core, own, row_start) for b in range(BLOCKS)], axis=0
            )
            fold(keys, values, mask, qt_ref, m_ref, l_ref, acc_ref)

        return carry

    lax.fori_loop(0, steps, step, 0)


def near_kernel(meta_ref, table_ref, kv_ref, side_ref, ids_ref, qt_ref, m_in, l_in, acc_in,
                m_ref, l_ref, acc_ref, prefix_ref):
    m_ref[...] = m_in[...]
    l_ref[...] = l_in[...]
    acc_ref[...] = acc_in[...]
    own = meta_ref[0]
    core, x = own % 2, own // (2 * NY)
    for i in range(PAGES):
        page = table_ref[i]
        start = (page // 2) % NY * SLOT + ROWS + (x + NX - page // (2 * NY)) % NX * PAGE
        rows = pl.ds(pl.multiple_of(start, PAGE), PAGE)

        @pl.when(page % 2 == core)
        def _():
            prefix_ref[i * PAGE:(i + 1) * PAGE, :] = kv_ref[rows, :]

        @pl.when(page % 2 != core)
        def _():
            prefix_ref[i * PAGE:(i + 1) * PAGE, :] = side_ref[rows, :]

    fold(prefix_ref[:, :D], prefix_ref[:, D:], None, qt_ref, m_ref, l_ref, acc_ref)
    limits = starts_of(ids_ref, own)
    window(kv_ref, 0, SLOT, core, own, limits, qt_ref, m_ref, l_ref, acc_ref)
    window(side_ref, 0, SLOT, 1 - core, own, limits, qt_ref, m_ref, l_ref, acc_ref)


def far_kernel(meta_ref, kv_ref, ids_ref, qt_ref, m_in, l_in, acc_in, m_ref, l_ref, acc_ref):
    m_ref[...] = m_in[...]
    l_ref[...] = l_in[...]
    acc_ref[...] = acc_in[...]
    own = meta_ref[0]
    window(kv_ref, NEAR, ROWS, own % 2, own, starts_of(ids_ref, own), qt_ref, m_ref, l_ref, acc_ref)


def last_kernel(meta_ref, kv_ref, ids_ref, qt_ref, m_in, l_in, acc_in, out_ref, m_ref, l_ref, acc_ref):
    m_ref[...] = m_in[...]
    l_ref[...] = l_in[...]
    acc_ref[...] = acc_in[...]
    own = meta_ref[0]
    window(kv_ref, NEAR, ROWS, 1 - own % 2, own, starts_of(ids_ref, own), qt_ref, m_ref, l_ref, acc_ref)
    result = (acc_ref[...] * (1.0 / l_ref[...])).astype(jnp.bfloat16)
    for g in range(GROUP):
        out_ref[:, g * D:(g + 1) * D] = result[:, g * ROWS:(g + 1) * ROWS].T


VM = pl.BlockSpec(memory_space=pltpu.VMEM)
SM = pl.BlockSpec(memory_space=pltpu.SMEM)


def cost(keys):
    return pl.CostEstimate(flops=4 * D * QR * keys, bytes_accessed=1 << 20, transcendentals=QR * keys)


def per_device(queries, branch_key_value, branch_ids, pool, page_table):
    me = lax.axis_index("seq")
    y = (me // 2) % NY
    page = pool.reshape(1, PAGE, PAIR)
    raw = jnp.concatenate([jnp.transpose(branch_key_value, (1, 0, 2)), page], axis=0)
    one_raw = lax.ppermute(raw, "seq", x_ring(1))
    wide = jnp.concatenate([jnp.transpose(queries, (1, 0, 2)), raw[:8], one_raw[:8]], axis=2)
    wide = lax.all_to_all(wide, "head", split_axis=0, concat_axis=0, tiled=True).reshape(ROWS, -1)
    own, before = wide[:, GROUP * D:GROUP * D + PAIR], wide[:, GROUP * D + PAIR:]
    two_page = lax.ppermute(page, "seq", x_ring(2))
    three_page = lax.ppermute(page, "seq", x_ring(3))
    target = jnp.arange(NY, dtype=jnp.int32)[:, None, None]
    block = jnp.where(target > y, own[None], before[None])
    pages = jnp.concatenate([page, one_raw[8:], two_page, three_page], axis=0).reshape(1, NX * PAGE, PAIR)
    send = jnp.concatenate([block, jnp.broadcast_to(pages, (NY, NX * PAGE, PAIR))], axis=1)
    near = lax.all_to_all(send, "seq", split_axis=0, concat_axis=0, tiled=True, axis_index_groups=Y_GROUPS)
    later, _ = lax.optimization_barrier((own, send))
    side = lax.ppermute(later, "seq", SWAP)
    far = lax.ppermute(near[:, :ROWS], "seq", x_ring(1))
    near, own = lax.optimization_barrier((near, own))

    ids = branch_ids.reshape(2 * NX * NY, ROWS)
    meta = me.astype(jnp.int32).reshape(1)
    state = [
        jax.ShapeDtypeStruct((1, QR), jnp.float32),
        jax.ShapeDtypeStruct((1, QR), jnp.float32),
        jax.ShapeDtypeStruct((D, QR), jnp.float32),
    ]
    params = pltpu.CompilerParams(vmem_limit_bytes=40 * 1024 * 1024)
    def near_part(operands):
        near, own, side, wide = operands
        near = near.reshape(NY * SLOT, PAIR)
        near_side = lax.ppermute(near, "seq", SWAP)
        qt, *now = pl.pallas_call(
            own_kernel,
            out_shape=[jax.ShapeDtypeStruct((PAIR, QR), jnp.bfloat16)] + state,
            in_specs=[SM] + [VM] * 4,
            out_specs=[VM] * 4,
            compiler_params=params,
            cost_estimate=cost(256),
            name="own_chip",
        )(meta, own, side, ids, wide)
        now = pl.pallas_call(
            near_kernel,
            out_shape=state,
            in_specs=[SM, SM] + [VM] * 7,
            out_specs=[VM] * 3,
            scratch_shapes=[pltpu.VMEM((PAGES * PAGE, PAIR), jnp.bfloat16)],
            compiler_params=params,
            cost_estimate=cost(2560),
            name="near_window_and_prefix",
        )(meta, page_table.reshape(PAGES), near, near_side, ids, qt, *now)
        return [qt, *now]

    def nothing(operands):
        return [jnp.zeros(a.shape, a.dtype) for a in [jax.ShapeDtypeStruct((PAIR, QR), jnp.bfloat16)] + state]

    qt, *now = lax.cond(branch_ids[0] >= 0, near_part, nothing, (near, own, side, wide))
    far, now = lax.optimization_barrier((far, now))
    far = far.reshape(NY * ROWS, PAIR)
    far_side = lax.ppermute(far, "seq", SWAP)
    now = pl.pallas_call(
        far_kernel,
        out_shape=state,
        in_specs=[SM] + [VM] * 6,
        out_specs=[VM] * 3,
        compiler_params=params,
        cost_estimate=cost(1024),
        name="far_window",
    )(meta, far, ids, qt, *now)
    out = pl.pallas_call(
        last_kernel,
        out_shape=jax.ShapeDtypeStruct((ROWS, GROUP * D), jnp.bfloat16),
        in_specs=[SM] + [VM] * 6,
        out_specs=VM,
        scratch_shapes=[
            pltpu.VMEM((1, QR), jnp.float32),
            pltpu.VMEM((1, QR), jnp.float32),
            pltpu.VMEM((D, QR), jnp.float32),
        ],
        compiler_params=params,
        cost_estimate=cost(1024),
        name="far_other_core",
    )(meta, far_side, ids, qt, *now)
    out = lax.all_to_all(out.reshape(8, ROWS // 8, GROUP * D), "head", split_axis=0, concat_axis=0, tiled=True)
    return jnp.transpose(out, (1, 0, 2))


def solution(mesh):
    return jax.shard_map(
        per_device,
        mesh=mesh,
        in_specs=(
            P(("seq", "head"), None, None),
            P(("seq", "head"), None, None),
            P(),
            P("seq", None, "head", None),
            P("head", None),
        ),
        out_specs=P(("seq", "head"), None, None),
        check_vma=False,
    )
```

```python
import jax
import jax.numpy as jnp
from jax import lax
from jax.experimental import pallas as pl
from jax.experimental.pallas import tpu as pltpu
from jax.sharding import PartitionSpec as P

D = 128
PAIR = 2 * D
ROWS = 128
GROUP = 8
QR = ROWS * GROUP
NX, NY = 4, 8
PAGES = 32
PAGE = 16
BLOCKS = 4
TILE = 512
SCALE2 = D ** (-0.5) * 1.4426950408889634
LOW = -1e30
SLOT = ROWS + NX * PAGE
NEAR = 8


def x_ring(by):
    return [
        ((x * NY + y) * 2 + c, (((x + by) % NX) * NY + y) * 2 + c)
        for x in range(NX) for y in range(NY) for c in range(2)
    ]


SWAP = [(i, i ^ 1) for i in range(2 * NX * NY)]
Y_GROUPS = [[(x * NY + y) * 2 + c for y in range(NY)] for x in range(NX) for c in range(2)]


def fold(keys, values, mask, qt_ref, m_ref, l_ref, acc_ref):
    twice = jnp.concatenate([keys, keys], axis=1)
    lifted = jnp.concatenate([values.T, jnp.ones((16, keys.shape[0]), jnp.bfloat16)], axis=0)

    def scores_of(at):
        scores = jnp.dot(twice, qt_ref[:, at:at + TILE], preferred_element_type=jnp.float32)
        if mask is not None:
            scores = jnp.where(jnp.concatenate([mask] * (TILE // ROWS), axis=1), scores, LOW)
        return scores

    coming = scores_of(0)
    for at in range(0, QR, TILE):
        cols = slice(at, at + TILE)
        scores = coming
        if at + TILE < QR:
            coming = scores_of(at + TILE)
        old = m_ref[:, cols]
        top = jnp.maximum(old, jnp.max(scores, axis=0, keepdims=True))
        weights = jnp.exp2(scores - top).astype(jnp.bfloat16)
        factor = jnp.exp2(old - top)
        m_ref[:, cols] = top
        mixed = jnp.dot(lifted, weights, preferred_element_type=jnp.float32)
        l_ref[:, cols] = l_ref[:, cols] * factor + mixed[D:D + 1]
        acc_ref[:, cols] = acc_ref[:, cols] * factor + mixed[:D]


def starts_of(ids_ref, own):
    ids = ids_ref[...]
    starts = [jnp.sum((ids < b).astype(jnp.int32)) for b in range(1, 4)]
    own_ids = ids_ref[pl.ds(own, 1), :]
    row_start = jnp.zeros_like(own_ids)
    for b in range(1, 4):
        row_start = jnp.where(own_ids == b, starts[b - 1], row_start)
    return row_start, jnp.min(row_start), jnp.max(row_start)


def mask_of(block, own, row_start):
    key_rows = lax.broadcasted_iota(jnp.int32, (ROWS, ROWS), 0) + block * ROWS
    query_rows = lax.broadcasted_iota(jnp.int32, (ROWS, ROWS), 1) + own * ROWS
    return (key_rows >= row_start) & (key_rows <= query_rows)


def own_kernel(meta_ref, mine_ref, side_ref, ids_ref, q_ref, qt_ref, m_ref, l_ref, acc_ref):
    own = meta_ref[0]
    row_start, first, last = starts_of(ids_ref, own)
    for g in range(GROUP):
        scaled = q_ref[:, g * D:(g + 1) * D].astype(jnp.float32) * SCALE2
        high = scaled.astype(jnp.bfloat16)
        low = (scaled - high.astype(jnp.float32)).astype(jnp.bfloat16)
        qt_ref[:D, g * ROWS:(g + 1) * ROWS] = high.T
        qt_ref[D:, g * ROWS:(g + 1) * ROWS] = low.T
    m_ref[...] = jnp.full_like(m_ref, LOW)
    l_ref[...] = jnp.zeros_like(l_ref)
    acc_ref[...] = jnp.zeros_like(acc_ref)
    state = (qt_ref, m_ref, l_ref, acc_ref)
    fold(mine_ref[:, :D], mine_ref[:, D:], mask_of(own, own, row_start), *state)

    @pl.when((own % 2 == 1) & (own * ROWS > first))
    def _():
        fold(side_ref[:, :D], side_ref[:, D:], mask_of(own - 1, own, row_start), *state)


def window(kv_ref, skip, slot, core, own, limits, qt_ref, m_ref, l_ref, acc_ref):
    row_start, first, last = limits
    chip = own // 2 - skip
    lowest = jnp.maximum((jnp.maximum(first // ROWS - core, -1) + 1) // 2, chip - NEAR)
    steps = jnp.maximum(chip - lowest + BLOCKS - 1, 0) // BLOCKS

    def step(i, carry):
        base = chip - BLOCKS * (i + 1)
        pairs = []
        for b in range(BLOCKS):
            start = (base + b + 4 * NY) % NY * slot
            pairs.append(kv_ref[pl.ds(pl.multiple_of(start, PAGE), ROWS), :])
        keys = jnp.concatenate([pair[:, :D] for pair in pairs], axis=0)
        values = jnp.concatenate([pair[:, D:] for pair in pairs], axis=0)
        whole = (2 * base + core) * ROWS >= last

        @pl.when(whole)
        def _():
            fold(keys, values, None, qt_ref, m_ref, l_ref, acc_ref)

        @pl.when(jnp.logical_not(whole))
        def _():
            mask = jnp.concatenate(
                [mask_of(2 * (base + b) + core, own, row_start) for b in range(BLOCKS)], axis=0
            )
            fold(keys, values, mask, qt_ref, m_ref, l_ref, acc_ref)

        return carry

    lax.fori_loop(0, steps, step, 0)


def near_kernel(meta_ref, table_ref, kv_ref, side_ref, ids_ref, qt_ref, m_in, l_in, acc_in,
                m_ref, l_ref, acc_ref, prefix_ref):
    m_ref[...] = m_in[...]
    l_ref[...] = l_in[...]
    acc_ref[...] = acc_in[...]
    own = meta_ref[0]
    core, x = own % 2, own // (2 * NY)
    for i in range(PAGES):
        page = table_ref[i]
        start = (page // 2) % NY * SLOT + ROWS + (x + NX - page // (2 * NY)) % NX * PAGE
        rows = pl.ds(pl.multiple_of(start, PAGE), PAGE)

        @pl.when(page % 2 == core)
        def _():
            prefix_ref[i * PAGE:(i + 1) * PAGE, :] = kv_ref[rows, :]

        @pl.when(page % 2 != core)
        def _():
            prefix_ref[i * PAGE:(i + 1) * PAGE, :] = side_ref[rows, :]

    fold(prefix_ref[:, :D], prefix_ref[:, D:], None, qt_ref, m_ref, l_ref, acc_ref)
    limits = starts_of(ids_ref, own)
    window(kv_ref, 0, SLOT, core, own, limits, qt_ref, m_ref, l_ref, acc_ref)
    window(side_ref, 0, SLOT, 1 - core, own, limits, qt_ref, m_ref, l_ref, acc_ref)


def far_kernel(meta_ref, kv_ref, ids_ref, qt_ref, m_in, l_in, acc_in, m_ref, l_ref, acc_ref):
    m_ref[...] = m_in[...]
    l_ref[...] = l_in[...]
    acc_ref[...] = acc_in[...]
    own = meta_ref[0]
    window(kv_ref, NEAR, ROWS, own % 2, own, starts_of(ids_ref, own), qt_ref, m_ref, l_ref, acc_ref)


def last_kernel(meta_ref, kv_ref, ids_ref, qt_ref, m_in, l_in, acc_in, out_ref, m_ref, l_ref, acc_ref):
    m_ref[...] = m_in[...]
    l_ref[...] = l_in[...]
    acc_ref[...] = acc_in[...]
    own = meta_ref[0]
    window(kv_ref, NEAR, ROWS, 1 - own % 2, own, starts_of(ids_ref, own), qt_ref, m_ref, l_ref, acc_ref)
    result = (acc_ref[...] * (1.0 / l_ref[...])).astype(jnp.bfloat16)
    for g in range(GROUP):
        out_ref[:, g * D:(g + 1) * D] = result[:, g * ROWS:(g + 1) * ROWS].T


VM = pl.BlockSpec(memory_space=pltpu.VMEM)
SM = pl.BlockSpec(memory_space=pltpu.SMEM)


def cost(keys):
    return pl.CostEstimate(flops=4 * D * QR * keys, bytes_accessed=1 << 20, transcendentals=QR * keys)


def per_device(queries, branch_key_value, branch_ids, pool, page_table):
    me = lax.axis_index("seq")
    y = (me // 2) % NY
    page = pool.reshape(1, PAGE, PAIR)
    raw = jnp.concatenate([jnp.transpose(branch_key_value, (1, 0, 2)), page], axis=0)
    one_raw = lax.ppermute(raw, "seq", x_ring(1))
    wide = jnp.concatenate([jnp.transpose(queries, (1, 0, 2)), raw[:8], one_raw[:8]], axis=2)
    wide = lax.all_to_all(wide, "head", split_axis=0, concat_axis=0, tiled=True).reshape(ROWS, -1)
    own, before = wide[:, GROUP * D:GROUP * D + PAIR], wide[:, GROUP * D + PAIR:]
    two_page = lax.ppermute(page, "seq", x_ring(2))
    three_page = lax.ppermute(page, "seq", x_ring(3))
    target = jnp.arange(NY, dtype=jnp.int32)[:, None, None]
    block = jnp.where(target > y, own[None], before[None])
    pages = jnp.concatenate([page, one_raw[8:], two_page, three_page], axis=0).reshape(1, NX * PAGE, PAIR)
    send = jnp.concatenate([block, jnp.broadcast_to(pages, (NY, NX * PAGE, PAIR))], axis=1)
    near = lax.all_to_all(send, "seq", split_axis=0, concat_axis=0, tiled=True, axis_index_groups=Y_GROUPS)
    later, _ = lax.optimization_barrier((own, send))
    side = lax.ppermute(later, "seq", SWAP)
    ids = branch_ids.reshape(2 * NX * NY, ROWS)
    meta = me.astype(jnp.int32).reshape(1)
    state = [
        jax.ShapeDtypeStruct((1, QR), jnp.float32),
        jax.ShapeDtypeStruct((1, QR), jnp.float32),
        jax.ShapeDtypeStruct((D, QR), jnp.float32),
    ]
    params = pltpu.CompilerParams(vmem_limit_bytes=40 * 1024 * 1024)
    qt, *now = pl.pallas_call(
        own_kernel,
        out_shape=[jax.ShapeDtypeStruct((PAIR, QR), jnp.bfloat16)] + state,
        in_specs=[SM] + [VM] * 4,
        out_specs=[VM] * 4,
        compiler_params=params,
        cost_estimate=cost(256),
        name="own_chip",
    )(meta, own, side, ids, wide)
    near, qt, now = lax.optimization_barrier((near, qt, now))
    far = lax.ppermute(near[:, :ROWS], "seq", x_ring(1))

    def near_part(operands):
        near, qt, now = operands
        near = near.reshape(NY * SLOT, PAIR)
        near_side = lax.ppermute(near, "seq", SWAP)
        return list(pl.pallas_call(
            near_kernel,
            out_shape=state,
            in_specs=[SM, SM] + [VM] * 7,
            out_specs=[VM] * 3,
            scratch_shapes=[pltpu.VMEM((PAGES * PAGE, PAIR), jnp.bfloat16)],
            compiler_params=params,
            cost_estimate=cost(2560),
            name="near_window_and_prefix",
        )(meta, page_table.reshape(PAGES), near, near_side, ids, qt, *now))

    now = lax.cond(branch_ids[0] >= 0, near_part, lambda operands: list(operands[2]), (near, qt, now))
    far, now = lax.optimization_barrier((far, now))
    far = far.reshape(NY * ROWS, PAIR)
    far_side = lax.ppermute(far, "seq", SWAP)
    now = pl.pallas_call(
        far_kernel,
        out_shape=state,
        in_specs=[SM] + [VM] * 6,
        out_specs=[VM] * 3,
        compiler_params=params,
        cost_estimate=cost(1024),
        name="far_window",
    )(meta, far, ids, qt, *now)
    out = pl.pallas_call(
        last_kernel,
        out_shape=jax.ShapeDtypeStruct((ROWS, GROUP * D), jnp.bfloat16),
        in_specs=[SM] + [VM] * 6,
        out_specs=VM,
        scratch_shapes=[
            pltpu.VMEM((1, QR), jnp.float32),
            pltpu.VMEM((1, QR), jnp.float32),
            pltpu.VMEM((D, QR), jnp.float32),
        ],
        compiler_params=params,
        cost_estimate=cost(1024),
        name="far_other_core",
    )(meta, far_side, ids, qt, *now)
    out = lax.all_to_all(out.reshape(8, ROWS // 8, GROUP * D), "head", split_axis=0, concat_axis=0, tiled=True)
    return jnp.transpose(out, (1, 0, 2))


def solution(mesh):
    return jax.shard_map(
        per_device,
        mesh=mesh,
        in_specs=(
            P(("seq", "head"), None, None),
            P(("seq", "head"), None, None),
            P(),
            P("seq", None, "head", None),
            P("head", None),
        ),
        out_specs=P(("seq", "head"), None, None),
        check_vma=False,
    )
```

```python
import jax
import jax.numpy as jnp
from jax import lax
from jax.experimental import pallas as pl
from jax.experimental.pallas import tpu as pltpu
from jax.sharding import PartitionSpec as P

D = 128
PAIR = 2 * D
ROWS = 128
GROUP = 8
QR = ROWS * GROUP
NX, NY = 4, 8
PAGES = 32
PAGE = 16
BLOCKS = 4
TILE = 512
SCALE2 = D ** (-0.5) * 1.4426950408889634
LOW = -1e30
SLOT = ROWS + NX * PAGE
NEAR = 8


def x_ring(by):
    return [
        ((x * NY + y) * 2 + c, (((x + by) % NX) * NY + y) * 2 + c)
        for x in range(NX) for y in range(NY) for c in range(2)
    ]


SWAP = [(i, i ^ 1) for i in range(2 * NX * NY)]
Y_GROUPS = [[(x * NY + y) * 2 + c for y in range(NY)] for x in range(NX) for c in range(2)]


def fold(keys, values, mask, qt_ref, m_ref, l_ref, acc_ref):
    twice = jnp.concatenate([keys, keys], axis=1)
    lifted = jnp.concatenate([values.T, jnp.ones((16, keys.shape[0]), jnp.bfloat16)], axis=0)

    def scores_of(at):
        scores = jnp.dot(twice, qt_ref[:, at:at + TILE], preferred_element_type=jnp.float32)
        if mask is not None:
            scores = jnp.where(jnp.concatenate([mask] * (TILE // ROWS), axis=1), scores, LOW)
        return scores

    coming = scores_of(0)
    for at in range(0, QR, TILE):
        cols = slice(at, at + TILE)
        scores = coming
        if at + TILE < QR:
            coming = scores_of(at + TILE)
        old = m_ref[:, cols]
        top = jnp.maximum(old, jnp.max(scores, axis=0, keepdims=True))
        weights = jnp.exp2(scores - top).astype(jnp.bfloat16)
        factor = jnp.exp2(old - top)
        m_ref[:, cols] = top
        mixed = jnp.dot(lifted, weights, preferred_element_type=jnp.float32)
        l_ref[:, cols] = l_ref[:, cols] * factor + mixed[D:D + 1]
        acc_ref[:, cols] = acc_ref[:, cols] * factor + mixed[:D]


def starts_of(ids_ref, own):
    ids = ids_ref[...]
    starts = [jnp.sum((ids < b).astype(jnp.int32)) for b in range(1, 4)]
    own_ids = ids_ref[pl.ds(own, 1), :]
    row_start = jnp.zeros_like(own_ids)
    for b in range(1, 4):
        row_start = jnp.where(own_ids == b, starts[b - 1], row_start)
    return row_start, jnp.min(row_start), jnp.max(row_start)


def mask_of(block, own, row_start):
    key_rows = lax.broadcasted_iota(jnp.int32, (ROWS, ROWS), 0) + block * ROWS
    query_rows = lax.broadcasted_iota(jnp.int32, (ROWS, ROWS), 1) + own * ROWS
    return (key_rows >= row_start) & (key_rows <= query_rows)


def own_kernel(meta_ref, mine_ref, side_ref, ids_ref, q_ref, qt_ref, m_ref, l_ref, acc_ref):
    own = meta_ref[0]
    row_start, first, last = starts_of(ids_ref, own)
    for g in range(GROUP):
        scaled = q_ref[:, g * D:(g + 1) * D].astype(jnp.float32) * SCALE2
        high = scaled.astype(jnp.bfloat16)
        low = (scaled - high.astype(jnp.float32)).astype(jnp.bfloat16)
        qt_ref[:D, g * ROWS:(g + 1) * ROWS] = high.T
        qt_ref[D:, g * ROWS:(g + 1) * ROWS] = low.T
    m_ref[...] = jnp.full_like(m_ref, LOW)
    l_ref[...] = jnp.zeros_like(l_ref)
    acc_ref[...] = jnp.zeros_like(acc_ref)
    state = (qt_ref, m_ref, l_ref, acc_ref)
    fold(mine_ref[:, :D], mine_ref[:, D:], mask_of(own, own, row_start), *state)

    @pl.when((own % 2 == 1) & (own * ROWS > first))
    def _():
        fold(side_ref[:, :D], side_ref[:, D:], mask_of(own - 1, own, row_start), *state)


def window(kv_ref, skip, slot, core, own, limits, qt_ref, m_ref, l_ref, acc_ref):
    row_start, first, last = limits
    chip = own // 2 - skip
    lowest = jnp.maximum((jnp.maximum(first // ROWS - core, -1) + 1) // 2, chip - NEAR)
    steps = jnp.maximum(chip - lowest + BLOCKS - 1, 0) // BLOCKS

    def step(i, carry):
        base = chip - BLOCKS * (i + 1)
        pairs = []
        for b in range(BLOCKS):
            start = (base + b + 4 * NY) % NY * slot
            pairs.append(kv_ref[pl.ds(pl.multiple_of(start, PAGE), ROWS), :])
        keys = jnp.concatenate([pair[:, :D] for pair in pairs], axis=0)
        values = jnp.concatenate([pair[:, D:] for pair in pairs], axis=0)
        whole = (2 * base + core) * ROWS >= last

        @pl.when(whole)
        def _():
            fold(keys, values, None, qt_ref, m_ref, l_ref, acc_ref)

        @pl.when(jnp.logical_not(whole))
        def _():
            mask = jnp.concatenate(
                [mask_of(2 * (base + b) + core, own, row_start) for b in range(BLOCKS)], axis=0
            )
            fold(keys, values, mask, qt_ref, m_ref, l_ref, acc_ref)

        return carry

    lax.fori_loop(0, steps, step, 0)


def near_kernel(meta_ref, kv_ref, ids_ref, qt_ref, m_in, l_in, acc_in, m_ref, l_ref, acc_ref):
    m_ref[...] = m_in[...]
    l_ref[...] = l_in[...]
    acc_ref[...] = acc_in[...]
    own = meta_ref[0]
    window(kv_ref, 0, SLOT, own % 2, own, starts_of(ids_ref, own), qt_ref, m_ref, l_ref, acc_ref)


def near_side_kernel(meta_ref, table_ref, kv_ref, side_ref, ids_ref, qt_ref, m_in, l_in, acc_in,
                     m_ref, l_ref, acc_ref, prefix_ref):
    m_ref[...] = m_in[...]
    l_ref[...] = l_in[...]
    acc_ref[...] = acc_in[...]
    own = meta_ref[0]
    core, x = own % 2, own // (2 * NY)
    for i in range(PAGES):
        page = table_ref[i]
        start = (page // 2) % NY * SLOT + ROWS + (x + NX - page // (2 * NY)) % NX * PAGE
        rows = pl.ds(pl.multiple_of(start, PAGE), PAGE)
        prefix_ref[i * PAGE:(i + 1) * PAGE, :] = jnp.where(page % 2 == core, kv_ref[rows, :], side_ref[rows, :])

    fold(prefix_ref[:, :D], prefix_ref[:, D:], None, qt_ref, m_ref, l_ref, acc_ref)
    window(side_ref, 0, SLOT, 1 - core, own, starts_of(ids_ref, own), qt_ref, m_ref, l_ref, acc_ref)


def far_kernel(meta_ref, kv_ref, ids_ref, qt_ref, m_in, l_in, acc_in, m_ref, l_ref, acc_ref):
    m_ref[...] = m_in[...]
    l_ref[...] = l_in[...]
    acc_ref[...] = acc_in[...]
    own = meta_ref[0]
    window(kv_ref, NEAR, ROWS, own % 2, own, starts_of(ids_ref, own), qt_ref, m_ref, l_ref, acc_ref)


def last_kernel(meta_ref, kv_ref, ids_ref, qt_ref, m_in, l_in, acc_in, out_ref, m_ref, l_ref, acc_ref):
    m_ref[...] = m_in[...]
    l_ref[...] = l_in[...]
    acc_ref[...] = acc_in[...]
    own = meta_ref[0]
    window(kv_ref, NEAR, ROWS, 1 - own % 2, own, starts_of(ids_ref, own), qt_ref, m_ref, l_ref, acc_ref)
    result = (acc_ref[...] * (1.0 / l_ref[...])).astype(jnp.bfloat16)
    for g in range(GROUP):
        out_ref[:, g * D:(g + 1) * D] = result[:, g * ROWS:(g + 1) * ROWS].T


VM = pl.BlockSpec(memory_space=pltpu.VMEM)
SM = pl.BlockSpec(memory_space=pltpu.SMEM)


def cost(keys):
    return pl.CostEstimate(flops=4 * D * QR * keys, bytes_accessed=1 << 20, transcendentals=QR * keys)


def per_device(queries, branch_key_value, branch_ids, pool, page_table):
    me = lax.axis_index("seq")
    y = (me // 2) % NY
    page = pool.reshape(1, PAGE, PAIR)
    raw = jnp.concatenate([jnp.transpose(branch_key_value, (1, 0, 2)), page], axis=0)
    one_raw = lax.ppermute(raw, "seq", x_ring(1))
    wide = jnp.concatenate([jnp.transpose(queries, (1, 0, 2)), raw[:8], one_raw[:8]], axis=2)
    wide = lax.all_to_all(wide, "head", split_axis=0, concat_axis=0, tiled=True).reshape(ROWS, -1)
    own, before = wide[:, GROUP * D:GROUP * D + PAIR], wide[:, GROUP * D + PAIR:]
    two_page = lax.ppermute(page, "seq", x_ring(2))
    three_page = lax.ppermute(page, "seq", x_ring(3))
    target = jnp.arange(NY, dtype=jnp.int32)[:, None, None]
    block = jnp.where(target > y, own[None], before[None])
    pages = jnp.concatenate([page, one_raw[8:], two_page, three_page], axis=0).reshape(1, NX * PAGE, PAIR)
    send = jnp.concatenate([block, jnp.broadcast_to(pages, (NY, NX * PAGE, PAIR))], axis=1)
    near = lax.all_to_all(send, "seq", split_axis=0, concat_axis=0, tiled=True, axis_index_groups=Y_GROUPS)
    later, _ = lax.optimization_barrier((own, send))
    side = lax.ppermute(later, "seq", SWAP)
    ids = branch_ids.reshape(2 * NX * NY, ROWS)
    meta = me.astype(jnp.int32).reshape(1)
    state = [
        jax.ShapeDtypeStruct((1, QR), jnp.float32),
        jax.ShapeDtypeStruct((1, QR), jnp.float32),
        jax.ShapeDtypeStruct((D, QR), jnp.float32),
    ]
    params = pltpu.CompilerParams(vmem_limit_bytes=40 * 1024 * 1024)
    qt, *now = pl.pallas_call(
        own_kernel,
        out_shape=[jax.ShapeDtypeStruct((PAIR, QR), jnp.bfloat16)] + state,
        in_specs=[SM] + [VM] * 4,
        out_specs=[VM] * 4,
        compiler_params=params,
        cost_estimate=cost(256),
        name="own_chip",
    )(meta, own, side, ids, wide)
    near, qt, now = lax.optimization_barrier((near, qt, now))
    far = lax.ppermute(near[:, :ROWS], "seq", x_ring(1))

    def near_part(operands):
        near, qt, now = operands
        near = near.reshape(NY * SLOT, PAIR)
        near_side = lax.ppermute(near, "seq", SWAP)
        now = pl.pallas_call(
            near_kernel,
            out_shape=state,
            in_specs=[SM] + [VM] * 6,
            out_specs=[VM] * 3,
            compiler_params=params,
            cost_estimate=cost(1024),
            name="near_window",
        )(meta, near, ids, qt, *now)
        return list(pl.pallas_call(
            near_side_kernel,
            out_shape=state,
            in_specs=[SM, SM] + [VM] * 7,
            out_specs=[VM] * 3,
            scratch_shapes=[pltpu.VMEM((PAGES * PAGE, PAIR), jnp.bfloat16)],
            compiler_params=params,
            cost_estimate=cost(1536),
            name="near_other_core_and_prefix",
        )(meta, page_table.reshape(PAGES), near, near_side, ids, qt, *now))

    now = lax.cond(me < 2 * NX * NY, near_part, lambda operands: list(operands[2]), (near, qt, now))
    far, now = lax.optimization_barrier((far, now))
    far = far.reshape(NY * ROWS, PAIR)
    far_side = lax.ppermute(far, "seq", SWAP)
    now = pl.pallas_call(
        far_kernel,
        out_shape=state,
        in_specs=[SM] + [VM] * 6,
        out_specs=[VM] * 3,
        compiler_params=params,
        cost_estimate=cost(1024),
        name="far_window",
    )(meta, far, ids, qt, *now)
    out = pl.pallas_call(
        last_kernel,
        out_shape=jax.ShapeDtypeStruct((ROWS, GROUP * D), jnp.bfloat16),
        in_specs=[SM] + [VM] * 6,
        out_specs=VM,
        scratch_shapes=[
            pltpu.VMEM((1, QR), jnp.float32),
            pltpu.VMEM((1, QR), jnp.float32),
            pltpu.VMEM((D, QR), jnp.float32),
        ],
        compiler_params=params,
        cost_estimate=cost(1024),
        name="far_other_core",
    )(meta, far_side, ids, qt, *now)
    out = lax.all_to_all(out.reshape(8, ROWS // 8, GROUP * D), "head", split_axis=0, concat_axis=0, tiled=True)
    return jnp.transpose(out, (1, 0, 2))


def solution(mesh):
    return jax.shard_map(
        per_device,
        mesh=mesh,
        in_specs=(
            P(("seq", "head"), None, None),
            P(("seq", "head"), None, None),
            P(),
            P("seq", None, "head", None),
            P("head", None),
        ),
        out_specs=P(("seq", "head"), None, None),
        check_vma=False,
    )
```

```python
import jax
import jax.numpy as jnp
from jax import lax
from jax.experimental import pallas as pl
from jax.experimental.pallas import tpu as pltpu
from jax.sharding import PartitionSpec as P

D = 128
PAIR = 2 * D
ROWS = 128
GROUP = 8
QR = ROWS * GROUP
NX, NY = 4, 8
PAGES = 32
PAGE = 16
BLOCKS = 4
TILE = 512
SCALE2 = D ** (-0.5) * 1.4426950408889634
LOW = -1e30
SLOT = ROWS + NX * PAGE
NEAR = 8


def x_ring(by):
    return [
        ((x * NY + y) * 2 + c, (((x + by) % NX) * NY + y) * 2 + c)
        for x in range(NX) for y in range(NY) for c in range(2)
    ]


def x_next():
    return [pair for pair in x_ring(1) if pair[0] < pair[1]]


SWAP = [(i, i ^ 1) for i in range(2 * NX * NY)]
Y_GROUPS = [[(x * NY + y) * 2 + c for y in range(NY)] for x in range(NX) for c in range(2)]


def fold(keys, values, mask, qt_ref, m_ref, l_ref, acc_ref):
    twice = jnp.concatenate([keys, keys], axis=1)
    lifted = jnp.concatenate([values.T, jnp.ones((16, keys.shape[0]), jnp.bfloat16)], axis=0)

    def scores_of(at):
        scores = jnp.dot(twice, qt_ref[:, at:at + TILE], preferred_element_type=jnp.float32)
        if mask is not None:
            scores = jnp.where(jnp.concatenate([mask] * (TILE // ROWS), axis=1), scores, LOW)
        return scores

    coming = scores_of(0)
    for at in range(0, QR, TILE):
        cols = slice(at, at + TILE)
        scores = coming
        if at + TILE < QR:
            coming = scores_of(at + TILE)
        old = m_ref[:, cols]
        top = jnp.maximum(old, jnp.max(scores, axis=0, keepdims=True))
        weights = jnp.exp2(scores - top).astype(jnp.bfloat16)
        factor = jnp.exp2(old - top)
        m_ref[:, cols] = top
        mixed = jnp.dot(lifted, weights, preferred_element_type=jnp.float32)
        l_ref[:, cols] = l_ref[:, cols] * factor + mixed[D:D + 1]
        acc_ref[:, cols] = acc_ref[:, cols] * factor + mixed[:D]


def starts_of(ids_ref, own):
    ids = ids_ref[...]
    starts = [jnp.sum((ids < b).astype(jnp.int32)) for b in range(1, 4)]
    own_ids = ids_ref[pl.ds(own, 1), :]
    row_start = jnp.zeros_like(own_ids)
    for b in range(1, 4):
        row_start = jnp.where(own_ids == b, starts[b - 1], row_start)
    return row_start, jnp.min(row_start), jnp.max(row_start)


def mask_of(block, own, row_start):
    key_rows = lax.broadcasted_iota(jnp.int32, (ROWS, ROWS), 0) + block * ROWS
    query_rows = lax.broadcasted_iota(jnp.int32, (ROWS, ROWS), 1) + own * ROWS
    return (key_rows >= row_start) & (key_rows <= query_rows)


def own_kernel(meta_ref, mine_ref, side_ref, ids_ref, q_ref, qt_ref, start_ref, limit_ref, m_ref, l_ref, acc_ref):
    own = meta_ref[0]
    row_start, first, last = starts_of(ids_ref, own)
    start_ref[...] = row_start
    limit_ref[0] = first
    limit_ref[1] = last
    for g in range(GROUP):
        scaled = q_ref[:, g * D:(g + 1) * D].astype(jnp.float32) * SCALE2
        high = scaled.astype(jnp.bfloat16)
        low = (scaled - high.astype(jnp.float32)).astype(jnp.bfloat16)
        qt_ref[:D, g * ROWS:(g + 1) * ROWS] = high.T
        qt_ref[D:, g * ROWS:(g + 1) * ROWS] = low.T
    m_ref[...] = jnp.full_like(m_ref, LOW)
    l_ref[...] = jnp.zeros_like(l_ref)
    acc_ref[...] = jnp.zeros_like(acc_ref)
    state = (qt_ref, m_ref, l_ref, acc_ref)
    fold(mine_ref[:, :D], mine_ref[:, D:], mask_of(own, own, row_start), *state)

    @pl.when((own % 2 == 1) & (own * ROWS > first))
    def _():
        fold(side_ref[:, :D], side_ref[:, D:], mask_of(own - 1, own, row_start), *state)


def window(kv_ref, skip, slot, core, own, start_ref, limit_ref, qt_ref, m_ref, l_ref, acc_ref):
    first, last = limit_ref[0], limit_ref[1]
    chip = own // 2 - skip
    lowest = jnp.maximum((jnp.maximum(first // ROWS - core, -1) + 1) // 2, chip - NEAR)
    steps = jnp.maximum(chip - lowest + BLOCKS - 1, 0) // BLOCKS

    def step(i, carry):
        base = chip - BLOCKS * (i + 1)
        pairs = []
        for b in range(BLOCKS):
            start = (base + b + 4 * NY) % NY * slot
            pairs.append(kv_ref[pl.ds(pl.multiple_of(start, PAGE), ROWS), :])
        keys = jnp.concatenate([pair[:, :D] for pair in pairs], axis=0)
        values = jnp.concatenate([pair[:, D:] for pair in pairs], axis=0)
        whole = (2 * base + core) * ROWS >= last

        @pl.when(whole)
        def _():
            fold(keys, values, None, qt_ref, m_ref, l_ref, acc_ref)

        @pl.when(jnp.logical_not(whole))
        def _():
            mask = jnp.concatenate(
                [mask_of(2 * (base + b) + core, own, start_ref[...]) for b in range(BLOCKS)], axis=0
            )
            fold(keys, values, mask, qt_ref, m_ref, l_ref, acc_ref)

        return carry

    lax.fori_loop(0, steps, step, 0)


def near_kernel(meta_ref, kv_ref, start_ref, limit_ref, qt_ref, m_in, l_in, acc_in, m_ref, l_ref, acc_ref):
    m_ref[...] = m_in[...]
    l_ref[...] = l_in[...]
    acc_ref[...] = acc_in[...]
    own = meta_ref[0]
    window(kv_ref, 0, SLOT, own % 2, own, start_ref, limit_ref, qt_ref, m_ref, l_ref, acc_ref)


def near_side_kernel(meta_ref, table_ref, kv_ref, side_ref, start_ref, limit_ref, qt_ref, m_in, l_in, acc_in,
                     m_ref, l_ref, acc_ref, prefix_ref):
    m_ref[...] = m_in[...]
    l_ref[...] = l_in[...]
    acc_ref[...] = acc_in[...]
    own = meta_ref[0]
    core, x = own % 2, own // (2 * NY)
    for i in range(PAGES):
        page = table_ref[i]
        start = (page // 2) % NY * SLOT + ROWS + (x + NX - page // (2 * NY)) % NX * PAGE
        rows = pl.ds(pl.multiple_of(start, PAGE), PAGE)
        prefix_ref[i * PAGE:(i + 1) * PAGE, :] = jnp.where(page % 2 == core, kv_ref[rows, :], side_ref[rows, :])

    fold(prefix_ref[:, :D], prefix_ref[:, D:], None, qt_ref, m_ref, l_ref, acc_ref)
    window(side_ref, 0, SLOT, 1 - core, own, start_ref, limit_ref, qt_ref, m_ref, l_ref, acc_ref)


def far_kernel(meta_ref, kv_ref, start_ref, limit_ref, qt_ref, m_in, l_in, acc_in, m_ref, l_ref, acc_ref):
    m_ref[...] = m_in[...]
    l_ref[...] = l_in[...]
    acc_ref[...] = acc_in[...]
    own = meta_ref[0]
    window(kv_ref, NEAR, ROWS, own % 2, own, start_ref, limit_ref, qt_ref, m_ref, l_ref, acc_ref)


def last_kernel(meta_ref, kv_ref, start_ref, limit_ref, qt_ref, m_in, l_in, acc_in, out_ref, m_ref, l_ref, acc_ref):
    m_ref[...] = m_in[...]
    l_ref[...] = l_in[...]
    acc_ref[...] = acc_in[...]
    own = meta_ref[0]
    window(kv_ref, NEAR, ROWS, 1 - own % 2, own, start_ref, limit_ref, qt_ref, m_ref, l_ref, acc_ref)
    result = (acc_ref[...] * (1.0 / l_ref[...])).astype(jnp.bfloat16)
    for g in range(GROUP):
        out_ref[:, g * D:(g + 1) * D] = result[:, g * ROWS:(g + 1) * ROWS].T


VM = pl.BlockSpec(memory_space=pltpu.VMEM)
SM = pl.BlockSpec(memory_space=pltpu.SMEM)


def cost(keys):
    return pl.CostEstimate(flops=4 * D * QR * keys, bytes_accessed=1 << 20, transcendentals=QR * keys)


def per_device(queries, branch_key_value, branch_ids, pool, page_table):
    me = lax.axis_index("seq")
    y = (me // 2) % NY
    page = pool.reshape(1, PAGE, PAIR)
    raw = jnp.concatenate([jnp.transpose(branch_key_value, (1, 0, 2)), page], axis=0)
    one_raw = lax.ppermute(raw, "seq", x_ring(1))
    wide = jnp.concatenate([jnp.transpose(queries, (1, 0, 2)), raw[:8], one_raw[:8]], axis=2)
    wide = lax.all_to_all(wide, "head", split_axis=0, concat_axis=0, tiled=True).reshape(ROWS, -1)
    own, before = wide[:, GROUP * D:GROUP * D + PAIR], wide[:, GROUP * D + PAIR:]
    two_page = lax.ppermute(page, "seq", x_ring(2))
    three_page = lax.ppermute(page, "seq", x_ring(3))
    target = jnp.arange(NY, dtype=jnp.int32)[:, None, None]
    block = jnp.where(target > y, own[None], before[None])
    pages = jnp.concatenate([page, one_raw[8:], two_page, three_page], axis=0).reshape(1, NX * PAGE, PAIR)
    send = jnp.concatenate([block, jnp.broadcast_to(pages, (NY, NX * PAGE, PAIR))], axis=1)
    near = lax.all_to_all(send, "seq", split_axis=0, concat_axis=0, tiled=True, axis_index_groups=Y_GROUPS)
    later, _ = lax.optimization_barrier((own, send))
    side = lax.ppermute(later, "seq", SWAP)
    ids = branch_ids.reshape(2 * NX * NY, ROWS)
    meta = me.astype(jnp.int32).reshape(1)
    state = [
        jax.ShapeDtypeStruct((1, QR), jnp.float32),
        jax.ShapeDtypeStruct((1, QR), jnp.float32),
        jax.ShapeDtypeStruct((D, QR), jnp.float32),
    ]
    params = pltpu.CompilerParams(vmem_limit_bytes=40 * 1024 * 1024)
    qt, starts, limits, *now = pl.pallas_call(
        own_kernel,
        out_shape=[
            jax.ShapeDtypeStruct((PAIR, QR), jnp.bfloat16),
            jax.ShapeDtypeStruct((1, ROWS), jnp.int32),
            jax.ShapeDtypeStruct((2,), jnp.int32),
        ] + state,
        in_specs=[SM] + [VM] * 4,
        out_specs=[VM, VM, SM] + [VM] * 3,
        compiler_params=params,
        cost_estimate=cost(256),
        name="own_chip",
    )(meta, own, side, ids, wide)
    near, qt, now = lax.optimization_barrier((near, qt, now))
    far = lax.ppermute(near[:, :ROWS], "seq", x_next())

    def near_part(operands):
        near, qt, now = operands
        near = near.reshape(NY * SLOT, PAIR)
        near_side = lax.ppermute(near, "seq", SWAP)
        now = pl.pallas_call(
            near_kernel,
            out_shape=state,
            in_specs=[SM, VM, VM, SM] + [VM] * 4,
            out_specs=[VM] * 3,
            compiler_params=params,
            cost_estimate=cost(1024),
            name="near_window",
        )(meta, near, starts, limits, qt, *now)
        return list(pl.pallas_call(
            near_side_kernel,
            out_shape=state,
            in_specs=[SM, SM, VM, VM, VM, SM] + [VM] * 4,
            out_specs=[VM] * 3,
            scratch_shapes=[pltpu.VMEM((PAGES * PAGE, PAIR), jnp.bfloat16)],
            compiler_params=params,
            cost_estimate=cost(1536),
            name="near_other_core_and_prefix",
        )(meta, page_table.reshape(PAGES), near, near_side, starts, limits, qt, *now))

    now = lax.cond(me < 2 * NX * NY, near_part, lambda operands: list(operands[2]), (near, qt, now))
    far, now = lax.optimization_barrier((far, now))
    far = far.reshape(NY * ROWS, PAIR)
    far_side = lax.ppermute(far, "seq", SWAP)
    now = pl.pallas_call(
        far_kernel,
        out_shape=state,
        in_specs=[SM, VM, VM, SM] + [VM] * 4,
        out_specs=[VM] * 3,
        compiler_params=params,
        cost_estimate=cost(1024),
        name="far_window",
    )(meta, far, starts, limits, qt, *now)
    out = pl.pallas_call(
        last_kernel,
        out_shape=jax.ShapeDtypeStruct((ROWS, GROUP * D), jnp.bfloat16),
        in_specs=[SM, VM, VM, SM] + [VM] * 4,
        out_specs=VM,
        scratch_shapes=[
            pltpu.VMEM((1, QR), jnp.float32),
            pltpu.VMEM((1, QR), jnp.float32),
            pltpu.VMEM((D, QR), jnp.float32),
        ],
        compiler_params=params,
        cost_estimate=cost(1024),
        name="far_other_core",
    )(meta, far_side, starts, limits, qt, *now)
    out = lax.all_to_all(out.reshape(8, ROWS // 8, GROUP * D), "head", split_axis=0, concat_axis=0, tiled=True)
    return jnp.transpose(out, (1, 0, 2))


def solution(mesh):
    return jax.shard_map(
        per_device,
        mesh=mesh,
        in_specs=(
            P(("seq", "head"), None, None),
            P(("seq", "head"), None, None),
            P(),
            P("seq", None, "head", None),
            P("head", None),
        ),
        out_specs=P(("seq", "head"), None, None),
        check_vma=False,
    )
```

```python
import jax
import jax.numpy as jnp
from jax import lax
from jax.experimental import pallas as pl
from jax.experimental.pallas import tpu as pltpu
from jax.sharding import PartitionSpec as P

D = 128
PAIR = 2 * D
ROWS = 128
GROUP = 8
QR = ROWS * GROUP
NX, NY = 4, 8
PAGES = 32
PAGE = 16
BLOCKS = 4
TILE = 512
SCALE2 = D ** (-0.5) * 1.4426950408889634
LOW = -1e30
SLOT = ROWS + PAGE
NEAR = 8


def x_ring(by):
    return [
        ((x * NY + y) * 2 + c, (((x + by) % NX) * NY + y) * 2 + c)
        for x in range(NX) for y in range(NY) for c in range(2)
    ]


def x_next():
    return [pair for pair in x_ring(1) if pair[0] < pair[1]]


SWAP = [(i, i ^ 1) for i in range(2 * NX * NY)]
Y_GROUPS = [[(x * NY + y) * 2 + c for y in range(NY)] for x in range(NX) for c in range(2)]


def fold(keys, values, mask, qt_ref, m_ref, l_ref, acc_ref):
    twice = jnp.concatenate([keys, keys], axis=1)
    lifted = jnp.concatenate([values.T, jnp.ones((16, keys.shape[0]), jnp.bfloat16)], axis=0)

    def scores_of(at):
        scores = jnp.dot(twice, qt_ref[:, at:at + TILE], preferred_element_type=jnp.float32)
        if mask is not None:
            scores = jnp.where(jnp.concatenate([mask] * (TILE // ROWS), axis=1), scores, LOW)
        return scores

    coming = scores_of(0)
    for at in range(0, QR, TILE):
        cols = slice(at, at + TILE)
        scores = coming
        if at + TILE < QR:
            coming = scores_of(at + TILE)
        old = m_ref[:, cols]
        top = jnp.maximum(old, jnp.max(scores, axis=0, keepdims=True))
        weights = jnp.exp2(scores - top).astype(jnp.bfloat16)
        factor = jnp.exp2(old - top)
        m_ref[:, cols] = top
        mixed = jnp.dot(lifted, weights, preferred_element_type=jnp.float32)
        l_ref[:, cols] = l_ref[:, cols] * factor + mixed[D:D + 1]
        acc_ref[:, cols] = acc_ref[:, cols] * factor + mixed[:D]


def starts_of(ids_ref, own):
    ids = ids_ref[...]
    starts = [jnp.sum((ids < b).astype(jnp.int32)) for b in range(1, 4)]
    own_ids = ids_ref[pl.ds(own, 1), :]
    row_start = jnp.zeros_like(own_ids)
    for b in range(1, 4):
        row_start = jnp.where(own_ids == b, starts[b - 1], row_start)
    return row_start, jnp.min(row_start), jnp.max(row_start)


def mask_of(block, own, row_start):
    key_rows = lax.broadcasted_iota(jnp.int32, (ROWS, ROWS), 0) + block * ROWS
    query_rows = lax.broadcasted_iota(jnp.int32, (ROWS, ROWS), 1) + own * ROWS
    return (key_rows >= row_start) & (key_rows <= query_rows)


def own_kernel(meta_ref, mine_ref, side_ref, ids_ref, q_ref, qt_ref, m_ref, l_ref, acc_ref):
    own = meta_ref[0]
    row_start, first, last = starts_of(ids_ref, own)
    for g in range(GROUP):
        scaled = q_ref[:, g * D:(g + 1) * D].astype(jnp.float32) * SCALE2
        high = scaled.astype(jnp.bfloat16)
        low = (scaled - high.astype(jnp.float32)).astype(jnp.bfloat16)
        qt_ref[:D, g * ROWS:(g + 1) * ROWS] = high.T
        qt_ref[D:, g * ROWS:(g + 1) * ROWS] = low.T
    m_ref[...] = jnp.full_like(m_ref, LOW)
    l_ref[...] = jnp.zeros_like(l_ref)
    acc_ref[...] = jnp.zeros_like(acc_ref)
    state = (qt_ref, m_ref, l_ref, acc_ref)
    fold(mine_ref[:, :D], mine_ref[:, D:], mask_of(own, own, row_start), *state)

    @pl.when((own % 2 == 1) & (own * ROWS > first))
    def _():
        fold(side_ref[:, :D], side_ref[:, D:], mask_of(own - 1, own, row_start), *state)


def window(kv_ref, skip, slot, core, own, limits, qt_ref, m_ref, l_ref, acc_ref):
    row_start, first, last = limits
    chip = own // 2 - skip
    lowest = jnp.maximum((jnp.maximum(first // ROWS - core, -1) + 1) // 2, chip - NEAR)
    steps = jnp.maximum(chip - lowest + BLOCKS - 1, 0) // BLOCKS

    def step(i, carry):
        base = chip - BLOCKS * (i + 1)
        pairs = []
        for b in range(BLOCKS):
            start = (base + b + 4 * NY) % NY * slot
            pairs.append(kv_ref[pl.ds(pl.multiple_of(start, PAGE), ROWS), :])
        keys = jnp.concatenate([pair[:, :D] for pair in pairs], axis=0)
        values = jnp.concatenate([pair[:, D:] for pair in pairs], axis=0)
        whole = (2 * base + core) * ROWS >= last

        @pl.when(whole)
        def _():
            fold(keys, values, None, qt_ref, m_ref, l_ref, acc_ref)

        @pl.when(jnp.logical_not(whole))
        def _():
            mask = jnp.concatenate(
                [mask_of(2 * (base + b) + core, own, row_start) for b in range(BLOCKS)], axis=0
            )
            fold(keys, values, mask, qt_ref, m_ref, l_ref, acc_ref)

        return carry

    lax.fori_loop(0, steps, step, 0)


def near_kernel(meta_ref, kv_ref, ids_ref, qt_ref, m_in, l_in, acc_in, m_ref, l_ref, acc_ref):
    m_ref[...] = m_in[...]
    l_ref[...] = l_in[...]
    acc_ref[...] = acc_in[...]
    own = meta_ref[0]
    window(kv_ref, 0, SLOT, own % 2, own, starts_of(ids_ref, own), qt_ref, m_ref, l_ref, acc_ref)


def near_side_kernel(meta_ref, kv_ref, ids_ref, qt_ref, m_in, l_in, acc_in, m_ref, l_ref, acc_ref):
    m_ref[...] = m_in[...]
    l_ref[...] = l_in[...]
    acc_ref[...] = acc_in[...]
    own = meta_ref[0]
    window(kv_ref, 0, SLOT, 1 - own % 2, own, starts_of(ids_ref, own), qt_ref, m_ref, l_ref, acc_ref)


def far_kernel(meta_ref, kv_ref, ids_ref, qt_ref, m_in, l_in, acc_in, m_ref, l_ref, acc_ref):
    m_ref[...] = m_in[...]
    l_ref[...] = l_in[...]
    acc_ref[...] = acc_in[...]
    own = meta_ref[0]
    window(kv_ref, NEAR, SLOT, own % 2, own, starts_of(ids_ref, own), qt_ref, m_ref, l_ref, acc_ref)


def last_kernel(meta_ref, table_ref, near_ref, near_side_ref, far_ref, far_side_ref, two_ref, three_ref, ids_ref,
                qt_ref, m_in, l_in, acc_in, out_ref, m_ref, l_ref, acc_ref, prefix_ref):
    m_ref[...] = m_in[...]
    l_ref[...] = l_in[...]
    acc_ref[...] = acc_in[...]
    own = meta_ref[0]
    core, x = own % 2, own // (2 * NY)
    for i in range(PAGES):
        page = table_ref[i]
        yy = (page // 2) % NY
        back = (x + NX - page // (2 * NY)) % NX
        mine = page % 2 == core
        in_slot = pl.ds(pl.multiple_of(yy * SLOT + ROWS, PAGE), PAGE)
        in_page = pl.ds(pl.multiple_of((jnp.where(mine, 0, NY) + yy) * PAGE, PAGE), PAGE)
        prefix_ref[i * PAGE:(i + 1) * PAGE, :] = jnp.where(
            back < 2,
            jnp.where(
                back == 0,
                jnp.where(mine, near_ref[in_slot, :], near_side_ref[in_slot, :]),
                jnp.where(mine, far_ref[in_slot, :], far_side_ref[in_slot, :]),
            ),
            jnp.where(back == 2, two_ref[in_page, :], three_ref[in_page, :]),
        )

    fold(prefix_ref[:, :D], prefix_ref[:, D:], None, qt_ref, m_ref, l_ref, acc_ref)
    window(far_side_ref, NEAR, SLOT, 1 - core, own, starts_of(ids_ref, own), qt_ref, m_ref, l_ref, acc_ref)
    result = (acc_ref[...] * (1.0 / l_ref[...])).astype(jnp.bfloat16)
    for g in range(GROUP):
        out_ref[:, g * D:(g + 1) * D] = result[:, g * ROWS:(g + 1) * ROWS].T


VM = pl.BlockSpec(memory_space=pltpu.VMEM)
SM = pl.BlockSpec(memory_space=pltpu.SMEM)


def cost(keys):
    return pl.CostEstimate(flops=4 * D * QR * keys, bytes_accessed=1 << 20, transcendentals=QR * keys)


def per_device(queries, branch_key_value, branch_ids, pool, page_table):
    me = lax.axis_index("seq")
    y = (me // 2) % NY
    page = pool.reshape(PAGE, PAIR)
    wide = jnp.transpose(jnp.concatenate([queries, branch_key_value], axis=2), (1, 0, 2))
    wide = lax.all_to_all(wide, "head", split_axis=0, concat_axis=0, tiled=True).reshape(ROWS, -1)
    own = wide[:, GROUP * D:]
    before = lax.ppermute(own, "seq", x_next())
    target = jnp.arange(NY, dtype=jnp.int32)[:, None, None]
    block = jnp.where(target > y, own[None], before[None])
    send = jnp.concatenate([block, jnp.broadcast_to(page[None], (NY, PAGE, PAIR))], axis=1)
    near = lax.all_to_all(send, "seq", split_axis=0, concat_axis=0, tiled=True, axis_index_groups=Y_GROUPS)
    later, _ = lax.optimization_barrier((own, send))
    side = lax.ppermute(later, "seq", SWAP)

    ids = branch_ids.reshape(2 * NX * NY, ROWS)
    meta = me.astype(jnp.int32).reshape(1)
    state = [
        jax.ShapeDtypeStruct((1, QR), jnp.float32),
        jax.ShapeDtypeStruct((1, QR), jnp.float32),
        jax.ShapeDtypeStruct((D, QR), jnp.float32),
    ]
    params = pltpu.CompilerParams(vmem_limit_bytes=40 * 1024 * 1024)
    qt, *now = pl.pallas_call(
        own_kernel,
        out_shape=[jax.ShapeDtypeStruct((PAIR, QR), jnp.bfloat16)] + state,
        in_specs=[SM] + [VM] * 4,
        out_specs=[VM] * 4,
        compiler_params=params,
        cost_estimate=cost(256),
        name="own_chip",
    )(meta, own, side, ids, wide)
    near, qt, now = lax.optimization_barrier((near, qt, now))
    near = near.reshape(NY * SLOT, PAIR)
    far = lax.ppermute(near, "seq", x_ring(1))

    def near_part(operands):
        near, qt, now = operands
        near_side = lax.ppermute(near, "seq", SWAP)
        for kernel, kv in ((near_kernel, near), (near_side_kernel, near_side)):
            now = pl.pallas_call(
                kernel,
                out_shape=state,
                in_specs=[SM] + [VM] * 6,
                out_specs=[VM] * 3,
                compiler_params=params,
                cost_estimate=cost(1024),
                name=kernel.__name__,
            )(meta, kv, ids, qt, *now)
        return near_side, list(now)

    near_side, now = lax.cond(
        me < 2 * NX * NY, near_part, lambda operands: (operands[0], list(operands[2])), (near, qt, now)
    )
    pages = jnp.concatenate([a.reshape(NY, SLOT, PAIR)[:, ROWS:] for a in (near, near_side)], axis=0)
    pages = pages.reshape(2 * NY * PAGE, PAIR)
    two_pages = lax.ppermute(pages, "seq", x_ring(2))
    three_pages = lax.ppermute(pages, "seq", x_ring(3))
    far, now = lax.optimization_barrier((far, now))
    far_side = lax.ppermute(far, "seq", SWAP)
    now = pl.pallas_call(
        far_kernel,
        out_shape=state,
        in_specs=[SM] + [VM] * 6,
        out_specs=[VM] * 3,
        compiler_params=params,
        cost_estimate=cost(1024),
        name="far_window",
    )(meta, far, ids, qt, *now)
    out = pl.pallas_call(
        last_kernel,
        out_shape=jax.ShapeDtypeStruct((ROWS, GROUP * D), jnp.bfloat16),
        in_specs=[SM, SM] + [VM] * 11,
        out_specs=VM,
        scratch_shapes=[
            pltpu.VMEM((1, QR), jnp.float32),
            pltpu.VMEM((1, QR), jnp.float32),
            pltpu.VMEM((D, QR), jnp.float32),
            pltpu.VMEM((PAGES * PAGE, PAIR), jnp.bfloat16),
        ],
        compiler_params=params,
        cost_estimate=cost(1536),
        name="far_other_core_and_prefix",
    )(meta, page_table.reshape(PAGES), near, near_side, far, far_side, two_pages, three_pages, ids, qt, *now)
    out = lax.all_to_all(out.reshape(8, ROWS // 8, GROUP * D), "head", split_axis=0, concat_axis=0, tiled=True)
    return jnp.transpose(out, (1, 0, 2))


def solution(mesh):
    return jax.shard_map(
        per_device,
        mesh=mesh,
        in_specs=(
            P(("seq", "head"), None, None),
            P(("seq", "head"), None, None),
            P(),
            P("seq", None, "head", None),
            P("head", None),
        ),
        out_specs=P(("seq", "head"), None, None),
        check_vma=False,
    )
```

```python
import jax
import jax.numpy as jnp
from jax import lax
from jax.experimental import pallas as pl
from jax.experimental.pallas import tpu as pltpu
from jax.sharding import PartitionSpec as P

D = 128
PAIR = 2 * D
ROWS = 128
GROUP = 8
QR = ROWS * GROUP
NX, NY = 4, 8
PAGES = 32
PAGE = 16
BLOCKS = 4
TILE = 512
SCALE2 = D ** (-0.5) * 1.4426950408889634
LOW = -1e30
SLOT = ROWS + NX * PAGE
NEAR = 8


def x_ring(by):
    return [
        ((x * NY + y) * 2 + c, (((x + by) % NX) * NY + y) * 2 + c)
        for x in range(NX) for y in range(NY) for c in range(2)
    ]


def x_next():
    return [pair for pair in x_ring(1) if pair[0] < pair[1]]


SWAP = [(i, i ^ 1) for i in range(2 * NX * NY)]
Y_GROUPS = [[(x * NY + y) * 2 + c for y in range(NY)] for x in range(NX) for c in range(2)]


def fold(keys, values, mask, qt_ref, m_ref, l_ref, acc_ref):
    twice = jnp.concatenate([keys, keys], axis=1)
    lifted = jnp.concatenate([values.T, jnp.ones((16, keys.shape[0]), jnp.bfloat16)], axis=0)

    def scores_of(at):
        scores = jnp.dot(twice, qt_ref[:, at:at + TILE], preferred_element_type=jnp.float32)
        if mask is not None:
            scores = jnp.where(jnp.concatenate([mask] * (TILE // ROWS), axis=1), scores, LOW)
        return scores

    coming = scores_of(0)
    for at in range(0, QR, TILE):
        cols = slice(at, at + TILE)
        scores = coming
        if at + TILE < QR:
            coming = scores_of(at + TILE)
        old = m_ref[:, cols]
        top = jnp.maximum(old, jnp.max(scores, axis=0, keepdims=True))
        weights = jnp.exp2(scores - top).astype(jnp.bfloat16)
        factor = jnp.exp2(old - top)
        m_ref[:, cols] = top
        mixed = jnp.dot(lifted, weights, preferred_element_type=jnp.float32)
        l_ref[:, cols] = l_ref[:, cols] * factor + mixed[D:D + 1]
        acc_ref[:, cols] = acc_ref[:, cols] * factor + mixed[:D]


def starts_of(ids_ref, own):
    ids = ids_ref[...]
    starts = [jnp.sum((ids < b).astype(jnp.int32)) for b in range(1, 4)]
    own_ids = ids_ref[pl.ds(own, 1), :]
    row_start = jnp.zeros_like(own_ids)
    for b in range(1, 4):
        row_start = jnp.where(own_ids == b, starts[b - 1], row_start)
    return row_start, jnp.min(row_start), jnp.max(row_start)


def mask_of(block, own, row_start):
    key_rows = lax.broadcasted_iota(jnp.int32, (ROWS, ROWS), 0) + block * ROWS
    query_rows = lax.broadcasted_iota(jnp.int32, (ROWS, ROWS), 1) + own * ROWS
    return (key_rows >= row_start) & (key_rows <= query_rows)


def own_kernel(meta_ref, mine_ref, side_ref, ids_ref, q_ref, qt_ref, m_ref, l_ref, acc_ref):
    own = meta_ref[0]
    row_start, first, last = starts_of(ids_ref, own)
    for g in range(GROUP):
        scaled = q_ref[:, g * D:(g + 1) * D].astype(jnp.float32) * SCALE2
        high = scaled.astype(jnp.bfloat16)
        low = (scaled - high.astype(jnp.float32)).astype(jnp.bfloat16)
        qt_ref[:D, g * ROWS:(g + 1) * ROWS] = high.T
        qt_ref[D:, g * ROWS:(g + 1) * ROWS] = low.T
    m_ref[...] = jnp.full_like(m_ref, LOW)
    l_ref[...] = jnp.zeros_like(l_ref)
    acc_ref[...] = jnp.zeros_like(acc_ref)
    state = (qt_ref, m_ref, l_ref, acc_ref)
    fold(mine_ref[:, :D], mine_ref[:, D:], mask_of(own, own, row_start), *state)

    @pl.when((own % 2 == 1) & (own * ROWS > first))
    def _():
        fold(side_ref[:, :D], side_ref[:, D:], mask_of(own - 1, own, row_start), *state)


def window(kv_ref, skip, slot, core, own, limits, qt_ref, m_ref, l_ref, acc_ref):
    row_start, first, last = limits
    chip = own // 2 - skip
    lowest = jnp.maximum((jnp.maximum(first // ROWS - core, -1) + 1) // 2, chip - NEAR)
    steps = jnp.maximum(chip - lowest + BLOCKS - 1, 0) // BLOCKS

    def step(i, carry):
        base = chip - BLOCKS * (i + 1)
        pairs = []
        for b in range(BLOCKS):
            start = (base + b + 4 * NY) % NY * slot
            pairs.append(kv_ref[pl.ds(pl.multiple_of(start, PAGE), ROWS), :])
        keys = jnp.concatenate([pair[:, :D] for pair in pairs], axis=0)
        values = jnp.concatenate([pair[:, D:] for pair in pairs], axis=0)
        whole = (2 * base + core) * ROWS >= last

        @pl.when(whole)
        def _():
            fold(keys, values, None, qt_ref, m_ref, l_ref, acc_ref)

        @pl.when(jnp.logical_not(whole))
        def _():
            mask = jnp.concatenate(
                [mask_of(2 * (base + b) + core, own, row_start) for b in range(BLOCKS)], axis=0
            )
            fold(keys, values, mask, qt_ref, m_ref, l_ref, acc_ref)

        return carry

    lax.fori_loop(0, steps, step, 0)


def near_kernel(meta_ref, kv_ref, ids_ref, qt_ref, m_in, l_in, acc_in, m_ref, l_ref, acc_ref):
    m_ref[...] = m_in[...]
    l_ref[...] = l_in[...]
    acc_ref[...] = acc_in[...]
    own = meta_ref[0]
    window(kv_ref, 0, SLOT, own % 2, own, starts_of(ids_ref, own), qt_ref, m_ref, l_ref, acc_ref)


def near_side_kernel(meta_ref, table_ref, kv_ref, side_ref, ids_ref, qt_ref, m_in, l_in, acc_in,
                     m_ref, l_ref, acc_ref, prefix_ref):
    m_ref[...] = m_in[...]
    l_ref[...] = l_in[...]
    acc_ref[...] = acc_in[...]
    own = meta_ref[0]
    core, x = own % 2, own // (2 * NY)
    for i in range(PAGES):
        page = table_ref[i]
        start = (page // 2) % NY * SLOT + ROWS + (x + NX - page // (2 * NY)) % NX * PAGE
        rows = pl.ds(pl.multiple_of(start, PAGE), PAGE)
        prefix_ref[i * PAGE:(i + 1) * PAGE, :] = jnp.where(page % 2 == core, kv_ref[rows, :], side_ref[rows, :])

    fold(prefix_ref[:, :D], prefix_ref[:, D:], None, qt_ref, m_ref, l_ref, acc_ref)
    window(side_ref, 0, SLOT, 1 - core, own, starts_of(ids_ref, own), qt_ref, m_ref, l_ref, acc_ref)


def far_kernel(meta_ref, kv_ref, ids_ref, qt_ref, m_in, l_in, acc_in, m_ref, l_ref, acc_ref):
    m_ref[...] = m_in[...]
    l_ref[...] = l_in[...]
    acc_ref[...] = acc_in[...]
    own = meta_ref[0]
    window(kv_ref, NEAR, ROWS, own % 2, own, starts_of(ids_ref, own), qt_ref, m_ref, l_ref, acc_ref)


def last_kernel(meta_ref, kv_ref, ids_ref, qt_ref, m_in, l_in, acc_in, out_ref, m_ref, l_ref, acc_ref):
    m_ref[...] = m_in[...]
    l_ref[...] = l_in[...]
    acc_ref[...] = acc_in[...]
    own = meta_ref[0]
    window(kv_ref, NEAR, ROWS, 1 - own % 2, own, starts_of(ids_ref, own), qt_ref, m_ref, l_ref, acc_ref)
    result = (acc_ref[...] * (1.0 / l_ref[...])).astype(jnp.bfloat16)
    for g in range(GROUP):
        out_ref[:, g * D:(g + 1) * D] = result[:, g * ROWS:(g + 1) * ROWS].T


VM = pl.BlockSpec(memory_space=pltpu.VMEM)
SM = pl.BlockSpec(memory_space=pltpu.SMEM)


def cost(keys):
    return pl.CostEstimate(flops=4 * D * QR * keys, bytes_accessed=1 << 20, transcendentals=QR * keys)


def per_device(queries, branch_key_value, branch_ids, pool, page_table):
    me = lax.axis_index("seq")
    y = (me // 2) % NY
    page = pool.reshape(1, PAGE, PAIR)
    raw = jnp.concatenate([jnp.transpose(branch_key_value, (1, 0, 2)), page], axis=0)
    one_raw = lax.ppermute(raw, "seq", x_ring(1))
    three_page = lax.ppermute(page, "seq", x_ring(3))
    one_raw, three_page = lax.optimization_barrier((one_raw, three_page))
    wide = jnp.concatenate([jnp.transpose(queries, (1, 0, 2)), raw[:8], one_raw[:8]], axis=2)
    wide = lax.all_to_all(wide, "head", split_axis=0, concat_axis=0, tiled=True).reshape(ROWS, -1)
    own, before = wide[:, GROUP * D:GROUP * D + PAIR], wide[:, GROUP * D + PAIR:]
    two_page = lax.ppermute(page, "seq", x_ring(2))
    target = jnp.arange(NY, dtype=jnp.int32)[:, None, None]
    block = jnp.where(target > y, own[None], before[None])
    pages = jnp.concatenate([page, one_raw[8:], two_page, three_page], axis=0).reshape(1, NX * PAGE, PAIR)
    send = jnp.concatenate([block, jnp.broadcast_to(pages, (NY, NX * PAGE, PAIR))], axis=1)
    near = lax.all_to_all(send, "seq", split_axis=0, concat_axis=0, tiled=True, axis_index_groups=Y_GROUPS)
    later, _ = lax.optimization_barrier((own, send))
    side = lax.ppermute(later, "seq", SWAP)
    ids = branch_ids.reshape(2 * NX * NY, ROWS)
    meta = me.astype(jnp.int32).reshape(1)
    state = [
        jax.ShapeDtypeStruct((1, QR), jnp.float32),
        jax.ShapeDtypeStruct((1, QR), jnp.float32),
        jax.ShapeDtypeStruct((D, QR), jnp.float32),
    ]
    params = pltpu.CompilerParams(vmem_limit_bytes=40 * 1024 * 1024)
    qt, *now = pl.pallas_call(
        own_kernel,
        out_shape=[jax.ShapeDtypeStruct((PAIR, QR), jnp.bfloat16)] + state,
        in_specs=[SM] + [VM] * 4,
        out_specs=[VM] * 4,
        compiler_params=params,
        cost_estimate=cost(256),
        name="own_chip",
    )(meta, own, side, ids, wide)
    near, qt, now = lax.optimization_barrier((near, qt, now))
    far = lax.ppermute(near[:, :ROWS], "seq", x_next())

    def near_part(operands):
        near, qt, now = operands
        near = near.reshape(NY * SLOT, PAIR)
        near_side = lax.ppermute(near, "seq", SWAP)
        now = pl.pallas_call(
            near_kernel,
            out_shape=state,
            in_specs=[SM] + [VM] * 6,
            out_specs=[VM] * 3,
            compiler_params=params,
            cost_estimate=cost(1024),
            name="near_window",
        )(meta, near, ids, qt, *now)
        return list(pl.pallas_call(
            near_side_kernel,
            out_shape=state,
            in_specs=[SM, SM] + [VM] * 7,
            out_specs=[VM] * 3,
            scratch_shapes=[pltpu.VMEM((PAGES * PAGE, PAIR), jnp.bfloat16)],
            compiler_params=params,
            cost_estimate=cost(1536),
            name="near_other_core_and_prefix",
        )(meta, page_table.reshape(PAGES), near, near_side, ids, qt, *now))

    now = lax.cond(me < 2 * NX * NY, near_part, lambda operands: list(operands[2]), (near, qt, now))
    far, now = lax.optimization_barrier((far, now))
    far = far.reshape(NY * ROWS, PAIR)
    far_side = lax.ppermute(far, "seq", SWAP)
    now = pl.pallas_call(
        far_kernel,
        out_shape=state,
        in_specs=[SM] + [VM] * 6,
        out_specs=[VM] * 3,
        compiler_params=params,
        cost_estimate=cost(1024),
        name="far_window",
    )(meta, far, ids, qt, *now)
    out = pl.pallas_call(
        last_kernel,
        out_shape=jax.ShapeDtypeStruct((ROWS, GROUP * D), jnp.bfloat16),
        in_specs=[SM] + [VM] * 6,
        out_specs=VM,
        scratch_shapes=[
            pltpu.VMEM((1, QR), jnp.float32),
            pltpu.VMEM((1, QR), jnp.float32),
            pltpu.VMEM((D, QR), jnp.float32),
        ],
        compiler_params=params,
        cost_estimate=cost(1024),
        name="far_other_core",
    )(meta, far_side, ids, qt, *now)
    out = lax.all_to_all(out.reshape(8, ROWS // 8, GROUP * D), "head", split_axis=0, concat_axis=0, tiled=True)
    return jnp.transpose(out, (1, 0, 2))


def solution(mesh):
    return jax.shard_map(
        per_device,
        mesh=mesh,
        in_specs=(
            P(("seq", "head"), None, None),
            P(("seq", "head"), None, None),
            P(),
            P("seq", None, "head", None),
            P("head", None),
        ),
        out_specs=P(("seq", "head"), None, None),
        check_vma=False,
    )
```

```python
import jax
import jax.numpy as jnp
from jax import lax
from jax.experimental import pallas as pl
from jax.experimental.pallas import tpu as pltpu
from jax.sharding import PartitionSpec as P

D = 128
PAIR = 2 * D
ROWS = 128
GROUP = 8
QR = ROWS * GROUP
NX, NY = 4, 8
PAGES = 32
PAGE = 16
BLOCKS = 4
TILE = 512
SCALE2 = D ** (-0.5) * 1.4426950408889634
LOW = -1e30
SLOT = ROWS + NX * PAGE
NEAR = 8


def x_ring(by):
    return [
        ((x * NY + y) * 2 + c, (((x + by) % NX) * NY + y) * 2 + c)
        for x in range(NX) for y in range(NY) for c in range(2)
    ]


def x_next():
    return [pair for pair in x_ring(1) if pair[0] < pair[1]]


SWAP = [(i, i ^ 1) for i in range(2 * NX * NY)]
Y_GROUPS = [[(x * NY + y) * 2 + c for y in range(NY)] for x in range(NX) for c in range(2)]


def fold(keys, values, mask, qt_ref, m_ref, l_ref, acc_ref):
    twice = jnp.concatenate([keys, keys], axis=1)
    lifted = jnp.concatenate([values.T, jnp.ones((16, keys.shape[0]), jnp.bfloat16)], axis=0)

    def scores_of(at):
        scores = jnp.dot(twice, qt_ref[:, at:at + TILE], preferred_element_type=jnp.float32)
        if mask is not None:
            scores = jnp.where(jnp.concatenate([mask] * (TILE // ROWS), axis=1), scores, LOW)
        return scores

    coming = scores_of(0)
    for at in range(0, QR, TILE):
        cols = slice(at, at + TILE)
        scores = coming
        if at + TILE < QR:
            coming = scores_of(at + TILE)
        old = m_ref[:, cols]
        top = jnp.maximum(old, jnp.max(scores, axis=0, keepdims=True))
        weights = jnp.exp2(scores - top).astype(jnp.bfloat16)
        factor = jnp.exp2(old - top)
        m_ref[:, cols] = top
        mixed = jnp.dot(lifted, weights, preferred_element_type=jnp.float32)
        l_ref[:, cols] = l_ref[:, cols] * factor + mixed[D:D + 1]
        acc_ref[:, cols] = acc_ref[:, cols] * factor + mixed[:D]


def starts_of(ids_ref, own):
    ids = ids_ref[...]
    starts = [jnp.sum((ids < b).astype(jnp.int32)) for b in range(1, 4)]
    own_ids = ids_ref[pl.ds(own, 1), :]
    row_start = jnp.zeros_like(own_ids)
    for b in range(1, 4):
        row_start = jnp.where(own_ids == b, starts[b - 1], row_start)
    return row_start, jnp.min(row_start), jnp.max(row_start)


def mask_of(block, own, row_start):
    key_rows = lax.broadcasted_iota(jnp.int32, (ROWS, ROWS), 0) + block * ROWS
    query_rows = lax.broadcasted_iota(jnp.int32, (ROWS, ROWS), 1) + own * ROWS
    return (key_rows >= row_start) & (key_rows <= query_rows)


def own_kernel(meta_ref, mine_ref, side_ref, ids_ref, q_ref, qt_ref, m_ref, l_ref, acc_ref):
    own = meta_ref[0]
    row_start, first, last = starts_of(ids_ref, own)
    for g in range(GROUP):
        scaled = q_ref[:, g * D:(g + 1) * D].astype(jnp.float32) * SCALE2
        high = scaled.astype(jnp.bfloat16)
        low = (scaled - high.astype(jnp.float32)).astype(jnp.bfloat16)
        qt_ref[:D, g * ROWS:(g + 1) * ROWS] = high.T
        qt_ref[D:, g * ROWS:(g + 1) * ROWS] = low.T
    m_ref[...] = jnp.full_like(m_ref, LOW)
    l_ref[...] = jnp.zeros_like(l_ref)
    acc_ref[...] = jnp.zeros_like(acc_ref)
    state = (qt_ref, m_ref, l_ref, acc_ref)
    fold(mine_ref[:, :D], mine_ref[:, D:], mask_of(own, own, row_start), *state)

    @pl.when((own % 2 == 1) & (own * ROWS > first))
    def _():
        fold(side_ref[:, :D], side_ref[:, D:], mask_of(own - 1, own, row_start), *state)


def window(kv_ref, skip, slot, core, own, limits, qt_ref, m_ref, l_ref, acc_ref):
    row_start, first, last = limits
    chip = own // 2 - skip
    lowest = jnp.maximum((jnp.maximum(first // ROWS - core, -1) + 1) // 2, chip - NEAR)
    steps = jnp.maximum(chip - lowest + BLOCKS - 1, 0) // BLOCKS

    def step(i, carry):
        base = chip - BLOCKS * (i + 1)
        pairs = []
        for b in range(BLOCKS):
            start = (base + b + 4 * NY) % NY * slot
            pairs.append(kv_ref[pl.ds(pl.multiple_of(start, PAGE), ROWS), :])
        keys = jnp.concatenate([pair[:, :D] for pair in pairs], axis=0)
        values = jnp.concatenate([pair[:, D:] for pair in pairs], axis=0)
        whole = (2 * base + core) * ROWS >= last

        @pl.when(whole)
        def _():
            fold(keys, values, None, qt_ref, m_ref, l_ref, acc_ref)

        @pl.when(jnp.logical_not(whole))
        def _():
            mask = jnp.concatenate(
                [mask_of(2 * (base + b) + core, own, row_start) for b in range(BLOCKS)], axis=0
            )
            fold(keys, values, mask, qt_ref, m_ref, l_ref, acc_ref)

        return carry

    lax.fori_loop(0, steps, step, 0)


def near_kernel(meta_ref, kv_ref, ids_ref, qt_ref, m_in, l_in, acc_in, m_ref, l_ref, acc_ref):
    m_ref[...] = m_in[...]
    l_ref[...] = l_in[...]
    acc_ref[...] = acc_in[...]
    own = meta_ref[0]
    window(kv_ref, 0, SLOT, own % 2, own, starts_of(ids_ref, own), qt_ref, m_ref, l_ref, acc_ref)


def near_side_kernel(meta_ref, table_ref, kv_ref, side_ref, ids_ref, qt_ref, m_in, l_in, acc_in,
                     m_ref, l_ref, acc_ref, prefix_ref):
    m_ref[...] = m_in[...]
    l_ref[...] = l_in[...]
    acc_ref[...] = acc_in[...]
    own = meta_ref[0]
    core, x = own % 2, own // (2 * NY)
    for i in range(PAGES):
        page = table_ref[i]
        start = (page // 2) % NY * SLOT + ROWS + (x + NX - page // (2 * NY)) % NX * PAGE
        rows = pl.ds(pl.multiple_of(start, PAGE), PAGE)
        prefix_ref[i * PAGE:(i + 1) * PAGE, :] = jnp.where(page % 2 == core, kv_ref[rows, :], side_ref[rows, :])

    fold(prefix_ref[:, :D], prefix_ref[:, D:], None, qt_ref, m_ref, l_ref, acc_ref)
    window(side_ref, 0, SLOT, 1 - core, own, starts_of(ids_ref, own), qt_ref, m_ref, l_ref, acc_ref)


def far_kernel(meta_ref, kv_ref, ids_ref, qt_ref, m_in, l_in, acc_in, m_ref, l_ref, acc_ref):
    m_ref[...] = m_in[...]
    l_ref[...] = l_in[...]
    acc_ref[...] = acc_in[...]
    own = meta_ref[0]
    window(kv_ref, NEAR, ROWS, own % 2, own, starts_of(ids_ref, own), qt_ref, m_ref, l_ref, acc_ref)


def last_kernel(meta_ref, kv_ref, ids_ref, qt_ref, m_in, l_in, acc_in, out_ref, m_ref, l_ref, acc_ref):
    m_ref[...] = m_in[...]
    l_ref[...] = l_in[...]
    acc_ref[...] = acc_in[...]
    own = meta_ref[0]
    window(kv_ref, NEAR, ROWS, 1 - own % 2, own, starts_of(ids_ref, own), qt_ref, m_ref, l_ref, acc_ref)
    result = (acc_ref[...] * (1.0 / l_ref[...])).astype(jnp.bfloat16)
    for g in range(GROUP):
        out_ref[:, g * D:(g + 1) * D] = result[:, g * ROWS:(g + 1) * ROWS].T


VM = pl.BlockSpec(memory_space=pltpu.VMEM)
SM = pl.BlockSpec(memory_space=pltpu.SMEM)


def cost(keys):
    return pl.CostEstimate(flops=4 * D * QR * keys, bytes_accessed=1 << 20, transcendentals=QR * keys)


def per_device(queries, branch_key_value, branch_ids, pool, page_table):
    me = lax.axis_index("seq")
    y = (me // 2) % NY
    page = pool.reshape(1, PAGE, PAIR)
    raw = jnp.concatenate([jnp.transpose(branch_key_value, (1, 0, 2)), page], axis=0)
    one_raw = lax.ppermute(raw, "seq", x_ring(1))
    three_page = lax.ppermute(page, "seq", x_ring(3))
    wide = jnp.concatenate([jnp.transpose(queries, (1, 0, 2)), raw[:8], one_raw[:8]], axis=2)
    wide = lax.all_to_all(wide, "head", split_axis=0, concat_axis=0, tiled=True).reshape(ROWS, -1)
    own, before = wide[:, GROUP * D:GROUP * D + PAIR], wide[:, GROUP * D + PAIR:]
    two_page = lax.ppermute(page, "seq", x_ring(2))
    target = jnp.arange(NY, dtype=jnp.int32)[:, None, None]
    block = jnp.where(target > y, own[None], before[None])
    pages = jnp.concatenate([page, one_raw[8:], two_page, three_page], axis=0).reshape(1, NX * PAGE, PAIR)
    send = jnp.concatenate([block, jnp.broadcast_to(pages, (NY, NX * PAGE, PAIR))], axis=1)
    near = lax.all_to_all(send, "seq", split_axis=0, concat_axis=0, tiled=True, axis_index_groups=Y_GROUPS)
    later, _ = lax.optimization_barrier((own, send))
    side = lax.ppermute(later, "seq", SWAP)
    ids = branch_ids.reshape(2 * NX * NY, ROWS)
    meta = me.astype(jnp.int32).reshape(1)
    state = [
        jax.ShapeDtypeStruct((1, QR), jnp.float32),
        jax.ShapeDtypeStruct((1, QR), jnp.float32),
        jax.ShapeDtypeStruct((D, QR), jnp.float32),
    ]
    params = pltpu.CompilerParams(vmem_limit_bytes=40 * 1024 * 1024)
    qt, *now = pl.pallas_call(
        own_kernel,
        out_shape=[jax.ShapeDtypeStruct((PAIR, QR), jnp.bfloat16)] + state,
        in_specs=[SM] + [VM] * 4,
        out_specs=[VM] * 4,
        compiler_params=params,
        cost_estimate=cost(256),
        name="own_chip",
    )(meta, own, side, ids, wide)
    near, qt, now = lax.optimization_barrier((near, qt, now))
    far = lax.ppermute(near[:, :ROWS], "seq", x_next())

    def near_part(operands):
        near, qt, now = operands
        near = near.reshape(NY * SLOT, PAIR)
        near_side = lax.ppermute(near, "seq", SWAP)
        now = pl.pallas_call(
            near_kernel,
            out_shape=state,
            in_specs=[SM] + [VM] * 6,
            out_specs=[VM] * 3,
            compiler_params=params,
            cost_estimate=cost(1024),
            name="near_window",
        )(meta, near, ids, qt, *now)
        return list(pl.pallas_call(
            near_side_kernel,
            out_shape=state,
            in_specs=[SM, SM] + [VM] * 7,
            out_specs=[VM] * 3,
            scratch_shapes=[pltpu.VMEM((PAGES * PAGE, PAIR), jnp.bfloat16)],
            compiler_params=params,
            cost_estimate=cost(1536),
            name="near_other_core_and_prefix",
        )(meta, page_table.reshape(PAGES), near, near_side, ids, qt, *now))

    now = lax.cond(me < 2 * NX * NY, near_part, lambda operands: list(operands[2]), (near, qt, now))
    far, now = lax.optimization_barrier((far, now))
    far = far.reshape(NY * ROWS, PAIR)
    far_side = lax.ppermute(far, "seq", SWAP)
    now = pl.pallas_call(
        far_kernel,
        out_shape=state,
        in_specs=[SM] + [VM] * 6,
        out_specs=[VM] * 3,
        compiler_params=params,
        cost_estimate=cost(1024),
        name="far_window",
    )(meta, far, ids, qt, *now)
    out = pl.pallas_call(
        last_kernel,
        out_shape=jax.ShapeDtypeStruct((ROWS, GROUP * D), jnp.bfloat16),
        in_specs=[SM] + [VM] * 6,
        out_specs=VM,
        scratch_shapes=[
            pltpu.VMEM((1, QR), jnp.float32),
            pltpu.VMEM((1, QR), jnp.float32),
            pltpu.VMEM((D, QR), jnp.float32),
        ],
        compiler_params=params,
        cost_estimate=cost(1024),
        name="far_other_core",
    )(meta, far_side, ids, qt, *now)
    out = lax.all_to_all(out.reshape(8, ROWS // 8, GROUP * D), "head", split_axis=0, concat_axis=0, tiled=True)
    return jnp.transpose(out, (1, 0, 2))


def solution(mesh):
    return jax.shard_map(
        per_device,
        mesh=mesh,
        in_specs=(
            P(("seq", "head"), None, None),
            P(("seq", "head"), None, None),
            P(),
            P("seq", None, "head", None),
            P("head", None),
        ),
        out_specs=P(("seq", "head"), None, None),
        check_vma=False,
    )
```

```python
import jax
import jax.numpy as jnp
from jax import lax
from jax.experimental import pallas as pl
from jax.experimental.pallas import tpu as pltpu
from jax.sharding import PartitionSpec as P

D = 128
PAIR = 2 * D
ROWS = 128
GROUP = 8
QR = ROWS * GROUP
NX, NY = 4, 8
PAGES = 32
PAGE = 16
BLOCKS = 4
TILE = 512
SCALE2 = D ** (-0.5) * 1.4426950408889634
LOW = -1e30
SLOT = ROWS + NX * PAGE
NEAR = 8


def x_ring(by):
    return [
        ((x * NY + y) * 2 + c, (((x + by) % NX) * NY + y) * 2 + c)
        for x in range(NX) for y in range(NY) for c in range(2)
    ]


def x_next():
    return [pair for pair in x_ring(1) if pair[0] < pair[1]]


SWAP = [(i, i ^ 1) for i in range(2 * NX * NY)]
Y_GROUPS = [[(x * NY + y) * 2 + c for y in range(NY)] for x in range(NX) for c in range(2)]


def fold(keys, values, mask, qt_ref, m_ref, l_ref, acc_ref):
    twice = jnp.concatenate([keys, keys], axis=1)
    lifted = jnp.concatenate([values.T, jnp.ones((16, keys.shape[0]), jnp.bfloat16)], axis=0)

    def scores_of(at):
        scores = jnp.dot(twice, qt_ref[:, at:at + TILE], preferred_element_type=jnp.float32)
        if mask is not None:
            scores = jnp.where(jnp.concatenate([mask] * (TILE // ROWS), axis=1), scores, LOW)
        return scores

    coming = scores_of(0)
    for at in range(0, QR, TILE):
        cols = slice(at, at + TILE)
        scores = coming
        if at + TILE < QR:
            coming = scores_of(at + TILE)
        old = m_ref[:, cols]
        top = jnp.maximum(old, jnp.max(scores, axis=0, keepdims=True))
        weights = jnp.exp2(scores - top).astype(jnp.bfloat16)
        factor = jnp.exp2(old - top)
        m_ref[:, cols] = top
        mixed = jnp.dot(lifted, weights, preferred_element_type=jnp.float32)
        l_ref[:, cols] = l_ref[:, cols] * factor + mixed[D:D + 1]
        acc_ref[:, cols] = acc_ref[:, cols] * factor + mixed[:D]


def starts_of(ids_ref, own):
    ids = ids_ref[...]
    starts = [jnp.sum((ids < b).astype(jnp.int32)) for b in range(1, 4)]
    own_ids = ids_ref[pl.ds(own, 1), :]
    row_start = jnp.zeros_like(own_ids)
    for b in range(1, 4):
        row_start = jnp.where(own_ids == b, starts[b - 1], row_start)
    return row_start, jnp.min(row_start), jnp.max(row_start)


def mask_of(block, own, row_start):
    key_rows = lax.broadcasted_iota(jnp.int32, (ROWS, ROWS), 0) + block * ROWS
    query_rows = lax.broadcasted_iota(jnp.int32, (ROWS, ROWS), 1) + own * ROWS
    return (key_rows >= row_start) & (key_rows <= query_rows)


def own_kernel(meta_ref, mine_ref, side_ref, ids_ref, q_ref, qt_ref, m_ref, l_ref, acc_ref):
    own = meta_ref[0]
    row_start, first, last = starts_of(ids_ref, own)
    for g in range(GROUP):
        scaled = q_ref[:, g * D:(g + 1) * D].astype(jnp.float32) * SCALE2
        high = scaled.astype(jnp.bfloat16)
        low = (scaled - high.astype(jnp.float32)).astype(jnp.bfloat16)
        qt_ref[:D, g * ROWS:(g + 1) * ROWS] = high.T
        qt_ref[D:, g * ROWS:(g + 1) * ROWS] = low.T
    m_ref[...] = jnp.full_like(m_ref, LOW)
    l_ref[...] = jnp.zeros_like(l_ref)
    acc_ref[...] = jnp.zeros_like(acc_ref)
    state = (qt_ref, m_ref, l_ref, acc_ref)
    fold(mine_ref[:, :D], mine_ref[:, D:], mask_of(own, own, row_start), *state)

    @pl.when((own % 2 == 1) & (own * ROWS > first))
    def _():
        fold(side_ref[:, :D], side_ref[:, D:], mask_of(own - 1, own, row_start), *state)


def window(kv_ref, skip, slot, core, own, limits, qt_ref, m_ref, l_ref, acc_ref):
    row_start, first, last = limits
    chip = own // 2 - skip
    lowest = jnp.maximum((jnp.maximum(first // ROWS - core, -1) + 1) // 2, chip - NEAR)
    steps = jnp.maximum(chip - lowest + BLOCKS - 1, 0) // BLOCKS

    def step(i, carry):
        base = chip - BLOCKS * (i + 1)
        pairs = []
        for b in range(BLOCKS):
            start = (base + b + 4 * NY) % NY * slot
            pairs.append(kv_ref[pl.ds(pl.multiple_of(start, PAGE), ROWS), :])
        keys = jnp.concatenate([pair[:, :D] for pair in pairs], axis=0)
        values = jnp.concatenate([pair[:, D:] for pair in pairs], axis=0)
        whole = (2 * base + core) * ROWS >= last

        @pl.when(whole)
        def _():
            fold(keys, values, None, qt_ref, m_ref, l_ref, acc_ref)

        @pl.when(jnp.logical_not(whole))
        def _():
            mask = jnp.concatenate(
                [mask_of(2 * (base + b) + core, own, row_start) for b in range(BLOCKS)], axis=0
            )
            fold(keys, values, mask, qt_ref, m_ref, l_ref, acc_ref)

        return carry

    lax.fori_loop(0, steps, step, 0)


def near_kernel(meta_ref, kv_ref, ids_ref, qt_ref, m_in, l_in, acc_in, m_ref, l_ref, acc_ref):
    m_ref[...] = m_in[...]
    l_ref[...] = l_in[...]
    acc_ref[...] = acc_in[...]
    own = meta_ref[0]
    window(kv_ref, 0, SLOT, own % 2, own, starts_of(ids_ref, own), qt_ref, m_ref, l_ref, acc_ref)


def near_side_kernel(meta_ref, table_ref, kv_ref, side_ref, ids_ref, qt_ref, m_in, l_in, acc_in,
                     m_ref, l_ref, acc_ref, prefix_ref):
    m_ref[...] = m_in[...]
    l_ref[...] = l_in[...]
    acc_ref[...] = acc_in[...]
    own = meta_ref[0]
    core, x = own % 2, own // (2 * NY)
    for i in range(PAGES):
        page = table_ref[i]
        start = (page // 2) % NY * SLOT + ROWS + (x + NX - page // (2 * NY)) % NX * PAGE
        rows = pl.ds(pl.multiple_of(start, PAGE), PAGE)
        prefix_ref[i * PAGE:(i + 1) * PAGE, :] = jnp.where(page % 2 == core, kv_ref[rows, :], side_ref[rows, :])

    fold(prefix_ref[:, :D], prefix_ref[:, D:], None, qt_ref, m_ref, l_ref, acc_ref)
    window(side_ref, 0, SLOT, 1 - core, own, starts_of(ids_ref, own), qt_ref, m_ref, l_ref, acc_ref)


def far_kernel(meta_ref, kv_ref, ids_ref, qt_ref, m_in, l_in, acc_in, m_ref, l_ref, acc_ref):
    m_ref[...] = m_in[...]
    l_ref[...] = l_in[...]
    acc_ref[...] = acc_in[...]
    own = meta_ref[0]
    window(kv_ref, NEAR, ROWS, own % 2, own, starts_of(ids_ref, own), qt_ref, m_ref, l_ref, acc_ref)


def last_kernel(meta_ref, kv_ref, ids_ref, qt_ref, m_in, l_in, acc_in, out_ref, m_ref, l_ref, acc_ref):
    m_ref[...] = m_in[...]
    l_ref[...] = l_in[...]
    acc_ref[...] = acc_in[...]
    own = meta_ref[0]
    window(kv_ref, NEAR, ROWS, 1 - own % 2, own, starts_of(ids_ref, own), qt_ref, m_ref, l_ref, acc_ref)
    result = (acc_ref[...] * (1.0 / l_ref[...])).astype(jnp.bfloat16)
    for g in range(GROUP):
        out_ref[:, g * D:(g + 1) * D] = result[:, g * ROWS:(g + 1) * ROWS].T


VM = pl.BlockSpec(memory_space=pltpu.VMEM)
SM = pl.BlockSpec(memory_space=pltpu.SMEM)


def cost(keys):
    return pl.CostEstimate(flops=4 * D * QR * keys, bytes_accessed=1 << 20, transcendentals=QR * keys)


def per_device(queries, branch_key_value, branch_ids, pool, page_table):
    me = lax.axis_index("seq")
    y = (me // 2) % NY
    page = pool.reshape(PAGE, PAIR)
    wide = jnp.transpose(jnp.concatenate([queries, branch_key_value], axis=2), (1, 0, 2))
    wide = lax.all_to_all(wide, "head", split_axis=0, concat_axis=0, tiled=True).reshape(ROWS, -1)
    two_page = lax.ppermute(page, "seq", x_ring(2))
    wide, two_page, later = lax.optimization_barrier((wide, two_page, page))
    own = wide[:, GROUP * D:]
    one_back = lax.ppermute(jnp.concatenate([own, page], axis=0), "seq", x_ring(1))
    three_page = lax.ppermute(later, "seq", x_ring(3))
    target = jnp.arange(NY, dtype=jnp.int32)[:, None, None]
    block = jnp.where(target > y, own[None], one_back[None, :ROWS])
    pages = jnp.concatenate([page, one_back[ROWS:], two_page, three_page], axis=0)[None]
    send = jnp.concatenate([block, jnp.broadcast_to(pages, (NY, NX * PAGE, PAIR))], axis=1)
    near = lax.all_to_all(send, "seq", split_axis=0, concat_axis=0, tiled=True, axis_index_groups=Y_GROUPS)
    later, _ = lax.optimization_barrier((own, send))
    side = lax.ppermute(later, "seq", SWAP)
    ids = branch_ids.reshape(2 * NX * NY, ROWS)
    meta = me.astype(jnp.int32).reshape(1)
    state = [
        jax.ShapeDtypeStruct((1, QR), jnp.float32),
        jax.ShapeDtypeStruct((1, QR), jnp.float32),
        jax.ShapeDtypeStruct((D, QR), jnp.float32),
    ]
    params = pltpu.CompilerParams(vmem_limit_bytes=40 * 1024 * 1024)
    qt, *now = pl.pallas_call(
        own_kernel,
        out_shape=[jax.ShapeDtypeStruct((PAIR, QR), jnp.bfloat16)] + state,
        in_specs=[SM] + [VM] * 4,
        out_specs=[VM] * 4,
        compiler_params=params,
        cost_estimate=cost(256),
        name="own_chip",
    )(meta, own, side, ids, wide)
    near, qt, now = lax.optimization_barrier((near, qt, now))
    far = lax.ppermute(near[:, :ROWS], "seq", x_next())

    def near_part(operands):
        near, qt, now = operands
        near = near.reshape(NY * SLOT, PAIR)
        near_side = lax.ppermute(near, "seq", SWAP)
        now = pl.pallas_call(
            near_kernel,
            out_shape=state,
            in_specs=[SM] + [VM] * 6,
            out_specs=[VM] * 3,
            compiler_params=params,
            cost_estimate=cost(1024),
            name="near_window",
        )(meta, near, ids, qt, *now)
        return list(pl.pallas_call(
            near_side_kernel,
            out_shape=state,
            in_specs=[SM, SM] + [VM] * 7,
            out_specs=[VM] * 3,
            scratch_shapes=[pltpu.VMEM((PAGES * PAGE, PAIR), jnp.bfloat16)],
            compiler_params=params,
            cost_estimate=cost(1536),
            name="near_other_core_and_prefix",
        )(meta, page_table.reshape(PAGES), near, near_side, ids, qt, *now))

    now = lax.cond(me < 2 * NX * NY, near_part, lambda operands: list(operands[2]), (near, qt, now))
    far, now = lax.optimization_barrier((far, now))
    far = far.reshape(NY * ROWS, PAIR)
    far_side = lax.ppermute(far, "seq", SWAP)
    now = pl.pallas_call(
        far_kernel,
        out_shape=state,
        in_specs=[SM] + [VM] * 6,
        out_specs=[VM] * 3,
        compiler_params=params,
        cost_estimate=cost(1024),
        name="far_window",
    )(meta, far, ids, qt, *now)
    out = pl.pallas_call(
        last_kernel,
        out_shape=jax.ShapeDtypeStruct((ROWS, GROUP * D), jnp.bfloat16),
        in_specs=[SM] + [VM] * 6,
        out_specs=VM,
        scratch_shapes=[
            pltpu.VMEM((1, QR), jnp.float32),
            pltpu.VMEM((1, QR), jnp.float32),
            pltpu.VMEM((D, QR), jnp.float32),
        ],
        compiler_params=params,
        cost_estimate=cost(1024),
        name="far_other_core",
    )(meta, far_side, ids, qt, *now)
    out = lax.all_to_all(out.reshape(8, ROWS // 8, GROUP * D), "head", split_axis=0, concat_axis=0, tiled=True)
    return jnp.transpose(out, (1, 0, 2))


def solution(mesh):
    return jax.shard_map(
        per_device,
        mesh=mesh,
        in_specs=(
            P(("seq", "head"), None, None),
            P(("seq", "head"), None, None),
            P(),
            P("seq", None, "head", None),
            P("head", None),
        ),
        out_specs=P(("seq", "head"), None, None),
        check_vma=False,
    )
```

```python
import jax
import jax.numpy as jnp
from jax import lax
from jax.experimental import pallas as pl
from jax.experimental.pallas import tpu as pltpu
from jax.sharding import PartitionSpec as P

D = 128
PAIR = 2 * D
ROWS = 128
GROUP = 8
QR = ROWS * GROUP
NX, NY = 4, 8
PAGES = 32
PAGE = 16
BLOCKS = 4
TILE = 512
SCALE2 = D ** (-0.5) * 1.4426950408889634
LOW = -1e30
SLOT = ROWS + NX * PAGE
NEAR = 8


def x_ring(by):
    return [
        ((x * NY + y) * 2 + c, (((x + by) % NX) * NY + y) * 2 + c)
        for x in range(NX) for y in range(NY) for c in range(2)
    ]


def x_next():
    return [pair for pair in x_ring(1) if pair[0] < pair[1]]


SWAP = [(i, i ^ 1) for i in range(2 * NX * NY)]
Y_GROUPS = [[(x * NY + y) * 2 + c for y in range(NY)] for x in range(NX) for c in range(2)]


def fold(keys, values, mask, qt_ref, m_ref, l_ref, acc_ref):
    twice = jnp.concatenate([keys, keys], axis=1)
    lifted = jnp.concatenate([values.T, jnp.ones((16, keys.shape[0]), jnp.bfloat16)], axis=0)

    def scores_of(at):
        scores = jnp.dot(twice, qt_ref[:, at:at + TILE], preferred_element_type=jnp.float32)
        if mask is not None:
            scores = jnp.where(jnp.concatenate([mask] * (TILE // ROWS), axis=1), scores, LOW)
        return scores

    coming = scores_of(0)
    for at in range(0, QR, TILE):
        cols = slice(at, at + TILE)
        scores = coming
        if at + TILE < QR:
            coming = scores_of(at + TILE)
        old = m_ref[:, cols]
        top = jnp.maximum(old, jnp.max(scores, axis=0, keepdims=True))
        weights = jnp.exp2(scores - top).astype(jnp.bfloat16)
        factor = jnp.exp2(old - top)
        m_ref[:, cols] = top
        mixed = jnp.dot(lifted, weights, preferred_element_type=jnp.float32)
        l_ref[:, cols] = l_ref[:, cols] * factor + mixed[D:D + 1]
        acc_ref[:, cols] = acc_ref[:, cols] * factor + mixed[:D]


def starts_of(ids_ref, own):
    ids = ids_ref[...]
    starts = [jnp.sum((ids < b).astype(jnp.int32)) for b in range(1, 4)]
    own_ids = ids_ref[pl.ds(own, 1), :]
    row_start = jnp.zeros_like(own_ids)
    for b in range(1, 4):
        row_start = jnp.where(own_ids == b, starts[b - 1], row_start)
    return row_start, jnp.min(row_start), jnp.max(row_start)


def mask_of(block, own, row_start):
    key_rows = lax.broadcasted_iota(jnp.int32, (ROWS, ROWS), 0) + block * ROWS
    query_rows = lax.broadcasted_iota(jnp.int32, (ROWS, ROWS), 1) + own * ROWS
    return (key_rows >= row_start) & (key_rows <= query_rows)


def by_head_kernel(q_ref, kv_ref, out_ref):
    out_ref[:, :, :GROUP * D] = jnp.transpose(q_ref[...], (1, 0, 2))
    out_ref[:, :, GROUP * D:] = jnp.transpose(kv_ref[...], (1, 0, 2))


def own_kernel(meta_ref, mine_ref, side_ref, ids_ref, q_ref, qt_ref, m_ref, l_ref, acc_ref):
    own = meta_ref[0]
    row_start, first, last = starts_of(ids_ref, own)
    for g in range(GROUP):
        scaled = q_ref[:, g * D:(g + 1) * D].astype(jnp.float32) * SCALE2
        high = scaled.astype(jnp.bfloat16)
        low = (scaled - high.astype(jnp.float32)).astype(jnp.bfloat16)
        qt_ref[:D, g * ROWS:(g + 1) * ROWS] = high.T
        qt_ref[D:, g * ROWS:(g + 1) * ROWS] = low.T
    m_ref[...] = jnp.full_like(m_ref, LOW)
    l_ref[...] = jnp.zeros_like(l_ref)
    acc_ref[...] = jnp.zeros_like(acc_ref)
    state = (qt_ref, m_ref, l_ref, acc_ref)
    fold(mine_ref[:, :D], mine_ref[:, D:], mask_of(own, own, row_start), *state)

    @pl.when((own % 2 == 1) & (own * ROWS > first))
    def _():
        fold(side_ref[:, :D], side_ref[:, D:], mask_of(own - 1, own, row_start), *state)


def window(kv_ref, skip, slot, core, own, limits, qt_ref, m_ref, l_ref, acc_ref):
    row_start, first, last = limits
    chip = own // 2 - skip
    lowest = jnp.maximum((jnp.maximum(first // ROWS - core, -1) + 1) // 2, chip - NEAR)
    steps = jnp.maximum(chip - lowest + BLOCKS - 1, 0) // BLOCKS

    def step(i, carry):
        base = chip - BLOCKS * (i + 1)
        pairs = []
        for b in range(BLOCKS):
            start = (base + b + 4 * NY) % NY * slot
            pairs.append(kv_ref[pl.ds(pl.multiple_of(start, PAGE), ROWS), :])
        keys = jnp.concatenate([pair[:, :D] for pair in pairs], axis=0)
        values = jnp.concatenate([pair[:, D:] for pair in pairs], axis=0)
        whole = (2 * base + core) * ROWS >= last

        @pl.when(whole)
        def _():
            fold(keys, values, None, qt_ref, m_ref, l_ref, acc_ref)

        @pl.when(jnp.logical_not(whole))
        def _():
            mask = jnp.concatenate(
                [mask_of(2 * (base + b) + core, own, row_start) for b in range(BLOCKS)], axis=0
            )
            fold(keys, values, mask, qt_ref, m_ref, l_ref, acc_ref)

        return carry

    lax.fori_loop(0, steps, step, 0)


def near_kernel(meta_ref, kv_ref, ids_ref, qt_ref, m_in, l_in, acc_in, m_ref, l_ref, acc_ref):
    m_ref[...] = m_in[...]
    l_ref[...] = l_in[...]
    acc_ref[...] = acc_in[...]
    own = meta_ref[0]
    window(kv_ref, 0, SLOT, own % 2, own, starts_of(ids_ref, own), qt_ref, m_ref, l_ref, acc_ref)


def near_side_kernel(meta_ref, table_ref, kv_ref, side_ref, ids_ref, qt_ref, m_in, l_in, acc_in,
                     m_ref, l_ref, acc_ref, prefix_ref):
    m_ref[...] = m_in[...]
    l_ref[...] = l_in[...]
    acc_ref[...] = acc_in[...]
    own = meta_ref[0]
    core, x = own % 2, own // (2 * NY)
    for i in range(PAGES):
        page = table_ref[i]
        start = (page // 2) % NY * SLOT + ROWS + (x + NX - page // (2 * NY)) % NX * PAGE
        rows = pl.ds(pl.multiple_of(start, PAGE), PAGE)
        prefix_ref[i * PAGE:(i + 1) * PAGE, :] = jnp.where(page % 2 == core, kv_ref[rows, :], side_ref[rows, :])

    fold(prefix_ref[:, :D], prefix_ref[:, D:], None, qt_ref, m_ref, l_ref, acc_ref)
    window(side_ref, 0, SLOT, 1 - core, own, starts_of(ids_ref, own), qt_ref, m_ref, l_ref, acc_ref)


def far_kernel(meta_ref, kv_ref, ids_ref, qt_ref, m_in, l_in, acc_in, m_ref, l_ref, acc_ref):
    m_ref[...] = m_in[...]
    l_ref[...] = l_in[...]
    acc_ref[...] = acc_in[...]
    own = meta_ref[0]
    window(kv_ref, NEAR, ROWS, own % 2, own, starts_of(ids_ref, own), qt_ref, m_ref, l_ref, acc_ref)


def last_kernel(meta_ref, kv_ref, ids_ref, qt_ref, m_in, l_in, acc_in, out_ref, m_ref, l_ref, acc_ref):
    m_ref[...] = m_in[...]
    l_ref[...] = l_in[...]
    acc_ref[...] = acc_in[...]
    own = meta_ref[0]
    window(kv_ref, NEAR, ROWS, 1 - own % 2, own, starts_of(ids_ref, own), qt_ref, m_ref, l_ref, acc_ref)
    result = (acc_ref[...] * (1.0 / l_ref[...])).astype(jnp.bfloat16)
    for g in range(GROUP):
        out_ref[:, g * D:(g + 1) * D] = result[:, g * ROWS:(g + 1) * ROWS].T


VM = pl.BlockSpec(memory_space=pltpu.VMEM)
SM = pl.BlockSpec(memory_space=pltpu.SMEM)


def cost(keys):
    return pl.CostEstimate(flops=4 * D * QR * keys, bytes_accessed=1 << 20, transcendentals=QR * keys)


def per_device(queries, branch_key_value, branch_ids, pool, page_table):
    me = lax.axis_index("seq")
    y = (me // 2) % NY
    page = pool.reshape(PAGE, PAIR)
    wide = pl.pallas_call(
        by_head_kernel,
        out_shape=jax.ShapeDtypeStruct((8, ROWS // 8, GROUP * D + PAIR), jnp.bfloat16),
        in_specs=[VM] * 2,
        out_specs=VM,
        name="by_head",
    )(queries, branch_key_value)
    wide = lax.all_to_all(wide, "head", split_axis=0, concat_axis=0, tiled=True).reshape(ROWS, -1)
    two_page = lax.ppermute(page, "seq", x_ring(2))
    wide, two_page = lax.optimization_barrier((wide, two_page))
    own = wide[:, GROUP * D:]
    one_back = lax.ppermute(jnp.concatenate([own, page, two_page], axis=0), "seq", x_ring(1))
    target = jnp.arange(NY, dtype=jnp.int32)[:, None, None]
    block = jnp.where(target > y, own[None], one_back[None, :ROWS])
    pages = jnp.concatenate([page, one_back[ROWS:ROWS + PAGE], two_page, one_back[ROWS + PAGE:]], axis=0)[None]
    send = jnp.concatenate([block, jnp.broadcast_to(pages, (NY, NX * PAGE, PAIR))], axis=1)
    near = lax.all_to_all(send, "seq", split_axis=0, concat_axis=0, tiled=True, axis_index_groups=Y_GROUPS)
    later, _ = lax.optimization_barrier((own, send))
    side = lax.ppermute(later, "seq", SWAP)
    ids = branch_ids.reshape(2 * NX * NY, ROWS)
    meta = me.astype(jnp.int32).reshape(1)
    state = [
        jax.ShapeDtypeStruct((1, QR), jnp.float32),
        jax.ShapeDtypeStruct((1, QR), jnp.float32),
        jax.ShapeDtypeStruct((D, QR), jnp.float32),
    ]
    params = pltpu.CompilerParams(vmem_limit_bytes=40 * 1024 * 1024)
    qt, *now = pl.pallas_call(
        own_kernel,
        out_shape=[jax.ShapeDtypeStruct((PAIR, QR), jnp.bfloat16)] + state,
        in_specs=[SM] + [VM] * 4,
        out_specs=[VM] * 4,
        compiler_params=params,
        cost_estimate=cost(256),
        name="own_chip",
    )(meta, own, side, ids, wide)
    near, qt, now = lax.optimization_barrier((near, qt, now))
    far = lax.ppermute(near[:, :ROWS], "seq", x_next())

    def near_part(operands):
        near, qt, now = operands
        near = near.reshape(NY * SLOT, PAIR)
        near_side = lax.ppermute(near, "seq", SWAP)
        now = pl.pallas_call(
            near_kernel,
            out_shape=state,
            in_specs=[SM] + [VM] * 6,
            out_specs=[VM] * 3,
            compiler_params=params,
            cost_estimate=cost(1024),
            name="near_window",
        )(meta, near, ids, qt, *now)
        return list(pl.pallas_call(
            near_side_kernel,
            out_shape=state,
            in_specs=[SM, SM] + [VM] * 7,
            out_specs=[VM] * 3,
            scratch_shapes=[pltpu.VMEM((PAGES * PAGE, PAIR), jnp.bfloat16)],
            compiler_params=params,
            cost_estimate=cost(1536),
            name="near_other_core_and_prefix",
        )(meta, page_table.reshape(PAGES), near, near_side, ids, qt, *now))

    now = lax.cond(me < 2 * NX * NY, near_part, lambda operands: list(operands[2]), (near, qt, now))
    far, now = lax.optimization_barrier((far, now))
    far = far.reshape(NY * ROWS, PAIR)
    far_side = lax.ppermute(far, "seq", SWAP)
    now = pl.pallas_call(
        far_kernel,
        out_shape=state,
        in_specs=[SM] + [VM] * 6,
        out_specs=[VM] * 3,
        compiler_params=params,
        cost_estimate=cost(1024),
        name="far_window",
    )(meta, far, ids, qt, *now)
    out = pl.pallas_call(
        last_kernel,
        out_shape=jax.ShapeDtypeStruct((ROWS, GROUP * D), jnp.bfloat16),
        in_specs=[SM] + [VM] * 6,
        out_specs=VM,
        scratch_shapes=[
            pltpu.VMEM((1, QR), jnp.float32),
            pltpu.VMEM((1, QR), jnp.float32),
            pltpu.VMEM((D, QR), jnp.float32),
        ],
        compiler_params=params,
        cost_estimate=cost(1024),
        name="far_other_core",
    )(meta, far_side, ids, qt, *now)
    out = lax.all_to_all(out.reshape(8, ROWS // 8, GROUP * D), "head", split_axis=0, concat_axis=0, tiled=True)
    return jnp.transpose(out, (1, 0, 2))


def solution(mesh):
    return jax.shard_map(
        per_device,
        mesh=mesh,
        in_specs=(
            P(("seq", "head"), None, None),
            P(("seq", "head"), None, None),
            P(),
            P("seq", None, "head", None),
            P("head", None),
        ),
        out_specs=P(("seq", "head"), None, None),
        check_vma=False,
    )
```

```python
import jax
import jax.numpy as jnp
from jax import lax
from jax.experimental import pallas as pl
from jax.experimental.pallas import tpu as pltpu
from jax.sharding import PartitionSpec as P

D = 128
PAIR = 2 * D
ROWS = 128
GROUP = 8
QR = ROWS * GROUP
NX, NY = 4, 8
PAGES = 32
PAGE = 16
BLOCKS = 4
TILE = 512
SCALE2 = D ** (-0.5) * 1.4426950408889634
LOW = -1e30
NEAR = 8


def x_ring(by):
    return [
        ((x * NY + y) * 2 + c, (((x + by) % NX) * NY + y) * 2 + c)
        for x in range(NX) for y in range(NY) for c in range(2)
    ]


def x_next():
    return [pair for pair in x_ring(1) if pair[0] < pair[1]]


def y_ring(by):
    return [
        ((x * NY + y) * 2 + c, (x * NY + (y + by) % NY) * 2 + c)
        for x in range(NX) for y in range(NY) for c in range(2)
    ]


SWAP = [(i, i ^ 1) for i in range(2 * NX * NY)]
Y_GROUPS = [[(x * NY + y) * 2 + c for y in range(NY)] for x in range(NX) for c in range(2)]


def fold(keys, values, mask, qt_ref, m_ref, l_ref, acc_ref):
    twice = jnp.concatenate([keys, keys], axis=1)
    lifted = jnp.concatenate([values.T, jnp.ones((16, keys.shape[0]), jnp.bfloat16)], axis=0)

    def scores_of(at):
        scores = jnp.dot(twice, qt_ref[:, at:at + TILE], preferred_element_type=jnp.float32)
        if mask is not None:
            scores = jnp.where(jnp.concatenate([mask] * (TILE // ROWS), axis=1), scores, LOW)
        return scores

    coming = scores_of(0)
    for at in range(0, QR, TILE):
        cols = slice(at, at + TILE)
        scores = coming
        if at + TILE < QR:
            coming = scores_of(at + TILE)
        old = m_ref[:, cols]
        top = jnp.maximum(old, jnp.max(scores, axis=0, keepdims=True))
        weights = jnp.exp2(scores - top).astype(jnp.bfloat16)
        factor = jnp.exp2(old - top)
        m_ref[:, cols] = top
        mixed = jnp.dot(lifted, weights, preferred_element_type=jnp.float32)
        l_ref[:, cols] = l_ref[:, cols] * factor + mixed[D:D + 1]
        acc_ref[:, cols] = acc_ref[:, cols] * factor + mixed[:D]


def starts_of(ids_ref, own):
    ids = ids_ref[...]
    starts = [jnp.sum((ids < b).astype(jnp.int32)) for b in range(1, 4)]
    own_ids = ids_ref[pl.ds(own, 1), :]
    row_start = jnp.zeros_like(own_ids)
    for b in range(1, 4):
        row_start = jnp.where(own_ids == b, starts[b - 1], row_start)
    return row_start, jnp.min(row_start), jnp.max(row_start)


def mask_of(block, own, row_start):
    key_rows = lax.broadcasted_iota(jnp.int32, (ROWS, ROWS), 0) + block * ROWS
    query_rows = lax.broadcasted_iota(jnp.int32, (ROWS, ROWS), 1) + own * ROWS
    return (key_rows >= row_start) & (key_rows <= query_rows)


def by_head_kernel(q_ref, kv_ref, out_ref):
    out_ref[:, :, :GROUP * D] = jnp.transpose(q_ref[...], (1, 0, 2))
    out_ref[:, :, GROUP * D:] = jnp.transpose(kv_ref[...], (1, 0, 2))


def own_kernel(meta_ref, table_ref, mine_ref, side_ref, ids_ref, q_ref, qt_ref, m_ref, l_ref, acc_ref, prefix_ref):
    own = meta_ref[0]
    row_start, first, last = starts_of(ids_ref, own)
    for g in range(GROUP):
        scaled = q_ref[:, g * D:(g + 1) * D].astype(jnp.float32) * SCALE2
        high = scaled.astype(jnp.bfloat16)
        low = (scaled - high.astype(jnp.float32)).astype(jnp.bfloat16)
        qt_ref[:D, g * ROWS:(g + 1) * ROWS] = high.T
        qt_ref[D:, g * ROWS:(g + 1) * ROWS] = low.T
    m_ref[...] = jnp.full_like(m_ref, LOW)
    l_ref[...] = jnp.zeros_like(l_ref)
    acc_ref[...] = jnp.zeros_like(acc_ref)
    state = (qt_ref, m_ref, l_ref, acc_ref)
    fold(mine_ref[:ROWS, :D], mine_ref[:ROWS, D:], mask_of(own, own, row_start), *state)

    @pl.when((own % 2 == 1) & (own * ROWS > first))
    def _():
        fold(side_ref[:ROWS, :D], side_ref[:ROWS, D:], mask_of(own - 1, own, row_start), *state)

    core, y, x = own % 2, (own // 2) % NY, own // (2 * NY)
    for i in range(PAGES):
        page = table_ref[i]
        off = (y + NY - (page // 2) % NY) % NY
        unit = NY * ((x + NX - page // (2 * NY)) % NX) + off // 4 + 2 * (off // 2 % 2) + 4 * (off % 2)
        rows = pl.ds(pl.multiple_of(ROWS + unit * PAGE, PAGE), PAGE)
        prefix_ref[i * PAGE:(i + 1) * PAGE, :] = jnp.where(page % 2 == core, mine_ref[rows, :], side_ref[rows, :])

    fold(prefix_ref[:, :D], prefix_ref[:, D:], None, *state)


def window(kv_ref, skip, core, own, limits, qt_ref, m_ref, l_ref, acc_ref):
    row_start, first, last = limits
    chip = own // 2 - skip
    lowest = jnp.maximum((jnp.maximum(first // ROWS - core, -1) + 1) // 2, chip - NEAR)
    steps = jnp.maximum(chip - lowest + BLOCKS - 1, 0) // BLOCKS

    def step(i, carry):
        base = chip - BLOCKS * (i + 1)
        pairs = []
        for b in range(BLOCKS):
            start = (base + b + 4 * NY) % NY * ROWS
            pairs.append(kv_ref[pl.ds(pl.multiple_of(start, PAGE), ROWS), :])
        keys = jnp.concatenate([pair[:, :D] for pair in pairs], axis=0)
        values = jnp.concatenate([pair[:, D:] for pair in pairs], axis=0)
        whole = (2 * base + core) * ROWS >= last

        @pl.when(whole)
        def _():
            fold(keys, values, None, qt_ref, m_ref, l_ref, acc_ref)

        @pl.when(jnp.logical_not(whole))
        def _():
            mask = jnp.concatenate(
                [mask_of(2 * (base + b) + core, own, row_start) for b in range(BLOCKS)], axis=0
            )
            fold(keys, values, mask, qt_ref, m_ref, l_ref, acc_ref)

        return carry

    lax.fori_loop(0, steps, step, 0)


def near_kernel(meta_ref, kv_ref, ids_ref, qt_ref, m_in, l_in, acc_in, m_ref, l_ref, acc_ref):
    m_ref[...] = m_in[...]
    l_ref[...] = l_in[...]
    acc_ref[...] = acc_in[...]
    own = meta_ref[0]
    window(kv_ref, 0, own % 2, own, starts_of(ids_ref, own), qt_ref, m_ref, l_ref, acc_ref)


def near_side_kernel(meta_ref, kv_ref, ids_ref, qt_ref, m_in, l_in, acc_in, m_ref, l_ref, acc_ref):
    m_ref[...] = m_in[...]
    l_ref[...] = l_in[...]
    acc_ref[...] = acc_in[...]
    own = meta_ref[0]
    window(kv_ref, 0, 1 - own % 2, own, starts_of(ids_ref, own), qt_ref, m_ref, l_ref, acc_ref)


def far_kernel(meta_ref, kv_ref, ids_ref, qt_ref, m_in, l_in, acc_in, m_ref, l_ref, acc_ref):
    m_ref[...] = m_in[...]
    l_ref[...] = l_in[...]
    acc_ref[...] = acc_in[...]
    own = meta_ref[0]
    window(kv_ref, NEAR, own % 2, own, starts_of(ids_ref, own), qt_ref, m_ref, l_ref, acc_ref)


def last_kernel(meta_ref, kv_ref, ids_ref, qt_ref, m_in, l_in, acc_in, out_ref, m_ref, l_ref, acc_ref):
    m_ref[...] = m_in[...]
    l_ref[...] = l_in[...]
    acc_ref[...] = acc_in[...]
    own = meta_ref[0]
    window(kv_ref, NEAR, 1 - own % 2, own, starts_of(ids_ref, own), qt_ref, m_ref, l_ref, acc_ref)
    result = (acc_ref[...] * (1.0 / l_ref[...])).astype(jnp.bfloat16)
    for g in range(GROUP):
        out_ref[:, g * D:(g + 1) * D] = result[:, g * ROWS:(g + 1) * ROWS].T


VM = pl.BlockSpec(memory_space=pltpu.VMEM)
SM = pl.BlockSpec(memory_space=pltpu.SMEM)


def cost(keys):
    return pl.CostEstimate(flops=4 * D * QR * keys, bytes_accessed=1 << 20, transcendentals=QR * keys)


def per_device(queries, branch_key_value, branch_ids, pool, page_table):
    me = lax.axis_index("seq")
    y = (me // 2) % NY
    pages = pool.reshape(PAGE, PAIR)
    pages = jnp.concatenate([pages, lax.ppermute(pages, "seq", y_ring(4))], axis=0)
    wide = pl.pallas_call(
        by_head_kernel,
        out_shape=jax.ShapeDtypeStruct((8, ROWS // 8, GROUP * D + PAIR), jnp.bfloat16),
        in_specs=[VM] * 2,
        out_specs=VM,
        name="by_head",
    )(queries, branch_key_value)
    wide = lax.all_to_all(wide, "head", split_axis=0, concat_axis=0, tiled=True).reshape(ROWS, -1)
    pages = jnp.concatenate([pages, lax.ppermute(pages, "seq", y_ring(2))], axis=0)
    wide, pages = lax.optimization_barrier((wide, pages))
    own = wide[:, GROUP * D:]
    before = lax.ppermute(own, "seq", x_next())
    last_pages = lax.ppermute(pages, "seq", y_ring(1))
    own, before, pages, last_pages = lax.optimization_barrier((own, before, pages, last_pages))
    target = jnp.arange(NY, dtype=jnp.int32)[:, None, None]
    send = jnp.where(target > y, own[None], before[None])
    near = lax.all_to_all(send, "seq", split_axis=0, concat_axis=0, tiled=True, axis_index_groups=Y_GROUPS)
    pages, own, _ = lax.optimization_barrier((jnp.concatenate([pages, last_pages], axis=0), own, send))
    mine = jnp.concatenate([own, pages] + [lax.ppermute(pages, "seq", x_ring(k)) for k in (1, 2, 3)], axis=0)
    side = lax.ppermute(mine, "seq", SWAP)

    ids = branch_ids.reshape(2 * NX * NY, ROWS)
    meta = me.astype(jnp.int32).reshape(1)
    state = [
        jax.ShapeDtypeStruct((1, QR), jnp.float32),
        jax.ShapeDtypeStruct((1, QR), jnp.float32),
        jax.ShapeDtypeStruct((D, QR), jnp.float32),
    ]
    params = pltpu.CompilerParams(vmem_limit_bytes=40 * 1024 * 1024)
    qt, *now = pl.pallas_call(
        own_kernel,
        out_shape=[jax.ShapeDtypeStruct((PAIR, QR), jnp.bfloat16)] + state,
        in_specs=[SM, SM] + [VM] * 4,
        out_specs=[VM] * 4,
        scratch_shapes=[pltpu.VMEM((PAGES * PAGE, PAIR), jnp.bfloat16)],
        compiler_params=params,
        cost_estimate=cost(768),
        name="own_chip_and_prefix",
    )(meta, page_table.reshape(PAGES), mine, side, ids, wide)
    near, qt, now = lax.optimization_barrier((near, qt, now))
    far = lax.ppermute(near, "seq", x_next())

    def near_part(operands):
        near, qt, now = operands
        near = near.reshape(NY * ROWS, PAIR)
        near_side = lax.ppermute(near, "seq", SWAP)
        now = pl.pallas_call(
            near_kernel,
            out_shape=state,
            in_specs=[SM] + [VM] * 6,
            out_specs=[VM] * 3,
            compiler_params=params,
            cost_estimate=cost(1024),
            name="near_window",
        )(meta, near, ids, qt, *now)
        return list(pl.pallas_call(
            near_side_kernel,
            out_shape=state,
            in_specs=[SM] + [VM] * 6,
            out_specs=[VM] * 3,
            compiler_params=params,
            cost_estimate=cost(1024),
            name="near_other_core",
        )(meta, near_side, ids, qt, *now))

    now = lax.cond(me < 2 * NX * NY, near_part, lambda operands: list(operands[2]), (near, qt, now))
    far, now = lax.optimization_barrier((far, now))
    far = far.reshape(NY * ROWS, PAIR)
    far_side = lax.ppermute(far, "seq", SWAP)
    now = pl.pallas_call(
        far_kernel,
        out_shape=state,
        in_specs=[SM] + [VM] * 6,
        out_specs=[VM] * 3,
        compiler_params=params,
        cost_estimate=cost(1024),
        name="far_window",
    )(meta, far, ids, qt, *now)
    out = pl.pallas_call(
        last_kernel,
        out_shape=jax.ShapeDtypeStruct((ROWS, GROUP * D), jnp.bfloat16),
        in_specs=[SM] + [VM] * 6,
        out_specs=VM,
        scratch_shapes=[
            pltpu.VMEM((1, QR), jnp.float32),
            pltpu.VMEM((1, QR), jnp.float32),
            pltpu.VMEM((D, QR), jnp.float32),
        ],
        compiler_params=params,
        cost_estimate=cost(1024),
        name="far_other_core",
    )(meta, far_side, ids, qt, *now)
    out = lax.all_to_all(out.reshape(8, ROWS // 8, GROUP * D), "head", split_axis=0, concat_axis=0, tiled=True)
    return jnp.transpose(out, (1, 0, 2))


def solution(mesh):
    return jax.shard_map(
        per_device,
        mesh=mesh,
        in_specs=(
            P(("seq", "head"), None, None),
            P(("seq", "head"), None, None),
            P(),
            P("seq", None, "head", None),
            P("head", None),
        ),
        out_specs=P(("seq", "head"), None, None),
        check_vma=False,
    )
```

```python
import jax
import jax.numpy as jnp
from jax import lax
from jax.experimental import pallas as pl
from jax.experimental.pallas import tpu as pltpu
from jax.sharding import PartitionSpec as P

D = 128
PAIR = 2 * D
ROWS = 128
GROUP = 8
QR = ROWS * GROUP
NX, NY = 4, 8
PAGES = 32
PAGE = 16
BLOCKS = 4
TILE = 512
SCALE2 = D ** (-0.5) * 1.4426950408889634
LOW = -1e30
SLOT = ROWS + 2 * PAGE
NEAR = 8


def x_ring(by):
    return [
        ((x * NY + y) * 2 + c, (((x + by) % NX) * NY + y) * 2 + c)
        for x in range(NX) for y in range(NY) for c in range(2)
    ]


def x_next():
    return [pair for pair in x_ring(1) if pair[0] < pair[1]]


SWAP = [(i, i ^ 1) for i in range(2 * NX * NY)]
Y_GROUPS = [[(x * NY + y) * 2 + c for y in range(NY)] for x in range(NX) for c in range(2)]


def fold(keys, values, mask, qt_ref, m_ref, l_ref, acc_ref):
    twice = jnp.concatenate([keys, keys], axis=1)
    lifted = jnp.concatenate([values.T, jnp.ones((16, keys.shape[0]), jnp.bfloat16)], axis=0)

    def scores_of(at):
        scores = jnp.dot(twice, qt_ref[:, at:at + TILE], preferred_element_type=jnp.float32)
        if mask is not None:
            scores = jnp.where(jnp.concatenate([mask] * (TILE // ROWS), axis=1), scores, LOW)
        return scores

    coming = scores_of(0)
    for at in range(0, QR, TILE):
        cols = slice(at, at + TILE)
        scores = coming
        if at + TILE < QR:
            coming = scores_of(at + TILE)
        old = m_ref[:, cols]
        top = jnp.maximum(old, jnp.max(scores, axis=0, keepdims=True))
        weights = jnp.exp2(scores - top).astype(jnp.bfloat16)
        factor = jnp.exp2(old - top)
        m_ref[:, cols] = top
        mixed = jnp.dot(lifted, weights, preferred_element_type=jnp.float32)
        l_ref[:, cols] = l_ref[:, cols] * factor + mixed[D:D + 1]
        acc_ref[:, cols] = acc_ref[:, cols] * factor + mixed[:D]


def starts_of(ids_ref, own):
    ids = ids_ref[...]
    starts = [jnp.sum((ids < b).astype(jnp.int32)) for b in range(1, 4)]
    own_ids = ids_ref[pl.ds(own, 1), :]
    row_start = jnp.zeros_like(own_ids)
    for b in range(1, 4):
        row_start = jnp.where(own_ids == b, starts[b - 1], row_start)
    return row_start, jnp.min(row_start), jnp.max(row_start)


def mask_of(block, own, row_start):
    key_rows = lax.broadcasted_iota(jnp.int32, (ROWS, ROWS), 0) + block * ROWS
    query_rows = lax.broadcasted_iota(jnp.int32, (ROWS, ROWS), 1) + own * ROWS
    return (key_rows >= row_start) & (key_rows <= query_rows)


def by_head_kernel(q_ref, kv_ref, out_ref):
    out_ref[:, :, :GROUP * D] = jnp.transpose(q_ref[...], (1, 0, 2))
    out_ref[:, :, GROUP * D:] = jnp.transpose(kv_ref[...], (1, 0, 2))


def own_kernel(meta_ref, mine_ref, side_ref, ids_ref, q_ref, qt_ref, m_ref, l_ref, acc_ref):
    own = meta_ref[0]
    row_start, first, last = starts_of(ids_ref, own)
    for g in range(GROUP):
        scaled = q_ref[:, g * D:(g + 1) * D].astype(jnp.float32) * SCALE2
        high = scaled.astype(jnp.bfloat16)
        low = (scaled - high.astype(jnp.float32)).astype(jnp.bfloat16)
        qt_ref[:D, g * ROWS:(g + 1) * ROWS] = high.T
        qt_ref[D:, g * ROWS:(g + 1) * ROWS] = low.T
    m_ref[...] = jnp.full_like(m_ref, LOW)
    l_ref[...] = jnp.zeros_like(l_ref)
    acc_ref[...] = jnp.zeros_like(acc_ref)
    state = (qt_ref, m_ref, l_ref, acc_ref)
    fold(mine_ref[:, :D], mine_ref[:, D:], mask_of(own, own, row_start), *state)

    @pl.when((own % 2 == 1) & (own * ROWS > first))
    def _():
        fold(side_ref[:, :D], side_ref[:, D:], mask_of(own - 1, own, row_start), *state)


def window(kv_ref, skip, core, own, limits, qt_ref, m_ref, l_ref, acc_ref):
    row_start, first, last = limits
    chip = own // 2 - skip
    lowest = jnp.maximum((jnp.maximum(first // ROWS - core, -1) + 1) // 2, chip - NEAR)
    steps = jnp.maximum(chip - lowest + BLOCKS - 1, 0) // BLOCKS

    def step(i, carry):
        base = chip - BLOCKS * (i + 1)
        pairs = []
        for b in range(BLOCKS):
            start = (base + b + 4 * NY) % NY * SLOT
            pairs.append(kv_ref[pl.ds(pl.multiple_of(start, PAGE), ROWS), :])
        keys = jnp.concatenate([pair[:, :D] for pair in pairs], axis=0)
        values = jnp.concatenate([pair[:, D:] for pair in pairs], axis=0)
        whole = (2 * base + core) * ROWS >= last

        @pl.when(whole)
        def _():
            fold(keys, values, None, qt_ref, m_ref, l_ref, acc_ref)

        @pl.when(jnp.logical_not(whole))
        def _():
            mask = jnp.concatenate(
                [mask_of(2 * (base + b) + core, own, row_start) for b in range(BLOCKS)], axis=0
            )
            fold(keys, values, mask, qt_ref, m_ref, l_ref, acc_ref)

        return carry

    lax.fori_loop(0, steps, step, 0)


def near_kernel(meta_ref, kv_ref, ids_ref, qt_ref, m_in, l_in, acc_in, m_ref, l_ref, acc_ref):
    m_ref[...] = m_in[...]
    l_ref[...] = l_in[...]
    acc_ref[...] = acc_in[...]
    own = meta_ref[0]
    window(kv_ref, 0, own % 2, own, starts_of(ids_ref, own), qt_ref, m_ref, l_ref, acc_ref)


def near_side_kernel(meta_ref, kv_ref, ids_ref, qt_ref, m_in, l_in, acc_in, m_ref, l_ref, acc_ref):
    m_ref[...] = m_in[...]
    l_ref[...] = l_in[...]
    acc_ref[...] = acc_in[...]
    own = meta_ref[0]
    window(kv_ref, 0, 1 - own % 2, own, starts_of(ids_ref, own), qt_ref, m_ref, l_ref, acc_ref)


def far_kernel(meta_ref, kv_ref, ids_ref, qt_ref, m_in, l_in, acc_in, m_ref, l_ref, acc_ref):
    m_ref[...] = m_in[...]
    l_ref[...] = l_in[...]
    acc_ref[...] = acc_in[...]
    own = meta_ref[0]
    window(kv_ref, NEAR, own % 2, own, starts_of(ids_ref, own), qt_ref, m_ref, l_ref, acc_ref)


def last_kernel(meta_ref, table_ref, near_ref, near_side_ref, far_ref, kv_ref, ids_ref, qt_ref, m_in, l_in, acc_in,
                out_ref, m_ref, l_ref, acc_ref, prefix_ref):
    m_ref[...] = m_in[...]
    l_ref[...] = l_in[...]
    acc_ref[...] = acc_in[...]
    own = meta_ref[0]
    core, x = own % 2, own // (2 * NY)
    for i in range(PAGES):
        page = table_ref[i]
        back = (x + NX - page // (2 * NY)) % NX
        start = (page // 2) % NY * SLOT + ROWS + back // 2 * PAGE
        rows = pl.ds(pl.multiple_of(start, PAGE), PAGE)
        prefix_ref[i * PAGE:(i + 1) * PAGE, :] = jnp.where(
            page % 2 == core,
            jnp.where(back % 2 == 0, near_ref[rows, :], far_ref[rows, :]),
            jnp.where(back % 2 == 0, near_side_ref[rows, :], kv_ref[rows, :]),
        )

    fold(prefix_ref[:, :D], prefix_ref[:, D:], None, qt_ref, m_ref, l_ref, acc_ref)
    window(kv_ref, NEAR, 1 - core, own, starts_of(ids_ref, own), qt_ref, m_ref, l_ref, acc_ref)
    result = (acc_ref[...] * (1.0 / l_ref[...])).astype(jnp.bfloat16)
    for g in range(GROUP):
        out_ref[:, g * D:(g + 1) * D] = result[:, g * ROWS:(g + 1) * ROWS].T


VM = pl.BlockSpec(memory_space=pltpu.VMEM)
SM = pl.BlockSpec(memory_space=pltpu.SMEM)


def cost(keys):
    return pl.CostEstimate(flops=4 * D * QR * keys, bytes_accessed=1 << 20, transcendentals=QR * keys)


def per_device(queries, branch_key_value, branch_ids, pool, page_table):
    me = lax.axis_index("seq")
    y = (me // 2) % NY
    page = pool.reshape(PAGE, PAIR)
    wide = pl.pallas_call(
        by_head_kernel,
        out_shape=jax.ShapeDtypeStruct((8, ROWS // 8, GROUP * D + PAIR), jnp.bfloat16),
        in_specs=[VM] * 2,
        out_specs=VM,
        name="by_head",
    )(queries, branch_key_value)
    wide = lax.all_to_all(wide, "head", split_axis=0, concat_axis=0, tiled=True).reshape(ROWS, -1)
    two_page = lax.ppermute(page, "seq", x_ring(2))
    wide, two_page = lax.optimization_barrier((wide, two_page))
    own = wide[:, GROUP * D:]
    before = lax.ppermute(own, "seq", x_next())
    target = jnp.arange(NY, dtype=jnp.int32)[:, None, None]
    block = jnp.where(target > y, own[None], before[None])
    pages = jnp.concatenate([page, two_page], axis=0)[None]
    send = jnp.concatenate([block, jnp.broadcast_to(pages, (NY, 2 * PAGE, PAIR))], axis=1)
    near = lax.all_to_all(send, "seq", split_axis=0, concat_axis=0, tiled=True, axis_index_groups=Y_GROUPS)
    later, _ = lax.optimization_barrier((own, send))
    side = lax.ppermute(later, "seq", SWAP)
    ids = branch_ids.reshape(2 * NX * NY, ROWS)
    meta = me.astype(jnp.int32).reshape(1)
    state = [
        jax.ShapeDtypeStruct((1, QR), jnp.float32),
        jax.ShapeDtypeStruct((1, QR), jnp.float32),
        jax.ShapeDtypeStruct((D, QR), jnp.float32),
    ]
    params = pltpu.CompilerParams(vmem_limit_bytes=40 * 1024 * 1024)
    qt, *now = pl.pallas_call(
        own_kernel,
        out_shape=[jax.ShapeDtypeStruct((PAIR, QR), jnp.bfloat16)] + state,
        in_specs=[SM] + [VM] * 4,
        out_specs=[VM] * 4,
        compiler_params=params,
        cost_estimate=cost(256),
        name="own_chip",
    )(meta, own, side, ids, wide)
    near, qt, now = lax.optimization_barrier((near, qt, now))
    near = near.reshape(NY * SLOT, PAIR)
    far = lax.ppermute(near, "seq", x_ring(1))

    def near_part(operands):
        near, qt, now = operands
        near_side = lax.ppermute(near, "seq", SWAP)
        for kernel, kv in ((near_kernel, near), (near_side_kernel, near_side)):
            now = pl.pallas_call(
                kernel,
                out_shape=state,
                in_specs=[SM] + [VM] * 6,
                out_specs=[VM] * 3,
                compiler_params=params,
                cost_estimate=cost(1024),
                name=kernel.__name__,
            )(meta, kv, ids, qt, *now)
        return near_side, list(now)

    near_side, now = lax.cond(
        me < 2 * NX * NY, near_part, lambda operands: (operands[0], list(operands[2])), (near, qt, now)
    )
    far, now = lax.optimization_barrier((far, now))
    far_side = lax.ppermute(far, "seq", SWAP)
    now = pl.pallas_call(
        far_kernel,
        out_shape=state,
        in_specs=[SM] + [VM] * 6,
        out_specs=[VM] * 3,
        compiler_params=params,
        cost_estimate=cost(1024),
        name="far_window",
    )(meta, far, ids, qt, *now)
    out = pl.pallas_call(
        last_kernel,
        out_shape=jax.ShapeDtypeStruct((ROWS, GROUP * D), jnp.bfloat16),
        in_specs=[SM, SM] + [VM] * 9,
        out_specs=VM,
        scratch_shapes=[
            pltpu.VMEM((1, QR), jnp.float32),
            pltpu.VMEM((1, QR), jnp.float32),
            pltpu.VMEM((D, QR), jnp.float32),
            pltpu.VMEM((PAGES * PAGE, PAIR), jnp.bfloat16),
        ],
        compiler_params=params,
        cost_estimate=cost(1536),
        name="far_other_core_and_prefix",
    )(meta, page_table.reshape(PAGES), near, near_side, far, far_side, ids, qt, *now)
    out = lax.all_to_all(out.reshape(8, ROWS // 8, GROUP * D), "head", split_axis=0, concat_axis=0, tiled=True)
    return jnp.transpose(out, (1, 0, 2))


def solution(mesh):
    return jax.shard_map(
        per_device,
        mesh=mesh,
        in_specs=(
            P(("seq", "head"), None, None),
            P(("seq", "head"), None, None),
            P(),
            P("seq", None, "head", None),
            P("head", None),
        ),
        out_specs=P(("seq", "head"), None, None),
        check_vma=False,
    )
```

```python
import jax
import jax.numpy as jnp
from jax import lax
from jax.experimental import pallas as pl
from jax.experimental.pallas import tpu as pltpu
from jax.sharding import PartitionSpec as P

D = 128
PAIR = 2 * D
ROWS = 128
GROUP = 8
QR = ROWS * GROUP
NX, NY = 4, 8
PAGES = 32
PAGE = 16
BLOCKS = 4
TILE = 512
SCALE2 = D ** (-0.5) * 1.4426950408889634
LOW = -1e30
SLOT = ROWS + NX * PAGE
NEAR = 8


def x_ring(by):
    return [
        ((x * NY + y) * 2 + c, (((x + by) % NX) * NY + y) * 2 + c)
        for x in range(NX) for y in range(NY) for c in range(2)
    ]


def x_next():
    return [pair for pair in x_ring(1) if pair[0] < pair[1]]


SWAP = [(i, i ^ 1) for i in range(2 * NX * NY)]
Y_GROUPS = [[(x * NY + y) * 2 + c for y in range(NY)] for x in range(NX) for c in range(2)]


def fold(keys, values, mask, qt_ref, m_ref, l_ref, acc_ref):
    twice = jnp.concatenate([keys, keys], axis=1)
    lifted = jnp.concatenate([values.T, jnp.ones((16, keys.shape[0]), jnp.bfloat16)], axis=0)

    def scores_of(at):
        scores = jnp.dot(twice, qt_ref[:, at:at + TILE], preferred_element_type=jnp.float32)
        if mask is not None:
            scores = jnp.where(jnp.concatenate([mask] * (TILE // ROWS), axis=1), scores, LOW)
        return scores

    coming = scores_of(0)
    for at in range(0, QR, TILE):
        cols = slice(at, at + TILE)
        scores = coming
        if at + TILE < QR:
            coming = scores_of(at + TILE)
        old = m_ref[:, cols]
        top = jnp.maximum(old, jnp.max(scores, axis=0, keepdims=True))
        weights = jnp.exp2(scores - top).astype(jnp.bfloat16)
        factor = jnp.exp2(old - top)
        m_ref[:, cols] = top
        mixed = jnp.dot(lifted, weights, preferred_element_type=jnp.float32)
        l_ref[:, cols] = l_ref[:, cols] * factor + mixed[D:D + 1]
        acc_ref[:, cols] = acc_ref[:, cols] * factor + mixed[:D]


def starts_of(ids_ref, own):
    ids = ids_ref[...]
    starts = [jnp.sum((ids < b).astype(jnp.int32)) for b in range(1, 4)]
    own_ids = ids_ref[pl.ds(own, 1), :]
    row_start = jnp.zeros_like(own_ids)
    for b in range(1, 4):
        row_start = jnp.where(own_ids == b, starts[b - 1], row_start)
    return row_start, jnp.min(row_start), jnp.max(row_start)


def mask_of(block, own, row_start):
    key_rows = lax.broadcasted_iota(jnp.int32, (ROWS, ROWS), 0) + block * ROWS
    query_rows = lax.broadcasted_iota(jnp.int32, (ROWS, ROWS), 1) + own * ROWS
    return (key_rows >= row_start) & (key_rows <= query_rows)


def by_head_kernel(q_ref, kv_ref, out_ref):
    out_ref[:, :, :GROUP * D] = jnp.transpose(q_ref[...], (1, 0, 2))
    out_ref[:, :, GROUP * D:] = jnp.transpose(kv_ref[...], (1, 0, 2))


def own_kernel(meta_ref, mine_ref, side_ref, ids_ref, q_ref, qt_ref, m_ref, l_ref, acc_ref):
    own = meta_ref[0]
    row_start, first, last = starts_of(ids_ref, own)
    for g in range(GROUP):
        scaled = q_ref[:, g * D:(g + 1) * D].astype(jnp.float32) * SCALE2
        high = scaled.astype(jnp.bfloat16)
        low = (scaled - high.astype(jnp.float32)).astype(jnp.bfloat16)
        qt_ref[:D, g * ROWS:(g + 1) * ROWS] = high.T
        qt_ref[D:, g * ROWS:(g + 1) * ROWS] = low.T
    m_ref[...] = jnp.full_like(m_ref, LOW)
    l_ref[...] = jnp.zeros_like(l_ref)
    acc_ref[...] = jnp.zeros_like(acc_ref)
    state = (qt_ref, m_ref, l_ref, acc_ref)
    fold(mine_ref[:, :D], mine_ref[:, D:], mask_of(own, own, row_start), *state)

    @pl.when((own % 2 == 1) & (own * ROWS > first))
    def _():
        fold(side_ref[:, :D], side_ref[:, D:], mask_of(own - 1, own, row_start), *state)


def window(kv_ref, skip, slot, blocks, core, own, limits, qt_ref, m_ref, l_ref, acc_ref):
    row_start, first, last = limits
    chip = own // 2 - skip
    lowest = jnp.maximum((jnp.maximum(first // ROWS - core, -1) + 1) // 2, chip - NEAR)
    steps = jnp.maximum(chip - lowest + blocks - 1, 0) // blocks

    def step(i, carry):
        base = chip - blocks * (i + 1)
        pairs = []
        for b in range(blocks):
            start = (base + b + 4 * NY) % NY * slot
            pairs.append(kv_ref[pl.ds(pl.multiple_of(start, PAGE), ROWS), :])
        keys = jnp.concatenate([pair[:, :D] for pair in pairs], axis=0)
        values = jnp.concatenate([pair[:, D:] for pair in pairs], axis=0)
        whole = (2 * base + core) * ROWS >= last

        @pl.when(whole)
        def _():
            fold(keys, values, None, qt_ref, m_ref, l_ref, acc_ref)

        @pl.when(jnp.logical_not(whole))
        def _():
            mask = jnp.concatenate(
                [mask_of(2 * (base + b) + core, own, row_start) for b in range(blocks)], axis=0
            )
            fold(keys, values, mask, qt_ref, m_ref, l_ref, acc_ref)

        return carry

    lax.fori_loop(0, steps, step, 0)


def near_kernel(meta_ref, kv_ref, ids_ref, qt_ref, m_in, l_in, acc_in, m_ref, l_ref, acc_ref):
    m_ref[...] = m_in[...]
    l_ref[...] = l_in[...]
    acc_ref[...] = acc_in[...]
    own = meta_ref[0]
    window(kv_ref, 0, SLOT, NEAR, own % 2, own, starts_of(ids_ref, own), qt_ref, m_ref, l_ref, acc_ref)


def near_side_kernel(meta_ref, table_ref, kv_ref, side_ref, ids_ref, qt_ref, m_in, l_in, acc_in,
                     m_ref, l_ref, acc_ref, prefix_ref):
    m_ref[...] = m_in[...]
    l_ref[...] = l_in[...]
    acc_ref[...] = acc_in[...]
    own = meta_ref[0]
    core, x = own % 2, own // (2 * NY)
    for i in range(PAGES):
        page = table_ref[i]
        start = (page // 2) % NY * SLOT + ROWS + (x + NX - page // (2 * NY)) % NX * PAGE
        rows = pl.ds(pl.multiple_of(start, PAGE), PAGE)
        prefix_ref[i * PAGE:(i + 1) * PAGE, :] = jnp.where(page % 2 == core, kv_ref[rows, :], side_ref[rows, :])

    fold(prefix_ref[:, :D], prefix_ref[:, D:], None, qt_ref, m_ref, l_ref, acc_ref)
    window(side_ref, 0, SLOT, NEAR, 1 - core, own, starts_of(ids_ref, own), qt_ref, m_ref, l_ref, acc_ref)


def far_kernel(meta_ref, kv_ref, ids_ref, qt_ref, m_in, l_in, acc_in, m_ref, l_ref, acc_ref):
    m_ref[...] = m_in[...]
    l_ref[...] = l_in[...]
    acc_ref[...] = acc_in[...]
    own = meta_ref[0]
    window(kv_ref, NEAR, ROWS, BLOCKS, own % 2, own, starts_of(ids_ref, own), qt_ref, m_ref, l_ref, acc_ref)


def last_kernel(meta_ref, kv_ref, ids_ref, qt_ref, m_in, l_in, acc_in, out_ref, m_ref, l_ref, acc_ref):
    m_ref[...] = m_in[...]
    l_ref[...] = l_in[...]
    acc_ref[...] = acc_in[...]
    own = meta_ref[0]
    window(kv_ref, NEAR, ROWS, BLOCKS, 1 - own % 2, own, starts_of(ids_ref, own), qt_ref, m_ref, l_ref, acc_ref)
    result = (acc_ref[...] * (1.0 / l_ref[...])).astype(jnp.bfloat16)
    for g in range(GROUP):
        out_ref[:, g * D:(g + 1) * D] = result[:, g * ROWS:(g + 1) * ROWS].T


VM = pl.BlockSpec(memory_space=pltpu.VMEM)
SM = pl.BlockSpec(memory_space=pltpu.SMEM)


def cost(keys):
    return pl.CostEstimate(flops=4 * D * QR * keys, bytes_accessed=1 << 20, transcendentals=QR * keys)


def per_device(queries, branch_key_value, branch_ids, pool, page_table):
    me = lax.axis_index("seq")
    y = (me // 2) % NY
    page = pool.reshape(PAGE, PAIR)
    wide = pl.pallas_call(
        by_head_kernel,
        out_shape=jax.ShapeDtypeStruct((8, ROWS // 8, GROUP * D + PAIR), jnp.bfloat16),
        in_specs=[VM] * 2,
        out_specs=VM,
        name="by_head",
    )(queries, branch_key_value)
    wide = lax.all_to_all(wide, "head", split_axis=0, concat_axis=0, tiled=True).reshape(ROWS, -1)
    two_page = lax.ppermute(page, "seq", x_ring(2))
    wide, two_page = lax.optimization_barrier((wide, two_page))
    own = wide[:, GROUP * D:]
    one_back = lax.ppermute(jnp.concatenate([own, page, two_page], axis=0), "seq", x_ring(1))
    target = jnp.arange(NY, dtype=jnp.int32)[:, None, None]
    block = jnp.where(target > y, own[None], one_back[None, :ROWS])
    pages = jnp.concatenate([page, one_back[ROWS:ROWS + PAGE], two_page, one_back[ROWS + PAGE:]], axis=0)[None]
    send = jnp.concatenate([block, jnp.broadcast_to(pages, (NY, NX * PAGE, PAIR))], axis=1)
    near = lax.all_to_all(send, "seq", split_axis=0, concat_axis=0, tiled=True, axis_index_groups=Y_GROUPS)
    later, _ = lax.optimization_barrier((own, send))
    side = lax.ppermute(later, "seq", SWAP)
    ids = branch_ids.reshape(2 * NX * NY, ROWS)
    meta = me.astype(jnp.int32).reshape(1)
    state = [
        jax.ShapeDtypeStruct((1, QR), jnp.float32),
        jax.ShapeDtypeStruct((1, QR), jnp.float32),
        jax.ShapeDtypeStruct((D, QR), jnp.float32),
    ]
    params = pltpu.CompilerParams(vmem_limit_bytes=40 * 1024 * 1024)
    qt, *now = pl.pallas_call(
        own_kernel,
        out_shape=[jax.ShapeDtypeStruct((PAIR, QR), jnp.bfloat16)] + state,
        in_specs=[SM] + [VM] * 4,
        out_specs=[VM] * 4,
        compiler_params=params,
        cost_estimate=cost(256),
        name="own_chip",
    )(meta, own, side, ids, wide)
    near, qt, now = lax.optimization_barrier((near, qt, now))
    far = lax.ppermute(near[:, :ROWS], "seq", x_next())

    def near_part(operands):
        near, qt, now = operands
        near = near.reshape(NY * SLOT, PAIR)
        near_side = lax.ppermute(near, "seq", SWAP)
        now = pl.pallas_call(
            near_kernel,
            out_shape=state,
            in_specs=[SM] + [VM] * 6,
            out_specs=[VM] * 3,
            compiler_params=params,
            cost_estimate=cost(1024),
            name="near_window",
        )(meta, near, ids, qt, *now)
        return list(pl.pallas_call(
            near_side_kernel,
            out_shape=state,
            in_specs=[SM, SM] + [VM] * 7,
            out_specs=[VM] * 3,
            scratch_shapes=[pltpu.VMEM((PAGES * PAGE, PAIR), jnp.bfloat16)],
            compiler_params=params,
            cost_estimate=cost(1536),
            name="near_other_core_and_prefix",
        )(meta, page_table.reshape(PAGES), near, near_side, ids, qt, *now))

    now = lax.cond(me < 2 * NX * NY, near_part, lambda operands: list(operands[2]), (near, qt, now))
    far, now = lax.optimization_barrier((far, now))
    far = far.reshape(NY * ROWS, PAIR)
    far_side = lax.ppermute(far, "seq", SWAP[2 * NY:])
    now = pl.pallas_call(
        far_kernel,
        out_shape=state,
        in_specs=[SM] + [VM] * 6,
        out_specs=[VM] * 3,
        compiler_params=params,
        cost_estimate=cost(1024),
        name="far_window",
    )(meta, far, ids, qt, *now)
    out = pl.pallas_call(
        last_kernel,
        out_shape=jax.ShapeDtypeStruct((ROWS, GROUP * D), jnp.bfloat16),
        in_specs=[SM] + [VM] * 6,
        out_specs=VM,
        scratch_shapes=[
            pltpu.VMEM((1, QR), jnp.float32),
            pltpu.VMEM((1, QR), jnp.float32),
            pltpu.VMEM((D, QR), jnp.float32),
        ],
        compiler_params=params,
        cost_estimate=cost(1024),
        name="far_other_core",
    )(meta, far_side, ids, qt, *now)
    out = lax.all_to_all(out.reshape(8, ROWS // 8, GROUP * D), "head", split_axis=0, concat_axis=0, tiled=True)
    return jnp.transpose(out, (1, 0, 2))


def solution(mesh):
    return jax.shard_map(
        per_device,
        mesh=mesh,
        in_specs=(
            P(("seq", "head"), None, None),
            P(("seq", "head"), None, None),
            P(),
            P("seq", None, "head", None),
            P("head", None),
        ),
        out_specs=P(("seq", "head"), None, None),
        check_vma=False,
    )
```

```python
import jax
import jax.numpy as jnp
from jax import lax
from jax.experimental import pallas as pl
from jax.experimental.pallas import tpu as pltpu
from jax.sharding import PartitionSpec as P

D = 128
PAIR = 2 * D
ROWS = 128
GROUP = 8
QR = ROWS * GROUP
NX, NY = 4, 8
PAGES = 32
PAGE = 16
BLOCKS = 4
TILE = 512
SCALE2 = D ** (-0.5) * 1.4426950408889634
LOW = -1e30
SLOT = ROWS + NX * PAGE
NEAR = 8


def x_ring(by):
    return [
        ((x * NY + y) * 2 + c, (((x + by) % NX) * NY + y) * 2 + c)
        for x in range(NX) for y in range(NY) for c in range(2)
    ]


def x_next():
    return [pair for pair in x_ring(1) if pair[0] < pair[1]]


SWAP = [(i, i ^ 1) for i in range(2 * NX * NY)]
Y_GROUPS = [[(x * NY + y) * 2 + c for y in range(NY)] for x in range(NX) for c in range(2)]


def fold(keys, values, mask, qt_ref, m_ref, l_ref, acc_ref):
    twice = jnp.concatenate([keys, keys], axis=1)
    lifted = jnp.concatenate([values.T, jnp.ones((16, keys.shape[0]), jnp.bfloat16)], axis=0)

    def scores_of(at):
        scores = jnp.dot(twice, qt_ref[:, at:at + TILE], preferred_element_type=jnp.float32)
        if mask is not None:
            scores = jnp.where(jnp.concatenate([mask] * (TILE // ROWS), axis=1), scores, LOW)
        return scores

    coming = scores_of(0)
    for at in range(0, QR, TILE):
        cols = slice(at, at + TILE)
        scores = coming
        if at + TILE < QR:
            coming = scores_of(at + TILE)
        old = m_ref[:, cols]
        top = jnp.maximum(old, jnp.max(scores, axis=0, keepdims=True))
        weights = jnp.exp2(scores - top).astype(jnp.bfloat16)
        factor = jnp.exp2(old - top)
        m_ref[:, cols] = top
        mixed = jnp.dot(lifted, weights, preferred_element_type=jnp.float32)
        l_ref[:, cols] = l_ref[:, cols] * factor + mixed[D:D + 1]
        acc_ref[:, cols] = acc_ref[:, cols] * factor + mixed[:D]


def starts_of(ids_ref, own):
    ids = ids_ref[...]
    starts = [jnp.sum((ids < b).astype(jnp.int32)) for b in range(1, 4)]
    own_ids = ids_ref[pl.ds(own, 1), :]
    row_start = jnp.zeros_like(own_ids)
    for b in range(1, 4):
        row_start = jnp.where(own_ids == b, starts[b - 1], row_start)
    return row_start, jnp.min(row_start), jnp.max(row_start)


def mask_of(block, own, row_start):
    key_rows = lax.broadcasted_iota(jnp.int32, (ROWS, ROWS), 0) + block * ROWS
    query_rows = lax.broadcasted_iota(jnp.int32, (ROWS, ROWS), 1) + own * ROWS
    return (key_rows >= row_start) & (key_rows <= query_rows)


def by_head_kernel(q_ref, kv_ref, out_ref):
    out_ref[:, :, :GROUP * D] = jnp.transpose(q_ref[...], (1, 0, 2))
    out_ref[:, :, GROUP * D:] = jnp.transpose(kv_ref[...], (1, 0, 2))


def own_kernel(meta_ref, mine_ref, side_ref, ids_ref, q_ref, qt_ref, m_ref, l_ref, acc_ref):
    own = meta_ref[0]
    row_start, first, last = starts_of(ids_ref, own)
    for g in range(GROUP):
        scaled = q_ref[:, g * D:(g + 1) * D].astype(jnp.float32) * SCALE2
        high = scaled.astype(jnp.bfloat16)
        low = (scaled - high.astype(jnp.float32)).astype(jnp.bfloat16)
        qt_ref[:D, g * ROWS:(g + 1) * ROWS] = high.T
        qt_ref[D:, g * ROWS:(g + 1) * ROWS] = low.T
    m_ref[...] = jnp.full_like(m_ref, LOW)
    l_ref[...] = jnp.zeros_like(l_ref)
    acc_ref[...] = jnp.zeros_like(acc_ref)
    state = (qt_ref, m_ref, l_ref, acc_ref)
    fold(mine_ref[:, :D], mine_ref[:, D:], mask_of(own, own, row_start), *state)

    @pl.when((own % 2 == 1) & (own * ROWS > first))
    def _():
        fold(side_ref[:, :D], side_ref[:, D:], mask_of(own - 1, own, row_start), *state)


def window(kv_ref, skip, slot, blocks, core, own, limits, qt_ref, m_ref, l_ref, acc_ref):
    row_start, first, last = limits
    chip = own // 2 - skip
    lowest = jnp.maximum((jnp.maximum(first // ROWS - core, -1) + 1) // 2, chip - NEAR)
    steps = jnp.maximum(chip - lowest + blocks - 1, 0) // blocks

    def step(i, carry):
        base = chip - blocks * (i + 1)
        pairs = []
        for b in range(blocks):
            start = ((base + b) & (NY - 1)) * slot
            pairs.append(kv_ref[pl.ds(pl.multiple_of(start, PAGE), ROWS), :])
        keys = jnp.concatenate([pair[:, :D] for pair in pairs], axis=0)
        values = jnp.concatenate([pair[:, D:] for pair in pairs], axis=0)
        whole = (2 * base + core) * ROWS >= last

        @pl.when(whole)
        def _():
            fold(keys, values, None, qt_ref, m_ref, l_ref, acc_ref)

        @pl.when(jnp.logical_not(whole))
        def _():
            mask = jnp.concatenate(
                [mask_of(2 * (base + b) + core, own, row_start) for b in range(blocks)], axis=0
            )
            fold(keys, values, mask, qt_ref, m_ref, l_ref, acc_ref)

        return carry

    lax.fori_loop(0, steps, step, 0)


def near_kernel(meta_ref, kv_ref, ids_ref, qt_ref, m_in, l_in, acc_in, m_ref, l_ref, acc_ref):
    m_ref[...] = m_in[...]
    l_ref[...] = l_in[...]
    acc_ref[...] = acc_in[...]
    own = meta_ref[0]
    window(kv_ref, 0, SLOT, NEAR, own % 2, own, starts_of(ids_ref, own), qt_ref, m_ref, l_ref, acc_ref)


def near_side_kernel(meta_ref, table_ref, kv_ref, side_ref, ids_ref, qt_ref, m_in, l_in, acc_in,
                     m_ref, l_ref, acc_ref, prefix_ref):
    m_ref[...] = m_in[...]
    l_ref[...] = l_in[...]
    acc_ref[...] = acc_in[...]
    own = meta_ref[0]
    core, x = own % 2, own // (2 * NY)
    for i in range(PAGES):
        page = table_ref[i]
        start = ((page >> 1) & (NY - 1)) * SLOT + ROWS + ((x - (page >> 4)) & (NX - 1)) * PAGE
        rows = pl.ds(pl.multiple_of(start, PAGE), PAGE)
        prefix_ref[i * PAGE:(i + 1) * PAGE, :] = jnp.where(page % 2 == core, kv_ref[rows, :], side_ref[rows, :])

    limits = starts_of(ids_ref, own)
    base = own // 2 - NEAR
    whole = (2 * base + 1 - core) * ROWS >= limits[2]

    @pl.when(whole)
    def _():
        pairs = [prefix_ref[...]]
        for b in range(NEAR):
            start = ((base + b) & (NY - 1)) * SLOT
            pairs.append(side_ref[pl.ds(pl.multiple_of(start, PAGE), ROWS), :])
        pairs = jnp.concatenate(pairs, axis=0)
        fold(pairs[:, :D], pairs[:, D:], None, qt_ref, m_ref, l_ref, acc_ref)

    @pl.when(jnp.logical_not(whole))
    def _():
        fold(prefix_ref[:, :D], prefix_ref[:, D:], None, qt_ref, m_ref, l_ref, acc_ref)
        window(side_ref, 0, SLOT, NEAR, 1 - core, own, limits, qt_ref, m_ref, l_ref, acc_ref)


def far_kernel(meta_ref, kv_ref, ids_ref, qt_ref, m_in, l_in, acc_in, m_ref, l_ref, acc_ref):
    m_ref[...] = m_in[...]
    l_ref[...] = l_in[...]
    acc_ref[...] = acc_in[...]
    own = meta_ref[0]
    window(kv_ref, NEAR, ROWS, BLOCKS, own % 2, own, starts_of(ids_ref, own), qt_ref, m_ref, l_ref, acc_ref)


def last_kernel(meta_ref, kv_ref, ids_ref, qt_ref, m_in, l_in, acc_in, out_ref, m_ref, l_ref, acc_ref):
    m_ref[...] = m_in[...]
    l_ref[...] = l_in[...]
    acc_ref[...] = acc_in[...]
    own = meta_ref[0]
    window(kv_ref, NEAR, ROWS, BLOCKS, 1 - own % 2, own, starts_of(ids_ref, own), qt_ref, m_ref, l_ref, acc_ref)
    result = (acc_ref[...] * (1.0 / l_ref[...])).astype(jnp.bfloat16)
    for g in range(GROUP):
        out_ref[:, g * D:(g + 1) * D] = result[:, g * ROWS:(g + 1) * ROWS].T


VM = pl.BlockSpec(memory_space=pltpu.VMEM)
SM = pl.BlockSpec(memory_space=pltpu.SMEM)


def cost(keys):
    return pl.CostEstimate(flops=4 * D * QR * keys, bytes_accessed=1 << 20, transcendentals=QR * keys)


def per_device(queries, branch_key_value, branch_ids, pool, page_table):
    me = lax.axis_index("seq")
    y = (me // 2) % NY
    page = pool.reshape(PAGE, PAIR)
    wide = pl.pallas_call(
        by_head_kernel,
        out_shape=jax.ShapeDtypeStruct((8, ROWS // 8, GROUP * D + PAIR), jnp.bfloat16),
        in_specs=[VM] * 2,
        out_specs=VM,
        name="by_head",
    )(queries, branch_key_value)
    wide = lax.all_to_all(wide, "head", split_axis=0, concat_axis=0, tiled=True).reshape(ROWS, -1)
    two_page = lax.ppermute(page, "seq", x_ring(2))
    wide, two_page = lax.optimization_barrier((wide, two_page))
    own = wide[:, GROUP * D:]
    one_back = lax.ppermute(jnp.concatenate([own, page, two_page], axis=0), "seq", x_ring(1))
    target = jnp.arange(NY, dtype=jnp.int32)[:, None, None]
    block = jnp.where(target > y, own[None], one_back[None, :ROWS])
    pages = jnp.concatenate([page, one_back[ROWS:ROWS + PAGE], two_page, one_back[ROWS + PAGE:]], axis=0)[None]
    send = jnp.concatenate([block, jnp.broadcast_to(pages, (NY, NX * PAGE, PAIR))], axis=1)
    near = lax.all_to_all(send, "seq", split_axis=0, concat_axis=0, tiled=True, axis_index_groups=Y_GROUPS)
    later, _ = lax.optimization_barrier((own, send))
    side = lax.ppermute(later, "seq", SWAP)
    ids = branch_ids.reshape(2 * NX * NY, ROWS)
    meta = me.astype(jnp.int32).reshape(1)
    state = [
        jax.ShapeDtypeStruct((1, QR), jnp.float32),
        jax.ShapeDtypeStruct((1, QR), jnp.float32),
        jax.ShapeDtypeStruct((D, QR), jnp.float32),
    ]
    params = pltpu.CompilerParams(vmem_limit_bytes=40 * 1024 * 1024)
    qt, *now = pl.pallas_call(
        own_kernel,
        out_shape=[jax.ShapeDtypeStruct((PAIR, QR), jnp.bfloat16)] + state,
        in_specs=[SM] + [VM] * 4,
        out_specs=[VM] * 4,
        compiler_params=params,
        cost_estimate=cost(256),
        name="own_chip",
    )(meta, own, side, ids, wide)
    near, qt, now = lax.optimization_barrier((near, qt, now))
    far = lax.ppermute(near[:, :ROWS], "seq", x_next())

    def near_part(operands):
        near, qt, now = operands
        near = near.reshape(NY * SLOT, PAIR)
        near_side = lax.ppermute(near, "seq", SWAP)
        now = pl.pallas_call(
            near_kernel,
            out_shape=state,
            in_specs=[SM] + [VM] * 6,
            out_specs=[VM] * 3,
            compiler_params=params,
            cost_estimate=cost(1024),
            name="near_window",
        )(meta, near, ids, qt, *now)
        return list(pl.pallas_call(
            near_side_kernel,
            out_shape=state,
            in_specs=[SM, SM] + [VM] * 7,
            out_specs=[VM] * 3,
            scratch_shapes=[pltpu.VMEM((PAGES * PAGE, PAIR), jnp.bfloat16)],
            compiler_params=params,
            cost_estimate=cost(1536),
            name="near_other_core_and_prefix",
        )(meta, page_table.reshape(PAGES), near, near_side, ids, qt, *now))

    now = lax.cond(me < 2 * NX * NY, near_part, lambda operands: list(operands[2]), (near, qt, now))
    far, now = lax.optimization_barrier((far, now))
    far = far.reshape(NY * ROWS, PAIR)
    far_side = lax.ppermute(far, "seq", SWAP[2 * NY:])
    now = pl.pallas_call(
        far_kernel,
        out_shape=state,
        in_specs=[SM] + [VM] * 6,
        out_specs=[VM] * 3,
        compiler_params=params,
        cost_estimate=cost(1024),
        name="far_window",
    )(meta, far, ids, qt, *now)
    out = pl.pallas_call(
        last_kernel,
        out_shape=jax.ShapeDtypeStruct((ROWS, GROUP * D), jnp.bfloat16),
        in_specs=[SM] + [VM] * 6,
        out_specs=VM,
        scratch_shapes=[
            pltpu.VMEM((1, QR), jnp.float32),
            pltpu.VMEM((1, QR), jnp.float32),
            pltpu.VMEM((D, QR), jnp.float32),
        ],
        compiler_params=params,
        cost_estimate=cost(1024),
        name="far_other_core",
    )(meta, far_side, ids, qt, *now)
    out = lax.all_to_all(out.reshape(8, ROWS // 8, GROUP * D), "head", split_axis=0, concat_axis=0, tiled=True)
    return jnp.transpose(out, (1, 0, 2))


def solution(mesh):
    return jax.shard_map(
        per_device,
        mesh=mesh,
        in_specs=(
            P(("seq", "head"), None, None),
            P(("seq", "head"), None, None),
            P(),
            P("seq", None, "head", None),
            P("head", None),
        ),
        out_specs=P(("seq", "head"), None, None),
        check_vma=False,
    )
```

```python
import jax
import jax.numpy as jnp
from jax import lax
from jax.experimental import pallas as pl
from jax.experimental.pallas import tpu as pltpu
from jax.sharding import PartitionSpec as P

D = 128
PAIR = 2 * D
ROWS = 128
GROUP = 8
QR = ROWS * GROUP
NX, NY = 4, 8
PAGES = 32
PAGE = 16
BLOCKS = 4
TILE = 512
SCALE2 = D ** (-0.5) * 1.4426950408889634
LOW = -1e30
SLOT = ROWS + NX * PAGE
NEAR = 8


def x_ring(by):
    return [
        ((x * NY + y) * 2 + c, (((x + by) % NX) * NY + y) * 2 + c)
        for x in range(NX) for y in range(NY) for c in range(2)
    ]


def x_next():
    return [pair for pair in x_ring(1) if pair[0] < pair[1]]


SWAP = [(i, i ^ 1) for i in range(2 * NX * NY)]
Y_GROUPS = [[(x * NY + y) * 2 + c for y in range(NY)] for x in range(NX) for c in range(2)]


def fold(keys, values, mask, qt_ref, m_ref, l_ref, acc_ref):
    twice = jnp.concatenate([keys, keys], axis=1)
    lifted = jnp.concatenate([values.T, jnp.ones((16, keys.shape[0]), jnp.bfloat16)], axis=0)

    def scores_of(at):
        scores = jnp.dot(twice, qt_ref[:, at:at + TILE], preferred_element_type=jnp.float32)
        if mask is not None:
            scores = jnp.where(jnp.concatenate([mask] * (TILE // ROWS), axis=1), scores, LOW)
        return scores

    coming = scores_of(0)
    for at in range(0, QR, TILE):
        cols = slice(at, at + TILE)
        scores = coming
        if at + TILE < QR:
            coming = scores_of(at + TILE)
        old = m_ref[:, cols]
        top = jnp.maximum(old, jnp.max(scores, axis=0, keepdims=True))
        weights = jnp.exp2(scores - top).astype(jnp.bfloat16)
        factor = jnp.exp2(old - top)
        m_ref[:, cols] = top
        mixed = jnp.dot(lifted, weights, preferred_element_type=jnp.float32)
        l_ref[:, cols] = l_ref[:, cols] * factor + mixed[D:D + 1]
        acc_ref[:, cols] = acc_ref[:, cols] * factor + mixed[:D]


def starts_of(ids_ref, own):
    ids = ids_ref[...]
    starts = [jnp.sum((ids < b).astype(jnp.int32)) for b in range(1, 4)]
    own_ids = ids_ref[pl.ds(own, 1), :]
    row_start = jnp.zeros_like(own_ids)
    for b in range(1, 4):
        row_start = jnp.where(own_ids == b, starts[b - 1], row_start)
    return row_start, jnp.min(row_start), jnp.max(row_start)


def mask_of(block, own, row_start):
    key_rows = lax.broadcasted_iota(jnp.int32, (ROWS, ROWS), 0) + block * ROWS
    query_rows = lax.broadcasted_iota(jnp.int32, (ROWS, ROWS), 1) + own * ROWS
    return (key_rows >= row_start) & (key_rows <= query_rows)


def by_head_kernel(q_ref, kv_ref, out_ref):
    out_ref[:, :, :GROUP * D] = jnp.transpose(q_ref[...], (1, 0, 2))
    out_ref[:, :, GROUP * D:] = jnp.transpose(kv_ref[...], (1, 0, 2))


def own_kernel(meta_ref, mine_ref, side_ref, ids_ref, q_ref, qt_ref, m_ref, l_ref, acc_ref):
    own = meta_ref[0]
    row_start, first, last = starts_of(ids_ref, own)
    for g in range(GROUP):
        scaled = q_ref[:, g * D:(g + 1) * D].astype(jnp.float32) * SCALE2
        high = scaled.astype(jnp.bfloat16)
        low = (scaled - high.astype(jnp.float32)).astype(jnp.bfloat16)
        qt_ref[:D, g * ROWS:(g + 1) * ROWS] = high.T
        qt_ref[D:, g * ROWS:(g + 1) * ROWS] = low.T
    m_ref[...] = jnp.full_like(m_ref, LOW)
    l_ref[...] = jnp.zeros_like(l_ref)
    acc_ref[...] = jnp.zeros_like(acc_ref)
    state = (qt_ref, m_ref, l_ref, acc_ref)
    fold(mine_ref[:, :D], mine_ref[:, D:], mask_of(own, own, row_start), *state)

    @pl.when((own % 2 == 1) & (own * ROWS > first))
    def _():
        fold(side_ref[:, :D], side_ref[:, D:], mask_of(own - 1, own, row_start), *state)


def window(kv_ref, skip, slot, blocks, core, own, limits, qt_ref, m_ref, l_ref, acc_ref):
    row_start, first, last = limits
    chip = own // 2 - skip
    lowest = jnp.maximum((jnp.maximum(first // ROWS - core, -1) + 1) // 2, chip - NEAR)
    steps = jnp.maximum(chip - lowest + blocks - 1, 0) // blocks

    def step(i, carry):
        base = chip - blocks * (i + 1)
        pairs = []
        for b in range(blocks):
            start = (base + b + 4 * NY) % NY * slot
            pairs.append(kv_ref[pl.ds(pl.multiple_of(start, PAGE), ROWS), :])
        keys = jnp.concatenate([pair[:, :D] for pair in pairs], axis=0)
        values = jnp.concatenate([pair[:, D:] for pair in pairs], axis=0)
        whole = (2 * base + core) * ROWS >= last

        @pl.when(whole)
        def _():
            fold(keys, values, None, qt_ref, m_ref, l_ref, acc_ref)

        @pl.when(jnp.logical_not(whole))
        def _():
            mask = jnp.concatenate(
                [mask_of(2 * (base + b) + core, own, row_start) for b in range(blocks)], axis=0
            )
            fold(keys, values, mask, qt_ref, m_ref, l_ref, acc_ref)

        return carry

    lax.fori_loop(0, steps, step, 0)


def near_kernel(meta_ref, kv_ref, ids_ref, qt_ref, m_in, l_in, acc_in, m_ref, l_ref, acc_ref):
    m_ref[...] = m_in[...]
    l_ref[...] = l_in[...]
    acc_ref[...] = acc_in[...]
    own = meta_ref[0]
    window(kv_ref, 0, SLOT, NEAR, own % 2, own, starts_of(ids_ref, own), qt_ref, m_ref, l_ref, acc_ref)


def near_side_kernel(meta_ref, table_ref, kv_ref, side_ref, ids_ref, qt_ref, m_in, l_in, acc_in,
                     m_ref, l_ref, acc_ref, prefix_ref):
    m_ref[...] = m_in[...]
    l_ref[...] = l_in[...]
    acc_ref[...] = acc_in[...]
    own = meta_ref[0]
    core, x = own % 2, own // (2 * NY)
    for i in range(PAGES):
        page = table_ref[i]
        start = (page // 2) % NY * SLOT + ROWS + (x + NX - page // (2 * NY)) % NX * PAGE
        rows = pl.ds(pl.multiple_of(start, PAGE), PAGE)
        prefix_ref[i * PAGE:(i + 1) * PAGE, :] = jnp.where(page % 2 == core, kv_ref[rows, :], side_ref[rows, :])

    fold(prefix_ref[:, :D], prefix_ref[:, D:], None, qt_ref, m_ref, l_ref, acc_ref)
    window(side_ref, 0, SLOT, NEAR, 1 - core, own, starts_of(ids_ref, own), qt_ref, m_ref, l_ref, acc_ref)


def far_kernel(meta_ref, kv_ref, ids_ref, qt_ref, m_in, l_in, acc_in, m_ref, l_ref, acc_ref):
    m_ref[...] = m_in[...]
    l_ref[...] = l_in[...]
    acc_ref[...] = acc_in[...]
    own = meta_ref[0]
    window(kv_ref, NEAR, ROWS, BLOCKS, own % 2, own, starts_of(ids_ref, own), qt_ref, m_ref, l_ref, acc_ref)


def last_kernel(meta_ref, kv_ref, ids_ref, qt_ref, m_in, l_in, acc_in, out_ref, m_ref, l_ref, acc_ref):
    m_ref[...] = m_in[...]
    l_ref[...] = l_in[...]
    acc_ref[...] = acc_in[...]
    own = meta_ref[0]
    window(kv_ref, NEAR, ROWS, BLOCKS, 1 - own % 2, own, starts_of(ids_ref, own), qt_ref, m_ref, l_ref, acc_ref)
    result = (acc_ref[...] * (1.0 / l_ref[...])).astype(jnp.bfloat16)
    for g in range(GROUP):
        out_ref[:, g * D:(g + 1) * D] = result[:, g * ROWS:(g + 1) * ROWS].T


VM = pl.BlockSpec(memory_space=pltpu.VMEM)
SM = pl.BlockSpec(memory_space=pltpu.SMEM)


def cost(keys):
    return pl.CostEstimate(flops=4 * D * QR * keys, bytes_accessed=1 << 20, transcendentals=QR * keys)


def per_device(queries, branch_key_value, branch_ids, pool, page_table):
    me = lax.axis_index("seq")
    y = (me // 2) % NY
    page = pool.reshape(PAGE, PAIR)
    wide = pl.pallas_call(
        by_head_kernel,
        out_shape=jax.ShapeDtypeStruct((8, ROWS // 8, GROUP * D + PAIR), jnp.bfloat16),
        in_specs=[VM] * 2,
        out_specs=VM,
        name="by_head",
    )(queries, branch_key_value)
    wide = lax.all_to_all(wide, "head", split_axis=0, concat_axis=0, tiled=True).reshape(ROWS, -1)
    two_page = lax.ppermute(page, "seq", x_ring(2))
    wide, two_page = lax.optimization_barrier((wide, two_page))
    own = wide[:, GROUP * D:]
    one_back = lax.ppermute(jnp.concatenate([own, page, two_page], axis=0), "seq", x_ring(1))
    target = jnp.arange(NY, dtype=jnp.int32)[:, None, None]
    block = jnp.where(target > y, own[None], one_back[None, :ROWS])
    pages = jnp.concatenate([page, one_back[ROWS:ROWS + PAGE], two_page, one_back[ROWS + PAGE:]], axis=0)[None]
    send = jnp.concatenate([block, jnp.broadcast_to(pages, (NY, NX * PAGE, PAIR))], axis=1)
    near = lax.all_to_all(send, "seq", split_axis=0, concat_axis=0, tiled=True, axis_index_groups=Y_GROUPS)
    later, _ = lax.optimization_barrier((own, send))
    side = lax.ppermute(later, "seq", SWAP[::2])
    ids = branch_ids.reshape(2 * NX * NY, ROWS)
    meta = me.astype(jnp.int32).reshape(1)
    state = [
        jax.ShapeDtypeStruct((1, QR), jnp.float32),
        jax.ShapeDtypeStruct((1, QR), jnp.float32),
        jax.ShapeDtypeStruct((D, QR), jnp.float32),
    ]
    params = pltpu.CompilerParams(vmem_limit_bytes=40 * 1024 * 1024)
    qt, *now = pl.pallas_call(
        own_kernel,
        out_shape=[jax.ShapeDtypeStruct((PAIR, QR), jnp.bfloat16)] + state,
        in_specs=[SM] + [VM] * 4,
        out_specs=[VM] * 4,
        compiler_params=params,
        cost_estimate=cost(256),
        name="own_chip",
    )(meta, own, side, ids, wide)
    near, qt, now = lax.optimization_barrier((near, qt, now))
    far = lax.ppermute(near[:, :ROWS], "seq", x_next())

    def near_part(operands):
        near, qt, now = operands
        near = near.reshape(NY * SLOT, PAIR)
        near_side = lax.ppermute(near, "seq", SWAP)
        now = pl.pallas_call(
            near_kernel,
            out_shape=state,
            in_specs=[SM] + [VM] * 6,
            out_specs=[VM] * 3,
            compiler_params=params,
            cost_estimate=cost(1024),
            name="near_window",
        )(meta, near, ids, qt, *now)
        return list(pl.pallas_call(
            near_side_kernel,
            out_shape=state,
            in_specs=[SM, SM] + [VM] * 7,
            out_specs=[VM] * 3,
            scratch_shapes=[pltpu.VMEM((PAGES * PAGE, PAIR), jnp.bfloat16)],
            compiler_params=params,
            cost_estimate=cost(1536),
            name="near_other_core_and_prefix",
        )(meta, page_table.reshape(PAGES), near, near_side, ids, qt, *now))

    now = lax.cond(me < 2 * NX * NY, near_part, lambda operands: list(operands[2]), (near, qt, now))
    far, now = lax.optimization_barrier((far, now))
    far = far.reshape(NY * ROWS, PAIR)
    far_side = lax.ppermute(far, "seq", SWAP[2 * NY:])
    now = pl.pallas_call(
        far_kernel,
        out_shape=state,
        in_specs=[SM] + [VM] * 6,
        out_specs=[VM] * 3,
        compiler_params=params,
        cost_estimate=cost(1024),
        name="far_window",
    )(meta, far, ids, qt, *now)
    out = pl.pallas_call(
        last_kernel,
        out_shape=jax.ShapeDtypeStruct((ROWS, GROUP * D), jnp.bfloat16),
        in_specs=[SM] + [VM] * 6,
        out_specs=VM,
        scratch_shapes=[
            pltpu.VMEM((1, QR), jnp.float32),
            pltpu.VMEM((1, QR), jnp.float32),
            pltpu.VMEM((D, QR), jnp.float32),
        ],
        compiler_params=params,
        cost_estimate=cost(1024),
        name="far_other_core",
    )(meta, far_side, ids, qt, *now)
    out = lax.all_to_all(out.reshape(8, ROWS // 8, GROUP * D), "head", split_axis=0, concat_axis=0, tiled=True)
    return jnp.transpose(out, (1, 0, 2))


def solution(mesh):
    return jax.shard_map(
        per_device,
        mesh=mesh,
        in_specs=(
            P(("seq", "head"), None, None),
            P(("seq", "head"), None, None),
            P(),
            P("seq", None, "head", None),
            P("head", None),
        ),
        out_specs=P(("seq", "head"), None, None),
        check_vma=False,
    )
```
